512 devices in a mesh: blk: 32 (over y_hi, x, core), expert: 16 (over y_lo, z).
Axes of the slice: x: 4, y: 8 (y_hi: 4, y_lo: 2; y = y_hi * 2 + y_lo), z: 8, core: 2. Of those that a mesh axis runs over, the one named last changes fastest.
Arguments:
- queries: bfloat16 [16, 72, 4096], P('expert', None, 'blk'), may hold values from -6 to 6
- keys: bfloat16 [16, 72, 4096], P('expert', None, 'blk'), may hold values from -6 to 6
- values: bfloat16 [16, 72, 4096], P('expert', None, 'blk'), may hold values from -24 to 24
- image_ids: int32 [1024], P('blk'), may hold values from 0 to 2, as said below
- placement: int32 [1024, 1], P('blk'), may hold values from 0 to 31; in each aligned block of 32 rows (0 to 31, 32 to 63, ...) at most 4 rows name the same one
- merge_gain: float32 [16, 288], P('expert'), may hold values from 0.1 to 1.9
- merge_weight: bfloat16 [16, 288, 2048], P('expert'), may hold values from -0.09375 to 0.09375
- text: bfloat16 [4096, 2048], P('blk'), may hold values from -6 to 6
- norm_gain: float32 [2048], replicated, may hold values from 0.1 to 1.9
- w_gate: bfloat16 [32, 3072, 2048], P('blk', 'expert'), may hold values from -0.125 to 0.125
- w_up: bfloat16 [32, 3072, 2048], P('blk', 'expert'), may hold values from -0.125 to 0.125
- w_down: bfloat16 [32, 3072, 2048], P('blk', 'expert'), may hold values from -0.15625 to 0.15625
- routes: int32 [4096, 8], P('blk'), may hold values from 0 to 127, all different within a row; in each aligned block of 128 rows (0 to 127, 128 to 255, ...) at most 10 rows name the same one
- route_gates: float32 [4096, 8], P('blk'), may hold values from 0.2 to 1
- cotangent: bfloat16 [4096, 2048], P('blk'), may hold values from -6 to 6
Outputs:
- llm_out: bfloat16 [4096, 2048], P('blk')
- attn_grad: float32 [16, 72, 4096], P('expert', None, 'blk')
The draws below stay inside these ranges and needn't reach their ends.
Inputs may be any that keep to these rules, and one draw needn't show every extreme that they name: `image_ids`: three images in order: ids never fall along the sequence; image 0 holds from 64 to 127 merged rows and image 2 from 65 to 128. `placement`: among the 32 rows of one encoder index no shard is named more than 4 times. `routes`: each token names 8 different experts; among the 128 tokens of one shard no expert is named more than 10 times.
All inputs are finite; a program needn't handle non-finite values.
Results may differ from the reference program's by a relative error of at most 0.03.
Values may be sent and summed in bfloat16 or wider, within the bound.
A program may use at most 64 MiB of HBM per device.

```python
import math
import jax
import jax.numpy as jnp
import numpy as np
from jax import lax

HEADS = 16
HD = 72
DW = 2048
FF = 1536
EXPERTS = 128
TOPK = 8
LTOK_DEV = 128
SEQ = 4096
MROWS_DEV = 32
MSEQ = 1024
LTOK = 4096
CAPV = 4
CAPX = 10
EXP_WIN = 64
N_BLK = 32
N_EXPERT = 16


def draw_queries(key, part):
    key = jax.random.fold_in(key, 1)
    return jnp.clip(jax.random.normal(key, (HEADS, HD, SEQ)), -4.0, 4.0).astype(jnp.bfloat16)


def draw_keys(key, part):
    key = jax.random.fold_in(key, 2)
    return jnp.clip(jax.random.normal(key, (HEADS, HD, SEQ)), -4.0, 4.0).astype(jnp.bfloat16)


def draw_values(key, part):
    key = jax.random.fold_in(key, 3)
    head_rise = jnp.arange(HEADS, dtype=jnp.float32)[:, None, None] / max(HEADS - 1, 1)
    base_draw = jnp.clip(jax.random.normal(key, (HEADS, HD, SEQ)), -4.0, 4.0)
    return (base_draw * 2.0 * 3.0 ** head_rise).astype(jnp.bfloat16)


def draw_image_ids(key, part):
    key = jax.random.fold_in(key, 4)
    first_end = jax.random.randint(jax.random.fold_in(key, 1), (), MSEQ // 16, MSEQ // 8)
    second = jax.random.randint(jax.random.fold_in(key, 2), (), MSEQ - MSEQ // 8, MSEQ - MSEQ // 16)
    row_index = jnp.arange(MSEQ, dtype=jnp.int32)
    return (row_index >= first_end).astype(jnp.int32) + (row_index >= second).astype(jnp.int32)


def shard_levels(key, shape, cuts, smallest, high):
    level = 1.0
    for dim, blocks in cuts:
        steps = jax.random.uniform(jax.random.fold_in(jax.random.fold_in(key, 6), dim), (blocks,), jnp.float32, smallest / len(cuts), high / len(cuts))
        level = level * jnp.repeat(jnp.exp(steps), shape[dim] // blocks).reshape((-1,) + (1,) * (len(shape) - 1 - dim))
    return level


def routed_block(stream_key, own, number, rows, number_of, top, bound, lean):
    ranking = jax.random.permutation(stream_key, number_of)
    crowded, usual = shares(number_of, rows * top, bound, lean, True), shares(number_of, rows * top, bound, lean, False)
    places = jnp.arange(number_of)

    def named(lengths, rotation):
        used = int((lengths > 0).sum())
        fixed = max(1, used // 4)
        shifted = fixed + (places - fixed + rotation * (used - fixed)) % max(1, number_of - fixed)
        return jnp.zeros((number_of,), jnp.int32).at[ranking[jnp.where(places < fixed, places, shifted)]].set(jnp.asarray(lengths, jnp.int32))

    lengths = jnp.where(number % 4 == 0, named(crowded, number // 4), named(usual, number - number // 4 - 1))
    mixed = jax.random.permutation(jax.random.fold_in(own, 3), number_of)
    donor, sink = mixed[0:number_of // 2 * 2:2], mixed[1:number_of // 2 * 2:2]
    room = jnp.minimum(lengths[donor] - 1, bound - lengths[sink]) // 2
    room = jnp.where((donor == ranking[0]) | (sink == ranking[0]) | (lengths[sink] == 0), 0, jnp.maximum(room, 0))
    shifted = jax.random.randint(jax.random.fold_in(own, 4), (number_of // 2,), 0, 1 << 20) % (room + 1)
    lengths = lengths.at[donor].add(-shifted).at[sink].add(shifted)
    items = jnp.searchsorted(jnp.cumsum(lengths), jnp.arange(rows * top), side="right").astype(jnp.int32)
    listing = items.reshape(top, rows).T
    listing = listing[jax.random.permutation(jax.random.fold_in(own, 1), rows)]
    rotation = jax.random.randint(jax.random.fold_in(own, 2), (rows, 1), 0, top)
    return jnp.take_along_axis(listing, (jnp.arange(top)[None, :] + rotation) % top, axis=1)


def shares(number_of, total, most, slope, full):
    weights = [(1 << 20) // math.isqrt(grade ** slope) + 1 for grade in range(1, number_of + 1)]
    largest = most if full else min(most, max(-(-total // number_of), total * weights[0] // sum(weights)))
    least = 1 if total - largest >= number_of - 1 else 0
    given, spare = [largest] + [least] * (number_of - 1), total - largest - least * (number_of - 1)
    while spare > 0:
        free = [i for i in range(1, number_of) if given[i] < largest] or [i for i in range(1, number_of) if given[i] < most]
        pool, budget = sum([weights[i] for i in free]), spare
        for i in free:
            addition = min(most - given[i], max(1, budget * weights[i] // pool), spare)
            given[i] = given[i] + addition
            spare = spare - addition
    return np.array(given)


def noise(rng, extent, width, most, shards=(), kind=jnp.bfloat16):
    array = jax.random.normal(rng, extent, jnp.float32) * width
    if len(shards) > 0:
        array = shard_levels(rng, extent, shards, -0.22, 0.18) * array
    return jnp.clip(array, min=-most, max=most).astype(kind)


def setup_inputs(seed: int = 0) -> dict:
    key_of = jax.random.split(jax.random.key(seed), 16)
    queries = draw_queries(jax.random.fold_in(key_of[15], 71), 0)
    keys = draw_keys(jax.random.fold_in(key_of[15], 71), 0)
    values = draw_values(jax.random.fold_in(key_of[15], 71), 0)
    image_ids = draw_image_ids(jax.random.fold_in(key_of[15], 71), 0)
    placement_keys = jax.random.split(jax.random.fold_in(key_of[4], 1), MSEQ // MROWS_DEV)
    placement_turns = jax.random.permutation(jax.random.fold_in(key_of[4], 3), MSEQ // MROWS_DEV)
    placement = jax.vmap(lambda own, number: routed_block(jax.random.fold_in(key_of[4], 2), own, number, MROWS_DEV, N_BLK, 1, CAPV, 2))(placement_keys, placement_turns).reshape((MSEQ, 1))
    merge_gain = jnp.clip(1.0 + 0.18 * jax.random.normal(key_of[5], (HEADS, 4 * HD), jnp.float32), 0.1, 1.9)
    merge_weight = noise(key_of[6], (HEADS, 4 * HD, DW), (HEADS * 4 * HD) ** -0.5, 0.09375, ((0, 16),))
    text = noise(key_of[7], (LTOK, DW), 1.0, 6.0, ((0, 32),))
    norm_gain = jnp.clip(1.0 + 0.18 * jax.random.normal(key_of[8], (DW,), jnp.float32), 0.1, 1.9)
    w_gate = noise(key_of[9], (EXP_WIN // 2, 2 * FF, DW), DW ** -0.5, 0.125, ((0, 32), (1, 16)))
    w_up = noise(key_of[10], (EXP_WIN // 2, 2 * FF, DW), DW ** -0.5, 0.125, ((0, 32), (1, 16)))
    w_down = noise(key_of[11], (EXP_WIN // 2, 2 * FF, DW), FF ** -0.5, 0.15625, ((0, 32), (1, 16)))
    routes_keys = jax.random.split(jax.random.fold_in(key_of[12], 1), LTOK // LTOK_DEV)
    routes_turns = jax.random.permutation(jax.random.fold_in(key_of[12], 3), LTOK // LTOK_DEV)
    routes = jax.vmap(lambda own, number: routed_block(jax.random.fold_in(key_of[12], 2), own, number, LTOK_DEV, EXPERTS, TOPK, CAPX, 2))(routes_keys, routes_turns).reshape((LTOK, TOPK))
    route_gates = jnp.clip(jnp.exp(math.log(1.0) - 1.609438 * jax.random.uniform(key_of[13], (LTOK, TOPK), jnp.float32) ** shard_levels(key_of[13], (LTOK, TOPK), ((0, 32),), -0.2, 0.2)), 0.2, 1.0)
    cotangent = noise(key_of[14], (LTOK, DW), 1.0, 6.0, ((0, 32),))
    return dict(queries=queries, keys=keys, values=values, image_ids=image_ids, placement=placement, merge_gain=merge_gain, merge_weight=merge_weight, text=text, norm_gain=norm_gain, w_gate=w_gate, w_up=w_up, w_down=w_down, routes=routes, route_gates=route_gates, cotangent=cotangent)


EPS = 1e-06

def attend(queries, keys, values, image_ids):
    patch_ids = jnp.repeat(image_ids, 4)
    block_rows = min(256, SEQ)
    score_scale = HD ** (-0.5)
    key_table = keys.astype(jnp.float32)
    value_table = values.astype(jnp.float32)

    def one_block(first_row):
        query_part = lax.dynamic_slice_in_dim(queries, first_row, block_rows, 2).astype(jnp.float32)
        query_ids = lax.dynamic_slice_in_dim(patch_ids, first_row, block_rows, 0)
        scores = jnp.einsum('hdq,hdk->hqk', query_part, key_table) * score_scale
        same_image = query_ids[:, None] == patch_ids[None, :]
        scores = jnp.where(same_image[None], scores, -1e+30)
        row_max = lax.optimization_barrier(jnp.max(scores, axis=-1, keepdims=True))
        weights = jnp.exp(scores - row_max)
        row_total = lax.optimization_barrier(jnp.sum(weights, axis=-1))
        rounded = lax.optimization_barrier(weights.astype(jnp.bfloat16))
        mixed_rows = jnp.einsum('hqk,hdk->hdq', rounded.astype(jnp.float32), value_table)
        return mixed_rows / row_total[:, None, :]
    starts = (jnp.arange(SEQ // block_rows) * block_rows).astype(jnp.int32)
    pieces = lax.map(one_block, starts)
    return jnp.transpose(pieces, (1, 2, 0, 3)).reshape(HEADS, HD, SEQ).astype(jnp.bfloat16)

def merge_rows(attn):
    spread = jnp.transpose(attn, (2, 0, 1)).reshape(MSEQ, 4, HEADS, HD)
    return jnp.transpose(spread, (0, 2, 1, 3)).reshape(MSEQ, HEADS * 4 * HD)

def split_rows(merged):
    spread = merged.reshape(MSEQ, HEADS, 4, HD).transpose(0, 2, 1, 3).reshape(SEQ, HEADS, HD)
    return jnp.transpose(spread, (1, 2, 0))

def rms_norm(inputs, norm_gain):
    return inputs * lax.rsqrt(lax.optimization_barrier(jnp.mean(inputs * inputs, axis=-1, keepdims=True)) + EPS) * norm_gain

def by_shards(pairs):
    group_count = N_EXPERT // 2
    shard_width = FF // group_count
    total_parts = None
    for act_part, weight_part in pairs:
        row_count = act_part.shape[0]
        term = jnp.einsum('rjf,jfd->rjd', act_part.reshape(row_count, group_count, shard_width).astype(jnp.float32), weight_part.reshape(group_count, shard_width, DW).astype(jnp.float32))
        total_parts = term if total_parts is None else total_parts + term
    rounded = lax.optimization_barrier(total_parts.astype(jnp.bfloat16))
    return lax.optimization_barrier(jnp.sum(rounded.astype(jnp.float32), axis=1))

def reference(queries, keys, values, image_ids, placement, merge_gain, merge_weight, text, norm_gain, w_gate, w_up, w_down, routes, route_gates, cotangent):
    attn = attend(queries, keys, values, image_ids)
    full_width = HEADS * 4 * HD
    merged = merge_rows(attn).astype(jnp.float32)
    row_mean = lax.optimization_barrier(jnp.sum(merged, axis=1)) / full_width
    mean_square = lax.optimization_barrier(jnp.sum(merged * merged, axis=1)) / full_width
    inv_std = lax.rsqrt(mean_square - row_mean * row_mean + EPS)
    normed = (merged - row_mean[:, None]) * inv_std[:, None]
    gain_flat = merge_gain.reshape(full_width)
    scaled = (normed * gain_flat).astype(jnp.bfloat16)
    weight_flat = merge_weight.reshape(full_width, DW)
    vision = jnp.dot(scaled, weight_flat, preferred_element_type=jnp.float32).astype(jnp.bfloat16)
    dest_shard = placement[:, 0].astype(jnp.int32)
    dest_hits = (dest_shard[:, None] == jnp.arange(N_BLK, dtype=jnp.int32)[None, :]).astype(jnp.int32)
    earlier = jnp.cumsum(dest_hits, axis=0).astype(jnp.int32) - dest_hits
    slot_index = lax.optimization_barrier(jnp.sum(earlier * dest_hits, axis=1)).astype(jnp.int32)
    position = (dest_shard * LTOK_DEV + slot_index).astype(jnp.int32)
    hidden_in = text.at[position].set(vision)
    inputs_f32 = hidden_in.astype(jnp.float32)
    normed_h, norm_pull = jax.vjp(lambda inputs: rms_norm(inputs, norm_gain), inputs_f32)
    h_rows = normed_h.astype(jnp.bfloat16)
    cot_rows = cotangent.astype(jnp.float32)
    pair_expert = routes.reshape(-1)
    pair_gate = route_gates.reshape(-1)
    max_rows = N_BLK * CAPX
    gate_all = w_gate.reshape(EXP_WIN, FF, DW)
    up_all = w_up.reshape(EXP_WIN, FF, DW)
    down_all = w_down.reshape(EXP_WIN, FF, DW)

    def one_expert(state_carry, expert_id):
        expert_sum, hidden_grad = state_carry
        chosen = pair_expert == expert_id
        pair_index = jnp.nonzero(chosen, size=max_rows, fill_value=0)[0].astype(jnp.int32)
        live_mask = (jnp.arange(max_rows) < jnp.sum(chosen.astype(jnp.int32))).astype(jnp.float32)
        token_index = (pair_index // TOPK).astype(jnp.int32)
        pair_weight = pair_gate[pair_index] * live_mask
        expert_rows = h_rows[token_index]
        gate_mat = gate_all[expert_id]
        up_mat = up_all[expert_id]
        down_mat = down_all[expert_id]
        gate_pre = jnp.dot(expert_rows, gate_mat.T, preferred_element_type=jnp.float32)
        up_proj = jnp.dot(expert_rows, up_mat.T, preferred_element_type=jnp.float32)
        activated = (jax.nn.silu(gate_pre) * up_proj).astype(jnp.bfloat16)
        down_part = by_shards(((activated, down_mat),))
        expert_sum = expert_sum.at[token_index].add(down_part * pair_weight[:, None])
        back_rows = (cot_rows[token_index] * pair_weight[:, None]).astype(jnp.bfloat16)
        act_grad = jnp.dot(back_rows, down_mat.T, preferred_element_type=jnp.float32)
        sigmoid_gate = jax.nn.sigmoid(gate_pre)
        gate_grad = (act_grad * up_proj * sigmoid_gate * (1.0 + gate_pre * (1.0 - sigmoid_gate))).astype(jnp.bfloat16)
        up_grad = (act_grad * gate_pre * sigmoid_gate).astype(jnp.bfloat16)
        row_grad = by_shards(((gate_grad, gate_mat), (up_grad, up_mat)))
        hidden_grad = hidden_grad.at[token_index].add(row_grad * live_mask[:, None])
        return ((expert_sum, hidden_grad), None)
    zero_rows = jnp.zeros((LTOK, DW), jnp.float32)
    (expert_sum, hidden_grad), unused_out = lax.scan(one_expert, (zero_rows, zero_rows), jnp.arange(EXP_WIN, dtype=jnp.int32))
    llm_out = (inputs_f32 + expert_sum).astype(jnp.bfloat16)
    input_grad = cot_rows + norm_pull(hidden_grad)[0]
    vision_grad = input_grad[position].astype(jnp.bfloat16)
    scaled_grad = jnp.dot(vision_grad, weight_flat.T, preferred_element_type=jnp.float32)
    normed_grad = scaled_grad * gain_flat
    grad_mean = lax.optimization_barrier(jnp.sum(normed_grad, axis=1)) / full_width
    cross_mean = lax.optimization_barrier(jnp.sum(normed_grad * normed, axis=1)) / full_width
    merged_grad = inv_std[:, None] * (normed_grad - grad_mean[:, None] - normed * cross_mean[:, None])
    return (llm_out, split_rows(merged_grad))
```

```python
import jax
import jax.numpy as jnp
from jax import lax
from jax.experimental import pallas as pl
from jax.experimental.pallas import tpu as pltpu
from jax.sharding import PartitionSpec as P

MESH = pl.DeviceIdType.MESH
F32 = jnp.float32
BF16 = jnp.bfloat16
EPS = 1e-06
NB = 32
NE = 16
NZ = 8
HD = 72
CAPX = 10
SLOT = 16
ROWS = NB * CAPX
HALF = ROWS // 2
COLS = 256
TOK = 128
MR = 32
WIDTH = 2048
FG = 192
MERGE = 4608
KVR = 160
STREAMS = ((1, 0, 4), (1, 1, 3), (-1, 0, 3), (-1, 1, 4))


def mm(a, b):
    return lax.dot_general(a, b, (((1,), (0,)), ((), ())), preferred_element_type=F32)


def mm_nt(a, b):
    return lax.dot_general(a, b, (((1,), (1,)), ((), ())), preferred_element_type=F32)


def mm_tn(a, b):
    return lax.dot_general(a, b, (((0,), (0,)), ((), ())), preferred_element_type=F32)


def iota(shape, dim):
    return lax.broadcasted_iota(jnp.int32, shape, dim)


def wait_bytes(ref, sem):
    pltpu.make_async_copy(ref, ref, sem).wait()


def kernel(
    qp_ref, kv_ref, plc_ref, rt_ref, gt_ref, gain_ref, gsp_ref, ng_ref,
    mw_hbm, text_hbm, cot_hbm, wg_hbm, wu_hbm, wd_hbm,
    llm_ref, ag_ref,
    mw, text, cot, wg, wu, wd, wgs, wus, local_sem,
    kvb, scores, kv_send, kv_recv,
    dmat, dg_hi, dg_lo, cmat, ga, gb, sa, sb,
    cot_out, cot_in, h_out, h_in, rg_out, rg_in, dn_out, dn_in, a2a_send, a2a_recv,
    cv_out, cv_in, vi_out, vi_in, hg_out, hg_in, row_send, row_recv,
    gw_all, st_all, vp, vp_all, hg_all, hg_mine, e_send, e_recv,
    vis_all, cv_all, z_send, z_recv,
    xc, xh, ring_send, ring_recv,
    gate_acc, up_acc, ss_acc, act_grad,
    rg_part, rg_o, rg_i, dn_part, dn_o, dn_i, rs_send, rs_recv,
    pair_out, pair_in, pair_send, pair_recv,
    llm_all, llm_send, llm_recv,
):
    b = lax.axis_index("blk")
    e = lax.axis_index("expert")
    y = e // NZ
    z = e % NZ
    core = b % 2
    x = (b // 2) % 4
    yh = b // 8

    def blk_of(yy, xx, cc):
        return (yy * 4 + xx) * 2 + cc

    def zdev(zz):
        return y * NZ + zz

    zcols = pl.ds(pl.multiple_of(z * COLS, COLS), COLS)
    locals_ = [
        pltpu.make_async_copy(cot_hbm.at[:, zcols], cot, local_sem.at[0]),
        pltpu.make_async_copy(text_hbm.at[:, zcols], text, local_sem.at[1]),
        pltpu.make_async_copy(mw_hbm.at[0], mw, local_sem.at[2]),
        pltpu.make_async_copy(wd_hbm.at[0], wd, local_sem.at[3]),
        pltpu.make_async_copy(wg_hbm.at[0], wg, local_sem.at[4]),
        pltpu.make_async_copy(wu_hbm.at[0], wu, local_sem.at[5]),
    ]
    for copy in locals_:
        copy.start()
    kvb[b] = kv_ref[...]

    barrier = pltpu.get_barrier_semaphore()

    def greet_blk(i, carry):
        pl.semaphore_signal(barrier, inc=1, device_id=((b + i) % NB, e), device_id_type=MESH)
        return carry

    def greet_expert(i, carry):
        pl.semaphore_signal(barrier, inc=1, device_id=(b, (e + i) % NE), device_id_type=MESH)
        return carry

    lax.fori_loop(1, NB, greet_blk, 0)
    lax.fori_loop(1, NE, greet_expert, 0)
    pl.semaphore_wait(barrier, NB - 1 + NE - 1)

    def send(src, dst, ssem, rsem, db, de):
        pltpu.make_async_remote_copy(
            src_ref=src, dst_ref=dst, send_sem=ssem, recv_sem=rsem, device_id=(db, de), device_id_type=MESH
        ).start()

    def a2a_start(src, dst, ssem, rsem):
        dst[b] = src[b]

        def one(i, carry):
            to = (b + i) % NB
            send(src.at[to], dst.at[b], ssem, rsem, to, e)
            return carry

        lax.fori_loop(1, NB, one, 0)

    def a2a_wait(dst, rsem):
        wait_bytes(dst.at[pl.ds(0, NB - 1)], rsem)

    def to_experts(src_of, dst, ssem, rsem):
        def one(i, carry):
            to = (e + i) % NE
            send(src_of(to), dst.at[e], ssem, rsem, b, to)
            return carry

        lax.fori_loop(1, NE, one, 0)

    def to_z(src, dst, ssem, rsem):
        def one(i, carry):
            to = (z + i) % NZ
            send(src, dst.at[z], ssem, rsem, b, zdev(to))
            return carry

        lax.fori_loop(1, NZ, one, 0)

    def ring_gather(buf, ssem, rsems, half_rows):
        def piece(src, half):
            return buf.at[src, pl.ds(half * half_rows, half_rows)]

        for k in range(5):
            for way, half, far in STREAMS:
                if k > far:
                    continue
                src = (z + 8 - way * k) % NZ
                if k > 0:
                    wait_bytes(piece(src, half), rsems.at[src * 2 + half])
                if k < far:
                    send(piece(src, half), piece(src, half), ssem, rsems.at[src * 2 + half], b, zdev((z + 8 + way) % NZ))
            yield k

    def ring_reduce(part, out, inn, ssem, rsems):
        for d in range(4, 0, -1):
            for index, (way, half, far) in enumerate(STREAMS):
                if d > far:
                    continue
                rows = pl.ds(half * HALF, HALF)
                dest = (z + 8 + way * d) % NZ
                value = part[dest, rows, :]
                here = index * 5 + d
                if d < far:
                    wait_bytes(inn.at[here], rsems.at[here])
                    value = value + inn[here].astype(F32)
                out[here] = value.astype(BF16)
                send(out.at[here], inn.at[here - 1], ssem, rsems.at[here - 1], b, zdev((z + 8 + way) % NZ))
            yield d
        for index in range(4):
            wait_bytes(inn.at[index * 5], rsems.at[index * 5])
        for half in range(2):
            rows = pl.ds(half * HALF, HALF)
            part[z, rows, :] = part[z, rows, :] + (inn[half * 5].astype(F32) + inn[(2 + half) * 5].astype(F32))
        yield 0

    def kv_go(block, to):
        send(kvb.at[block], kvb.at[block], kv_send.at[0], kv_recv.at[block], to, e)

    def kv_x(block):
        for dx in (1, 3, 2):
            kv_go(block, blk_of(yh, (x + dx) % 4, core))
        kv_go(block, blk_of(yh, x, 1 - core))

    for dy in (1, 3, 2):
        kv_go(b, blk_of((yh + dy) % 4, x, core))
    kv_x(b)

    upper = (iota((TOK, TOK), 0) < iota((TOK, TOK), 1)).astype(BF16)
    ids = 2 * iota((NB, TOK), 0) + y
    hit = jnp.zeros((NB, TOK), F32)
    gate = jnp.zeros((NB, TOK), F32)
    for k in range(8):
        same = rt_ref[k : k + 1, :] == ids
        hit = hit + jnp.where(same, 1.0, 0.0)
        gate = gate + jnp.where(same, gt_ref[k : k + 1, :], 0.0)
    rank = mm(hit.astype(BF16), upper)
    place = jnp.where(hit > 0.0, rank, -1.0)
    slot3 = iota((NB, SLOT, TOK), 1).astype(F32)
    one_hot = jnp.where(place[:, None, :] == slot3, 1.0, 0.0)
    gated = (one_hot * gate[:, None, :]).reshape(NB * SLOT, TOK)
    dmat[...] = one_hot.reshape(NB * SLOT, TOK).astype(BF16)
    high = gated.astype(BF16)
    dg_hi[...] = high
    dg_lo[...] = (gated - high.astype(F32)).astype(BF16)
    slot_gate = jnp.sum(gated, axis=1, keepdims=True)
    locals_[0].wait()
    back = (mm(dmat[...], cot[...]) * slot_gate).astype(BF16)
    cot_out[...] = back.reshape(NB, SLOT, COLS)

    for dy in (1, 3, 2):
        block = blk_of((yh + 4 - dy) % 4, x, core)
        wait_bytes(kvb.at[block], kv_recv.at[block])
        kv_x(block)
    a2a_start(cot_out, cot_in, a2a_send.at[0], a2a_recv.at[0])

    ci = iota((ROWS, NB * SLOT), 0)
    cj = iota((ROWS, NB * SLOT), 1)
    cmat[...] = jnp.where((ci == (cj >> 4) * CAPX + (cj & 15)) & ((cj & 15) < CAPX), 1.0, 0.0).astype(BF16)

    def kv_arrived_x(i, carry):
        dx = jnp.where(i < 4, 1, jnp.where(i < 8, 3, 2))
        block = blk_of((yh + 4 - i % 4) % 4, (x + 4 - dx) % 4, core)
        wait_bytes(kvb.at[block], kv_recv.at[block])
        kv_go(block, blk_of(yh, x, 1 - core))
        return carry

    lax.fori_loop(0, 12, kv_arrived_x, 0)

    locals_[2].wait()
    gw = mm(gsp_ref[...], mw[...])
    gw = gw[0:1, :] + gw[1:2, :]
    for c in range(NZ):
        gw_all[e, c : c + 1, :] = gw[:, c * COLS : (c + 1) * COLS]
    to_experts(lambda to: gw_all.at[e], gw_all, e_send.at[0], e_recv.at[0])

    def kv_arrived_core(i, carry):
        block = 2 * i + (1 - core)
        wait_bytes(kvb.at[block], kv_recv.at[block])
        return carry

    lax.fori_loop(0, 16, kv_arrived_core, 0)

    def score_block(i, carry):
        s = mm_tn(kvb[i], qp_ref[...])
        scores[pl.ds(pl.multiple_of(i * TOK, TOK), TOK), :] = s
        return jnp.maximum(carry, jnp.max(s.reshape(TOK // 8, 8, TOK), axis=0))

    top = lax.fori_loop(0, NB, score_block, jnp.full((8, TOK), -3e38, F32))
    top = jnp.max(top, axis=0, keepdims=True)

    def weigh_block(i, carry):
        acc, total = carry
        s = scores[pl.ds(pl.multiple_of(i * TOK, TOK), TOK), :]
        w = jnp.exp((s - top) * (HD ** -0.5))
        acc = acc + mm(kvb[i], w.astype(BF16))
        return acc, total + jnp.sum(w.reshape(TOK // 8, 8, TOK), axis=0)

    acc, total = lax.fori_loop(0, NB, weigh_block, (jnp.zeros((KVR, TOK), F32), jnp.zeros((8, TOK), F32)))
    total = jnp.sum(total, axis=0, keepdims=True)
    attn = (acc[HD : 2 * HD, :] / total).astype(BF16).astype(F32)

    def over_i(row):
        row = row + pltpu.roll(row, 32, 1)
        return row + pltpu.roll(row, 64, 1)

    sums = jnp.sum(attn, axis=0, keepdims=True)
    squares = jnp.sum(attn * attn, axis=0, keepdims=True)
    row8 = iota((8, TOK), 0)
    st_all[e] = over_i(jnp.where(row8 == 0, sums, jnp.where(row8 == 1, squares, 0.0)))
    to_experts(lambda to: st_all.at[e], st_all, e_send.at[1], e_recv.at[1])

    a2a_wait(cot_in, a2a_recv.at[0])
    xc[z] = mm(cmat[...], cot_in[...].reshape(NB * SLOT, COLS)).astype(BF16)
    cot_ring = ring_gather(xc, ring_send.at[0], ring_recv.at[0], HALF)
    next(cot_ring)

    wait_bytes(st_all.at[pl.ds(0, NE - 1)], e_recv.at[1])
    stats = jnp.sum(st_all[...], axis=0)
    mean = stats[0:1, :] * (1.0 / MERGE)
    inv_std = lax.rsqrt(stats[1:2, :] * (1.0 / MERGE) - mean * mean + EPS)
    normed = (attn - mean) * inv_std
    scaled = normed * gain_ref[...]
    group = iota((HD, TOK), 1) >> 5
    left = jnp.concatenate([jnp.where(group == i, scaled, 0.0) for i in range(4)], axis=0).astype(BF16)

    def merge_chunk(c, carry):
        cols = pl.ds(pl.multiple_of(c * COLS, COLS), COLS)
        v = mm_tn(left, mw[:, cols])
        vp[c] = (v[0:32] + v[32:64] + v[64:96] + v[96:128]).astype(BF16)
        return carry

    lax.fori_loop(0, NZ, merge_chunk, 0)
    vp_all[e] = vp[z]
    to_experts(lambda to: vp.at[to % NZ], vp_all, e_send.at[2], e_recv.at[2])

    places = kvb[:, 144:160, :].astype(F32)
    places = jnp.sum(jnp.where(iota((NB, 16, TOK), 1) == 3, places, 0.0), axis=1)
    named = jnp.where(places == b.astype(F32), 1.0, 0.0)
    count = jnp.broadcast_to(jnp.sum(named, axis=1, keepdims=True), (NB, TOK))
    below = (iota((NB, NB), 1) < iota((NB, NB), 0)).astype(BF16)
    base = mm(below, count.astype(BF16))
    placed = jnp.sum(count, axis=0, keepdims=True)[:, 0:1]
    q3 = iota((NB, 8, TOK), 1).astype(F32)
    k3 = jnp.where(q3 < 4.0, q3, q3 - 4.0)
    lane3 = iota((NB, 8, TOK), 2).astype(F32)
    mine = jnp.where((lane3 == base[:, None, :] + k3) & (k3 < count[:, None, :]), 1.0, 0.0)
    ga[...] = jnp.where(q3 < 4.0, mine, 0.0).reshape(NB * 8, TOK).astype(BF16)
    gb[...] = jnp.where(q3 < 4.0, 0.0, mine).reshape(NB * 8, TOK).astype(BF16)
    to_shard = jnp.where(plc_ref[0:1, :] == iota((NB, TOK), 0), 1.0, 0.0)
    order = mm(to_shard.astype(BF16), upper)
    order = jnp.where(to_shard > 0.0, order, -1.0)
    theirs = jnp.where(order[:, None, :] == k3, 1.0, 0.0)
    sa[...] = jnp.where(q3 < 4.0, theirs, 0.0).reshape(NB * 8, TOK).astype(BF16)
    sb[...] = jnp.where(q3 < 4.0, 0.0, theirs).reshape(NB * 8, TOK).astype(BF16)

    cv_out[...] = (mm(ga[...], cot[:, 0:TOK]) + mm(gb[...], cot[:, TOK:COLS])).reshape(NB, 8, TOK)
    a2a_start(cv_out, cv_in, row_send.at[0], row_recv.at[0])
    next(cot_ring)

    wait_bytes(vp_all.at[pl.ds(0, NE - 1)], e_recv.at[2])
    vision = jnp.sum(vp_all[...].astype(F32), axis=0).astype(BF16)
    vis_all[z] = vision
    fill = jnp.zeros((TOK - MR, COLS), BF16)
    padded = jnp.concatenate([vision, fill], axis=0)
    vi_out[...] = (mm(sa[...], padded[:, 0:TOK]) + mm(sb[...], padded[:, TOK:COLS])).reshape(NB, 8, TOK)
    a2a_start(vi_out, vi_in, row_send.at[1], row_recv.at[1])
    to_z(vis_all.at[z], vis_all, z_send.at[0], z_recv.at[0])
    next(cot_ring)

    locals_[4].wait()
    locals_[5].wait()

    def gain_chunk(c, carry):
        cols = pl.ds(pl.multiple_of(c * COLS, COLS), COLS)
        g = ng_ref[:, cols]
        wgs[:, cols] = (wg[:, cols].astype(F32) * g).astype(BF16)
        wus[:, cols] = (wu[:, cols].astype(F32) * g).astype(BF16)
        return carry

    lax.fori_loop(0, NZ, gain_chunk, 0)
    a2a_wait(cv_in, row_recv.at[0])
    cv = cv_in[...].reshape(NB * 8, TOK).astype(BF16)
    cv_all[z, :, 0:TOK] = mm_tn(sa[...], cv)[0:MR].astype(BF16)
    cv_all[z, :, TOK:COLS] = mm_tn(sb[...], cv)[0:MR].astype(BF16)
    to_z(cv_all.at[z], cv_all, z_send.at[1], z_recv.at[1])

    locals_[1].wait()
    a2a_wait(vi_in, row_recv.at[1])
    arrived = vi_in[...].reshape(NB * 8, TOK).astype(BF16)
    taken = iota((TOK, TOK), 0).astype(F32) < placed
    llm_a = jnp.where(taken, mm_tn(ga[...], arrived), text[:, 0:TOK].astype(F32))
    llm_b = jnp.where(taken, mm_tn(gb[...], arrived), text[:, TOK:COLS].astype(F32))
    text[:, 0:TOK] = llm_a.astype(BF16)
    text[:, TOK:COLS] = llm_b.astype(BF16)
    h_out[...] = mm(dmat[...], text[...]).astype(BF16).reshape(NB, SLOT, COLS)
    a2a_start(h_out, h_in, a2a_send.at[1], a2a_recv.at[1])

    for _ in cot_ring:
        pass
    locals_[3].wait()
    act_grad[...] = jnp.zeros_like(act_grad)
    gate_acc[...] = jnp.zeros_like(gate_acc)
    up_acc[...] = jnp.zeros_like(up_acc)
    ss_acc[...] = jnp.zeros_like(ss_acc)

    def act_chunk(c, carry):
        cols = pl.ds(pl.multiple_of(c * COLS, COLS), COLS)
        act_grad[...] += mm_nt(xc[c], wd[:, cols])
        return carry

    lax.fori_loop(0, NZ, act_chunk, 0)

    a2a_wait(h_in, a2a_recv.at[1])
    xh[z] = mm(cmat[...], h_in[...].reshape(NB * SLOT, COLS)).astype(BF16)
    h_ring = ring_gather(xh, ring_send.at[1], ring_recv.at[1], HALF)

    def project(c, carry):
        cols = pl.ds(pl.multiple_of(c * COLS, COLS), COLS)
        rows = xh[c]
        gate_acc[...] += mm_nt(rows, wgs[:, cols])
        up_acc[...] += mm_nt(rows, wus[:, cols])
        wide = rows.astype(F32)
        ss_acc[...] += wide[:, 0:TOK] * wide[:, 0:TOK] + wide[:, TOK:COLS] * wide[:, TOK:COLS]
        return carry

    for k in h_ring:
        if k == 0 or k == 4:
            project((z + k) % NZ, 0)
        else:
            lax.fori_loop(0, 2, lambda j, carry: project((z + 8 + (2 * j - 1) * k) % NZ, carry), 0)

    inv = lax.rsqrt(jnp.sum(ss_acc[...], axis=1, keepdims=True) * (1.0 / WIDTH) + EPS)
    gate_pre = gate_acc[...] * inv
    up_proj = up_acc[...] * inv
    sig = 1.0 / (1.0 + jnp.exp(-gate_pre))
    activated = (gate_pre * sig * up_proj).astype(BF16)
    grad = act_grad[...]
    gate_grad = (grad * up_proj * sig * (1.0 + gate_pre * (1.0 - sig))).astype(BF16)
    up_grad = (grad * gate_pre * sig).astype(BF16)

    def grad_chunk(c, carry):
        cols = pl.ds(pl.multiple_of(c * COLS, COLS), COLS)
        rg_part[c] = mm(gate_grad, wg[:, cols]) + mm(up_grad, wu[:, cols])
        return carry

    def down_chunk(c, carry):
        cols = pl.ds(pl.multiple_of(c * COLS, COLS), COLS)
        dn_part[c] = mm(activated, wd[:, cols])
        return carry

    lax.fori_loop(0, NZ, grad_chunk, 0)
    rg_ring = ring_reduce(rg_part, rg_o, rg_i, rs_send.at[0], rs_recv.at[0])
    next(rg_ring)
    lax.fori_loop(0, NZ, down_chunk, 0)
    dn_ring = ring_reduce(dn_part, dn_o, dn_i, rs_send.at[1], rs_recv.at[1])
    next(rg_ring)
    next(rg_ring)
    next(dn_ring)
    next(rg_ring)
    next(rg_ring)

    def give_back(part, out, inn, index):
        out[...] = mm_tn(cmat[...], part[z].astype(BF16)).astype(BF16).reshape(NB, SLOT, COLS)
        a2a_start(out, inn, a2a_send.at[index], a2a_recv.at[index])

    give_back(rg_part, rg_out, rg_in, 2)
    next(dn_ring)

    a2a_wait(rg_in, a2a_recv.at[2])
    hidden = mm_tn(dmat[...], rg_in[...].reshape(NB * SLOT, COLS)).astype(BF16)
    hg_out[...] = (mm(ga[...], hidden[:, 0:TOK]) + mm(gb[...], hidden[:, TOK:COLS])).reshape(NB, 8, TOK)
    a2a_start(hg_out, hg_in, row_send.at[2], row_recv.at[2])
    next(dn_ring)
    next(dn_ring)
    next(dn_ring)
    give_back(dn_part, dn_out, dn_in, 3)

    a2a_wait(hg_in, row_recv.at[2])
    hg = hg_in[...].reshape(NB * 8, TOK).astype(BF16)
    hg_mine[:, 0:TOK] = mm_tn(sa[...], hg)[0:MR].astype(BF16)
    hg_mine[:, TOK:COLS] = mm_tn(sb[...], hg)[0:MR].astype(BF16)
    hg_all[e] = hg_mine[...]
    to_experts(lambda to: hg_mine, hg_all, e_send.at[3], e_recv.at[3])

    a2a_wait(dn_in, a2a_recv.at[3])
    dn = dn_in[...].reshape(NB * SLOT, COLS)
    mine_sum = mm_tn(dg_hi[...], dn) + mm_tn(dg_lo[...], dn)
    pair_out[...] = mine_sum.astype(BF16)
    send(pair_out, pair_in, pair_send.at[0], pair_recv.at[0], b, (1 - y) * NZ + z)

    wait_bytes(vis_all.at[pl.ds(0, NZ - 1)], z_recv.at[0])
    wait_bytes(cv_all.at[pl.ds(0, NZ - 1)], z_recv.at[1])
    wait_bytes(gw_all.at[pl.ds(0, NE - 1)], e_recv.at[0])
    wait_bytes(hg_all.at[pl.ds(0, NE - 1)], e_recv.at[3])
    wait_bytes(pair_in, pair_recv.at[0])
    layer = pair_out[...].astype(F32) + pair_in[...].astype(F32)
    llm_all[z] = (text[...].astype(F32) + layer).astype(BF16)
    llm_ring = ring_gather(llm_all, llm_send.at[0], llm_recv.at[0], TOK // 2)
    next(llm_ring)

    gw_sum = jnp.sum(gw_all[...], axis=0)
    ssq = jnp.zeros((MR, COLS), F32)
    cross = jnp.zeros((MR, COLS), F32)
    for c in range(NZ):
        v = vis_all[c].astype(F32)
        ghg = (hg_all[c].astype(F32) + hg_all[NZ + c].astype(F32)) * ng_ref[:, c * COLS : (c + 1) * COLS]
        ssq = ssq + v * v
        cross = cross + ghg * v
    r = lax.rsqrt(jnp.sum(ssq, axis=1, keepdims=True) * (1.0 / WIDTH) + EPS)
    pull = jnp.sum(cross, axis=1, keepdims=True) * (1.0 / WIDTH) * r * r * r
    dot_g = jnp.zeros((MR, COLS), F32)
    dot_v = jnp.zeros((MR, COLS), F32)
    back_scaled = jnp.zeros((4 * HD, TOK), F32)
    for c in range(NZ):
        v = vis_all[c].astype(F32)
        ghg = (hg_all[c].astype(F32) + hg_all[NZ + c].astype(F32)) * ng_ref[:, c * COLS : (c + 1) * COLS]
        vg = (cv_all[c].astype(F32) + (r * ghg - v * pull)).astype(BF16)
        wide = vg.astype(F32)
        dot_g = dot_g + wide * gw_sum[c : c + 1, :]
        dot_v = dot_v + wide * v
        four = jnp.concatenate([vg, vg, vg, vg], axis=0)
        back_scaled = back_scaled + mm_nt(mw[:, c * COLS : (c + 1) * COLS], four)
    next(llm_ring)

    def to_lanes(columns):
        column = jnp.sum(columns, axis=1, keepdims=True)
        column = jnp.concatenate([column, column, column, column], axis=0)
        eye = iota((TOK, TOK), 0) == iota((TOK, TOK), 1)
        return jnp.sum(jnp.where(eye, column, 0.0), axis=0, keepdims=True)

    grad_mean = to_lanes(dot_g) * (1.0 / MERGE)
    cross_mean = to_lanes(dot_v) * (1.0 / MERGE)
    scaled_grad = jnp.zeros((HD, TOK), F32)
    for i in range(4):
        scaled_grad = jnp.where(group == i, back_scaled[i * HD : (i + 1) * HD, :], scaled_grad)
    merged_grad = inv_std * (scaled_grad * gain_ref[...] - grad_mean - normed * cross_mean)
    li = iota((TOK, TOK), 0)
    unfold = jnp.where(iota((TOK, TOK), 1) == 4 * (li & 31) + (li >> 5), 1.0, 0.0).astype(BF16)
    part1 = merged_grad.astype(BF16)
    rest = merged_grad - part1.astype(F32)
    part2 = rest.astype(BF16)
    part3 = (rest - part2.astype(F32)).astype(BF16)
    ag_ref[...] = mm(part1, unfold) + mm(part2, unfold) + mm(part3, unfold)
    for _ in llm_ring:
        pass
    for c in range(NZ):
        llm_ref[:, c * COLS : (c + 1) * COLS] = llm_all[c]

    wait_bytes(kvb.at[pl.ds(0, NB - 1)], kv_send.at[0])
    for index, buf in enumerate((cot_out, h_out, rg_out, dn_out)):
        wait_bytes(buf.at[pl.ds(0, NB - 1)], a2a_send.at[index])
    for index, buf in enumerate((cv_out, vi_out, hg_out)):
        wait_bytes(buf.at[pl.ds(0, NB - 1)], row_send.at[index])
    for index, buf in enumerate((gw_all, st_all, vp_all, hg_all)):
        wait_bytes(buf.at[pl.ds(0, NE - 1)], e_send.at[index])
    for index, buf in enumerate((vis_all, cv_all)):
        wait_bytes(buf.at[pl.ds(0, NZ - 1)], z_send.at[index])
    for index, buf in enumerate((xc, xh)):
        wait_bytes(buf.at[pl.ds(0, NZ - 1)], ring_send.at[index])
    for index, buf in enumerate((rg_o, dn_o)):
        wait_bytes(buf.at[pl.ds(0, 14)], rs_send.at[index])
    wait_bytes(pair_out, pair_send.at[0])
    wait_bytes(llm_all.at[pl.ds(0, NZ - 1)], llm_send.at[0])


def scratch_shapes():
    V = pltpu.VMEM
    D = pltpu.SemaphoreType.DMA
    routed = [V((NB, SLOT, COLS), BF16)] * 8
    rows = [V((NB, 8, TOK), F32)] * 6
    reduce_bufs = [V((NZ, ROWS, COLS), F32), V((20, HALF, COLS), BF16), V((20, HALF, COLS), BF16)]
    return (
        [V((4 * HD, WIDTH), BF16), V((TOK, COLS), BF16), V((TOK, COLS), BF16)]
        + [V((FG, WIDTH), BF16)] * 5
        + [D((6,))]
        + [V((NB, KVR, TOK), BF16), V((NB * TOK, TOK), F32), D((1,)), D((NB,))]
        + [V((NB * SLOT, TOK), BF16)] * 3
        + [V((ROWS, NB * SLOT), BF16)]
        + [V((NB * 8, TOK), BF16)] * 4
        + routed + [D((4,)), D((4,))]
        + rows + [D((3,)), D((3,))]
        + [V((NE, NZ, COLS), F32), V((NE, 8, TOK), F32), V((NZ, MR, COLS), BF16), V((NE, MR, COLS), BF16)]
        + [V((NE, MR, COLS), BF16), V((MR, COLS), BF16), D((4,)), D((4,))]
        + [V((NZ, MR, COLS), BF16)] * 2 + [D((2,)), D((2,))]
        + [V((NZ, ROWS, COLS), BF16)] * 2 + [D((2,)), D((2, 16))]
        + [V((ROWS, FG), F32), V((ROWS, FG), F32), V((ROWS, TOK), F32), V((ROWS, FG), F32)]
        + reduce_bufs + reduce_bufs + [D((2,)), D((2, 20))]
        + [V((TOK, COLS), BF16)] * 2 + [D((1,)), D((1,))]
        + [V((NZ, TOK, COLS), BF16), D((1,)), D((1, 16))]
    )


def body(
    queries, keys, values, image_ids, placement, merge_gain, merge_weight, text, norm_gain,
    w_gate, w_up, w_down, routes, route_gates, cotangent,
):
    three = jnp.arange(3, dtype=jnp.int32)[:, None]
    dest = placement[:, 0]
    key_ids = (jnp.repeat(image_ids, 4)[None, :] == three).astype(BF16)
    place_row = jnp.pad(dest, (0, TOK - MR), constant_values=-1)[None, :]
    kv = jnp.concatenate(
        [keys[0], values[0], key_ids, place_row.astype(BF16), jnp.zeros((12, TOK), BF16)], axis=0
    )
    queries = queries[0].reshape(HD, MR, 4).transpose(0, 2, 1).reshape(HD, TOK)
    other = jnp.where(jnp.tile(image_ids, 4)[None, :] == three, 0.0, -1e30).astype(BF16)
    qp = jnp.concatenate([queries, jnp.zeros((HD, TOK), BF16), other, jnp.zeros((13, TOK), BF16)], axis=0)
    plc = jnp.broadcast_to(place_row, (8, TOK))
    gain = jnp.repeat(merge_gain.reshape(4, HD).T, MR, axis=1)
    gain_hi = merge_gain.astype(BF16)
    gain_lo = (merge_gain - gain_hi.astype(F32)).astype(BF16)
    gsp = jnp.concatenate([gain_hi, gain_lo, jnp.zeros((14, 4 * HD), BF16)], axis=0)
    vm = pl.BlockSpec(memory_space=pltpu.VMEM)
    anywhere = pl.BlockSpec(memory_space=pl.ANY)
    llm_out, attn_grad = pl.pallas_call(
        kernel,
        out_shape=(
            jax.ShapeDtypeStruct((TOK, WIDTH), BF16),
            jax.ShapeDtypeStruct((HD, TOK), F32),
        ),
        in_specs=[vm] * 8 + [anywhere] * 6,
        out_specs=(vm, vm),
        scratch_shapes=scratch_shapes(),
        compiler_params=pltpu.CompilerParams(
            collective_id=0, has_side_effects=True, vmem_limit_bytes=50 * 1024 * 1024
        ),
    )(
        qp, kv, plc, routes.T, route_gates.T, gain, gsp, norm_gain[None, :],
        merge_weight, text, cotangent, w_gate, w_up, w_down,
    )
    return llm_out, attn_grad[None]


def solution(mesh):
    return jax.shard_map(
        body,
        mesh=mesh,
        in_specs=(
            P("expert", None, "blk"),
            P("expert", None, "blk"),
            P("expert", None, "blk"),
            P("blk"),
            P("blk", None),
            P("expert", None),
            P("expert", None, None),
            P("blk", None),
            P(),
            P("blk", "expert", None),
            P("blk", "expert", None),
            P("blk", "expert", None),
            P("blk", None),
            P("blk", None),
            P("blk", None),
        ),
        out_specs=(P("blk", None), P("expert", None, "blk")),
        check_vma=False,
    )
```

```python
import jax
import jax.numpy as jnp
from jax import lax
from jax.experimental import pallas as pl
from jax.experimental.pallas import tpu as pltpu
from jax.sharding import PartitionSpec as P

MESH = pl.DeviceIdType.MESH
F32 = jnp.float32
BF16 = jnp.bfloat16
EPS = 1e-06
NB = 32
NE = 16
NZ = 8
HD = 72
CAPX = 10
SLOT = 16
ROWS = NB * CAPX
HALF = ROWS // 2
QUARTER = HALF // 2
SET = NB // 2
COLS = 256
TOK = 128
MR = 32
WIDTH = 2048
FG = 192
MERGE = 4608
VMEM_BYTES = 63 * 1024 * 1024
KVR = 160
STREAMS = ((1, 0, 4), (1, 1, 3), (-1, 0, 3), (-1, 1, 4))


def mm(a, b):
    return lax.dot_general(a, b, (((1,), (0,)), ((), ())), preferred_element_type=F32)


def mm_nt(a, b):
    return lax.dot_general(a, b, (((1,), (1,)), ((), ())), preferred_element_type=F32)


def mm_tn(a, b):
    return lax.dot_general(a, b, (((0,), (0,)), ((), ())), preferred_element_type=F32)


def iota(shape, dim):
    return lax.broadcasted_iota(jnp.int32, shape, dim)


def wait_bytes(ref, sem):
    pltpu.make_async_copy(ref, ref, sem).wait()


def kernel(
    q_hbm, k_hbm, v_hbm, ids_hbm, place_hbm, gain_hbm, mw_hbm, text_hbm, ng_hbm,
    wg_hbm, wu_hbm, wd_hbm, routes_hbm, gates_hbm, cot_hbm,
    llm_ref, ag_ref,
    q_in, k_in, v_in, ids_in, place_in, gain_in, ng_ref, routes_in, gates_in,
    mw, text, cot, wg, wu, wd, wgs, wus, local_sem,
    kvb, kv_send, kv_recv,
    dmat, dg_hi, dg_lo, cmat, ga, gb, sa, sb,
    cot_out, cot_in, h_out, h_in, rg_out, rg_in, dn_out, dn_in, a2a_send, a2a_recv, set_recv,
    cv_out, cv_in, vi_out, vi_in, hg_out, hg_in, row_send, row_recv,
    gw_all, st_all, vp, vp_all, hg_all, hg_mine, e_send, e_recv,
    vis_all, cv_all, z_send, z_recv,
    xc, xh, ring_send, ring_recv,
    gate_acc, up_acc, ss_acc, act_grad, hidden,
    rs_out, rs_in, rs_send, rs_recv,
    pair_out, pair_in, pair_send, pair_recv,
    llm_all, llm_send, llm_recv,
):
    b = lax.axis_index("blk")
    e = lax.axis_index("expert")
    y = e // NZ
    z = e % NZ
    core = b % 2
    x = (b // 2) % 4
    yh = b // 8

    def blk_of(yy, xx, cc):
        return (yy * 4 + xx) * 2 + cc

    def zdev(zz):
        return y * NZ + zz

    zcols = pl.ds(pl.multiple_of(z * COLS, COLS), COLS)
    pairs = (
        (k_hbm.at[0], k_in), (v_hbm.at[0], v_in), (ids_hbm, ids_in), (place_hbm, place_in), (q_hbm.at[0], q_in),
        (routes_hbm, routes_in), (gates_hbm, gates_in), (gain_hbm, gain_in), (ng_hbm, ng_ref),
        (cot_hbm.at[:, zcols], cot), (mw_hbm.at[0], mw), (text_hbm.at[:, zcols], text),
        (wg_hbm.at[0], wg), (wu_hbm.at[0], wu), (wd_hbm.at[0], wd),
    )
    locals_ = [pltpu.make_async_copy(src, dst, local_sem.at[i]) for i, (src, dst) in enumerate(pairs)]
    for copy in locals_:
        copy.start()

    barrier = pltpu.get_barrier_semaphore()

    def greet_blk(i, carry):
        pl.semaphore_signal(barrier, inc=1, device_id=((b + i) % NB, e), device_id_type=MESH)
        return carry

    def greet_expert(i, carry):
        pl.semaphore_signal(barrier, inc=1, device_id=(b, (e + i) % NE), device_id_type=MESH)
        return carry

    lax.fori_loop(1, NB, greet_blk, 0)
    lax.fori_loop(1, NE, greet_expert, 0)

    for copy in locals_[:4]:
        copy.wait()
    ids16 = jnp.broadcast_to(ids_in[...], (16, MR)).astype(F32).astype(BF16)
    ri = iota((MR, TOK), 0)
    li = iota((MR, TOK), 1)
    row16 = iota((16, TOK), 0)
    patch_ids = mm(ids16, jnp.where(li >> 2 == ri, 1.0, 0.0).astype(BF16))
    place16 = jnp.broadcast_to(place_in[...], (16, MR)).astype(F32).astype(BF16)
    place_row = mm(place16, jnp.where(li == ri, 1.0, 0.0).astype(BF16))[0:1, :]
    place_row = jnp.where(iota((1, TOK), 1) < MR, place_row, -1.0)
    extra = jnp.where(row16 < 3, jnp.where(patch_ids == row16.astype(F32), 1.0, 0.0), 0.0)
    extra = jnp.where(row16 == 3, place_row, extra)
    kvb[b] = jnp.concatenate([k_in[...].astype(F32), v_in[...].astype(F32), extra], axis=0).astype(BF16)
    pl.semaphore_wait(barrier, NB - 1 + NE - 1)

    def send(src, dst, ssem, rsem, db, de):
        pltpu.make_async_remote_copy(
            src_ref=src, dst_ref=dst, send_sem=ssem, recv_sem=rsem, device_id=(db, de), device_id_type=MESH
        ).start()

    def a2a_start(src, dst, ssem, rsem):
        dst[b] = src[b]

        def one(i, carry):
            to = (b + i) % NB
            send(src.at[to], dst.at[b], ssem, rsem, to, e)
            return carry

        lax.fori_loop(1, NB, one, 0)

    def a2a_wait(dst, rsem):
        wait_bytes(dst.at[pl.ds(0, NB - 1)], rsem)

    def step(i, sign):
        group = i // 8
        along = (2 * group + 1 + 3 * (group // 2)) % 4
        return ((yh + 4 + sign * along) % 4) * 8 + (b % 8 + 8 + sign * (i % 8)) % 8

    def dispatch(src, dst, ssem, rsems):
        def one(i, carry):
            to = step(i, 1)
            send(src.at[to], dst.at[i], ssem, rsems.at[i // SET], to, e)
            return carry

        lax.fori_loop(0, SET, one, 0)
        dst[SET] = src[b]
        lax.fori_loop(SET + 1, NB, one, 0)

    def dispatch_wait(dst, rsems, which):
        wait_bytes(dst.at[pl.ds(0, SET - which)], rsems.at[which])

    def packed(landed, which):
        rows = landed[pl.ds(which * SET, SET)].reshape(SET * SLOT, COLS)
        return mm(cmat[...], rows).astype(BF16)

    def to_experts(src_of, dst, ssem, rsem):
        def one(i, carry):
            to = (e + i) % NE
            send(src_of(to), dst.at[e], ssem, rsem, b, to)
            return carry

        lax.fori_loop(1, NE, one, 0)

    def to_z(src, dst, ssem, rsem):
        def one(i, carry):
            to = (z + i) % NZ
            send(src, dst.at[z], ssem, rsem, b, zdev(to))
            return carry

        lax.fori_loop(1, NZ, one, 0)

    def ring_gather(buf, ssem, rsems, first, size):
        def piece(src, half):
            return buf.at[src, pl.ds(first + half * size, size)]

        for k in range(5):
            for way, half, far in STREAMS:
                if k > far:
                    continue
                src = (z + 8 - way * k) % NZ
                if k > 0:
                    wait_bytes(piece(src, half), rsems.at[src * 2 + half])
                if k < far:
                    send(piece(src, half), piece(src, half), ssem, rsems.at[src * 2 + half], b, zdev((z + 8 + way) % NZ))
            yield k

    def ring_reduce(term, out, inn, ssem, rsems):
        for d in range(4, 0, -1):
            right = term((z + d) % NZ)
            terms = {1: right, -1: right if d == 4 else term((z + 8 - d) % NZ)}
            for starts in (True, False):
                for index, (way, half, far) in enumerate(STREAMS):
                    if d > far or starts != (d == far):
                        continue
                    value = terms[way][half * QUARTER : (half + 1) * QUARTER]
                    here = index * 5 + d
                    if d < far:
                        wait_bytes(inn.at[here], rsems.at[here])
                        value = value + inn[here].astype(F32)
                    out[here] = value.astype(BF16)
                    send(out.at[here], inn.at[here - 1], ssem, rsems.at[here - 1], b, zdev((z + 8 + way) % NZ))
            yield None
        own = term(z)
        for index in range(4):
            wait_bytes(inn.at[index * 5], rsems.at[index * 5])
        arrived = [inn[half * 5].astype(F32) + inn[(2 + half) * 5].astype(F32) for half in range(2)]
        yield own + jnp.concatenate(arrived, axis=0)

    def kv_go(block, to):
        send(kvb.at[block], kvb.at[block], kv_send.at[0], kv_recv.at[block], to, e)

    def kv_x(block):
        for dx in (1, 3, 2):
            kv_go(block, blk_of(yh, (x + dx) % 4, core))
        kv_go(block, blk_of(yh, x, 1 - core))

    for dy in (1, 3, 2):
        kv_go(b, blk_of((yh + dy) % 4, x, core))
    kv_x(b)

    for copy in locals_[4:9]:
        copy.wait()
    pi = iota((TOK, TOK), 0)
    pj = iota((TOK, TOK), 1)
    fold = jnp.where(pi == 4 * (pj & 31) + (pj >> 5), 1.0, 0.0).astype(BF16)
    row_ids = mm(ids16, jnp.where((li & 31) == ri, 1.0, 0.0).astype(BF16))
    shut = jnp.where((row16 < 3) & (row_ids != row16.astype(F32)), -1e30, 0.0)
    qp = jnp.concatenate([mm(q_in[...], fold), jnp.zeros((HD, TOK), F32), shut], axis=0).astype(BF16)
    unit = (iota((KVR, KVR), 0) == iota((KVR, KVR), 1)).astype(BF16)
    qt = mm_tn(qp, unit).astype(BF16)

    group = iota((HD, TOK), 1) >> 5
    fi = iota((HD, 4 * HD), 0)
    fj = iota((HD, 4 * HD), 1)
    gain = jnp.zeros((HD, TOK), F32)
    for i in range(4):
        column = jnp.sum(jnp.where(fj == fi + i * HD, gain_in[...], 0.0), axis=1, keepdims=True)
        gain = jnp.where(group == i, column, gain)
    gain_hi = gain_in[...].astype(BF16).astype(F32)
    gi = iota((16, 4 * HD), 0)
    gain_rows = jnp.where(gi == 0, gain_hi, jnp.where(gi == 1, gain_in[...] - gain_hi, 0.0)).astype(BF16)

    upper = (iota((TOK, TOK), 0) < iota((TOK, TOK), 1)).astype(BF16)
    ids = 2 * iota((NB, TOK), 0) + y
    hit = jnp.zeros((NB, TOK), F32)
    gate = jnp.zeros((NB, TOK), F32)
    for k in range(8):
        same = routes_in[k : k + 1, :] == ids
        hit = hit + jnp.where(same, 1.0, 0.0)
        gate = gate + jnp.where(same, gates_in[k : k + 1, :], 0.0)
    rank = mm(hit.astype(BF16), upper)
    place = jnp.where(hit > 0.0, rank, -1.0)
    slot3 = iota((NB, SLOT, TOK), 1).astype(F32)
    one_hot = jnp.where(place[:, None, :] == slot3, 1.0, 0.0)
    gated = (one_hot * gate[:, None, :]).reshape(NB * SLOT, TOK)
    dmat[...] = one_hot.reshape(NB * SLOT, TOK).astype(BF16)
    high = gated.astype(BF16)
    dg_hi[...] = high
    dg_lo[...] = (gated - high.astype(F32)).astype(BF16)
    slot_gate = jnp.sum(gated, axis=1, keepdims=True)
    locals_[9].wait()
    back = (mm(dmat[...], cot[...]) * slot_gate).astype(BF16)
    cot_out[...] = back.reshape(NB, SLOT, COLS)

    locals_[10].wait()
    gw = mm(gain_rows, mw[...])
    gw = gw[0:1, :] + gw[1:2, :]
    for c in range(NZ):
        gw_all[e, c : c + 1, :] = gw[:, c * COLS : (c + 1) * COLS]
    to_experts(lambda to: gw_all.at[e], gw_all, e_send.at[0], e_recv.at[0])

    for dy in (1, 3, 2):
        block = blk_of((yh + 4 - dy) % 4, x, core)
        wait_bytes(kvb.at[block], kv_recv.at[block])
        kv_x(block)
    dispatch(cot_out, cot_in, a2a_send.at[0], set_recv.at[0])

    ci = iota((HALF, SET * SLOT), 0)
    cj = iota((HALF, SET * SLOT), 1)
    cmat[...] = jnp.where((ci == (cj >> 4) * CAPX + (cj & 15)) & ((cj & 15) < CAPX), 1.0, 0.0).astype(BF16)

    def kv_arrive(xx, cc):
        for yy in range(4):
            block = blk_of((yh + yy) % 4, xx, cc)
            wait_bytes(kvb.at[block], kv_recv.at[block])

    def kv_pass(dx):
        def one(i, carry):
            block = blk_of((yh + 4 - i) % 4, (x + 4 - dx) % 4, core)
            wait_bytes(kvb.at[block], kv_recv.at[block])
            kv_go(block, blk_of(yh, x, 1 - core))
            return carry

        lax.fori_loop(0, 4, one, 0)

    def attend(state, xx, cc):
        top, total, acc = state
        block = jnp.concatenate([kvb[blk_of(yy, xx, cc)] for yy in range(4)], axis=1)
        s = mm(qt, block)
        new_top = jnp.maximum(top, jnp.max(s, axis=1, keepdims=True))
        shrink = jnp.exp((top - new_top) * (HD ** -0.5))
        w = jnp.exp((s - new_top) * (HD ** -0.5))
        total = total * shrink + jnp.sum(w, axis=1, keepdims=True)
        return new_top, total, acc * shrink + mm_nt(w.astype(BF16), block)

    state = (jnp.full((TOK, 1), -1e30, F32), jnp.zeros((TOK, 1), F32), jnp.zeros((TOK, KVR), F32))
    state = attend(state, x, core)
    kv_pass(1)
    kv_arrive(x, 1 - core)
    state = attend(state, x, 1 - core)
    kv_pass(3)
    state = attend(state, (x + 3) % 4, core)
    kv_pass(2)
    kv_arrive((x + 3) % 4, 1 - core)
    state = attend(state, (x + 3) % 4, 1 - core)
    state = attend(state, (x + 1) % 4, core)
    kv_arrive((x + 1) % 4, 1 - core)
    state = attend(state, (x + 1) % 4, 1 - core)
    for which in range(2):
        dispatch_wait(cot_in, set_recv.at[0], which)
        xc[z, pl.ds(which * HALF, HALF), :] = packed(cot_in, which)
    cot_ring = ring_gather(xc, ring_send.at[0], ring_recv.at[0], 0, HALF)
    next(cot_ring)
    state = attend(state, (x + 2) % 4, core)
    kv_arrive((x + 2) % 4, 1 - core)
    _, total, acc = attend(state, (x + 2) % 4, 1 - core)
    pick = (iota((HD, KVR), 1) == iota((HD, KVR), 0) + HD).astype(BF16)
    attn = mm_nt(pick, (acc / total).astype(BF16))

    def over_i(row):
        row = row + pltpu.roll(row, 32, 1)
        return row + pltpu.roll(row, 64, 1)

    local_mean = over_i(jnp.broadcast_to(jnp.sum(attn, axis=0, keepdims=True), (8, TOK)))[0:1, :] * (1.0 / (4 * HD))
    centred = attn - local_mean
    squares = over_i(jnp.broadcast_to(jnp.sum(centred * centred, axis=0, keepdims=True), (8, TOK)))
    st_all[e] = jnp.where(iota((8, TOK), 0) == 0, local_mean, squares)
    to_experts(lambda to: st_all.at[e], st_all, e_send.at[1], e_recv.at[1])
    scaled = centred * gain
    left = jnp.concatenate([jnp.where(group == i, scaled, 0.0) for i in range(4)], axis=0).astype(BF16)

    def merge_chunk(c):
        cols = pl.ds(pl.multiple_of(c * COLS, COLS), COLS)
        v = mm_tn(left, mw[:, cols])
        vp[c] = (v[0:32] + v[32:64] + v[64:96] + v[96:128]).astype(BF16)

    def merge_send(i, carry):
        c = (z + 1 + i) % NZ
        merge_chunk(c)
        send(vp.at[c], vp_all.at[e], e_send.at[2], e_recv.at[2], b, c)
        send(vp.at[c], vp_all.at[e], e_send.at[2], e_recv.at[2], b, NZ + c)
        return carry

    lax.fori_loop(0, NZ - 1, merge_send, 0)
    merge_chunk(z)
    vp_all[e] = vp[z]
    send(vp.at[z], vp_all.at[e], e_send.at[2], e_recv.at[2], b, (1 - y) * NZ + z)

    places = kvb[:, 144:160, :].astype(F32)
    places = jnp.sum(jnp.where(iota((NB, 16, TOK), 1) == 3, places, 0.0), axis=1)
    named = jnp.where(places == b.astype(F32), 1.0, 0.0)
    count = jnp.broadcast_to(jnp.sum(named, axis=1, keepdims=True), (NB, TOK))
    below = (iota((NB, NB), 1) < iota((NB, NB), 0)).astype(BF16)
    base = mm(below, count.astype(BF16))
    placed = jnp.sum(count, axis=0, keepdims=True)[:, 0:1]
    q3 = iota((NB, 8, TOK), 1).astype(F32)
    k3 = jnp.where(q3 < 4.0, q3, q3 - 4.0)
    lane3 = iota((NB, 8, TOK), 2).astype(F32)
    mine = jnp.where((lane3 == base[:, None, :] + k3) & (k3 < count[:, None, :]), 1.0, 0.0)
    ga[...] = jnp.where(q3 < 4.0, mine, 0.0).reshape(NB * 8, TOK).astype(BF16)
    gb[...] = jnp.where(q3 < 4.0, 0.0, mine).reshape(NB * 8, TOK).astype(BF16)
    to_shard = jnp.where(place_row == iota((NB, TOK), 0).astype(F32), 1.0, 0.0)
    order = mm(to_shard.astype(BF16), upper)
    order = jnp.where(to_shard > 0.0, order, -1.0)
    theirs = jnp.where(order[:, None, :] == k3, 1.0, 0.0)
    sa[...] = jnp.where(q3 < 4.0, theirs, 0.0).reshape(NB * 8, TOK).astype(BF16)
    sb[...] = jnp.where(q3 < 4.0, 0.0, theirs).reshape(NB * 8, TOK).astype(BF16)

    cv_out[...] = (mm(ga[...], cot[:, 0:TOK]) + mm(gb[...], cot[:, TOK:COLS])).reshape(NB, 8, TOK)
    a2a_start(cv_out, cv_in, row_send.at[0], row_recv.at[0])

    wait_bytes(gw_all.at[pl.ds(0, NE - 1)], e_recv.at[0])
    wait_bytes(st_all.at[pl.ds(0, NE - 1)], e_recv.at[1])
    row_stats = st_all[...]
    first = iota((NE, 8, TOK), 1) == 0
    means = jnp.sum(jnp.where(first, row_stats, 0.0), axis=1)
    mean = jnp.sum(means, axis=0, keepdims=True) * (1.0 / NE)
    spread = means - mean
    inner = jnp.sum(row_stats[:, 1:2, :], axis=0)
    variance = (inner + jnp.sum(spread * spread, axis=0, keepdims=True) * (4.0 * HD)) * (1.0 / MERGE)
    inv_std = lax.rsqrt(variance + EPS)
    normed = (attn - mean) * inv_std
    here_z = iota((NE, NZ, COLS), 1) == z
    gw_slice = jnp.sum(jnp.where(here_z, gw_all[...], 0.0), axis=1)
    shift = lax.dot_general(
        spread, gw_slice, (((0,), (0,)), ((), ())), preferred_element_type=F32, precision=lax.Precision.HIGHEST
    )[0:MR]
    inv_column = jnp.sum(jnp.where(pi == pj, inv_std, 0.0), axis=1, keepdims=True)[0:MR]
    wait_bytes(vp_all.at[pl.ds(0, NE - 1)], e_recv.at[2])
    next(cot_ring)
    vision = ((jnp.sum(vp_all[...].astype(F32), axis=0) + shift) * inv_column).astype(BF16)
    vis_all[z] = vision
    fill = jnp.zeros((TOK - MR, COLS), BF16)
    padded = jnp.concatenate([vision, fill], axis=0)
    vi_out[...] = (mm(sa[...], padded[:, 0:TOK]) + mm(sb[...], padded[:, TOK:COLS])).reshape(NB, 8, TOK)
    a2a_start(vi_out, vi_in, row_send.at[1], row_recv.at[1])
    to_z(vis_all.at[z], vis_all, z_send.at[0], z_recv.at[0])

    locals_[12].wait()
    locals_[13].wait()

    def gain_chunk(c, carry):
        cols = pl.ds(pl.multiple_of(c * COLS, COLS), COLS)
        g = ng_ref[:, cols]
        wgs[:, cols] = (wg[:, cols].astype(F32) * g).astype(BF16)
        wus[:, cols] = (wu[:, cols].astype(F32) * g).astype(BF16)
        return carry

    lax.fori_loop(0, NZ, gain_chunk, 0)
    next(cot_ring)
    a2a_wait(cv_in, row_recv.at[0])
    cv = cv_in[...].reshape(NB * 8, TOK).astype(BF16)
    cv_all[z, :, 0:TOK] = mm_tn(sa[...], cv)[0:MR].astype(BF16)
    cv_all[z, :, TOK:COLS] = mm_tn(sb[...], cv)[0:MR].astype(BF16)
    to_z(cv_all.at[z], cv_all, z_send.at[1], z_recv.at[1])

    locals_[11].wait()
    a2a_wait(vi_in, row_recv.at[1])
    arrived = vi_in[...].reshape(NB * 8, TOK).astype(BF16)
    taken = iota((TOK, TOK), 0).astype(F32) < placed
    llm_a = jnp.where(taken, mm_tn(ga[...], arrived), text[:, 0:TOK].astype(F32))
    llm_b = jnp.where(taken, mm_tn(gb[...], arrived), text[:, TOK:COLS].astype(F32))
    text[:, 0:TOK] = llm_a.astype(BF16)
    text[:, TOK:COLS] = llm_b.astype(BF16)
    h_out[...] = mm(dmat[...], text[...]).astype(BF16).reshape(NB, SLOT, COLS)
    dispatch(h_out, h_in, a2a_send.at[1], set_recv.at[1])

    for _ in cot_ring:
        pass
    locals_[14].wait()
    act_grad[...] = jnp.zeros_like(act_grad)
    gate_acc[...] = jnp.zeros_like(gate_acc)
    up_acc[...] = jnp.zeros_like(up_acc)
    ss_acc[...] = jnp.zeros_like(ss_acc)

    def act_chunk(c, carry):
        cols = pl.ds(pl.multiple_of(c * COLS, COLS), COLS)
        act_grad[...] += mm_nt(xc[c], wd[:, cols])
        return carry

    lax.fori_loop(0, NZ, act_chunk, 0)

    def project(c, which):
        cols = pl.ds(pl.multiple_of(c * COLS, COLS), COLS)
        part = pl.ds(which * HALF, HALF)
        rows = xh[c, part, :]
        gate_acc[part, :] += mm_nt(rows, wgs[:, cols])
        up_acc[part, :] += mm_nt(rows, wus[:, cols])
        wide = rows.astype(F32)
        ss_acc[part, :] += wide[:, 0:TOK] * wide[:, 0:TOK] + wide[:, TOK:COLS] * wide[:, TOK:COLS]

    h_rings = [
        ring_gather(xh, ring_send.at[1 + which], ring_recv.at[1 + which], which * HALF, QUARTER) for which in range(2)
    ]

    def h_round(k, which):
        if k == 0:
            dispatch_wait(h_in, set_recv.at[1], which)
            xh[z, pl.ds(which * HALF, HALF), :] = packed(h_in, which)
        next(h_rings[which])
        project((z + k) % NZ, which)
        if 0 < k < 4:
            project((z + 8 - k) % NZ, which)

    def hidden_units(which):
        part = pl.ds(which * HALF, HALF)
        inv = lax.rsqrt(jnp.sum(ss_acc[part, :], axis=1, keepdims=True) * (1.0 / WIDTH) + EPS)
        gate_pre = gate_acc[part, :] * inv
        up_proj = up_acc[part, :] * inv
        sig = 1.0 / (1.0 + jnp.exp(-gate_pre))
        grad = act_grad[part, :]
        hidden[0, part, :] = (grad * up_proj * sig * (1.0 + gate_pre * (1.0 - sig))).astype(BF16)
        hidden[1, part, :] = (grad * gate_pre * sig).astype(BF16)
        hidden[2, part, :] = (gate_pre * sig * up_proj).astype(BF16)

    def reducers(which):
        part = pl.ds(which * HALF, HALF)

        def grad_term(c):
            cols = pl.ds(pl.multiple_of(c * COLS, COLS), COLS)
            return mm(hidden[0, part, :], wg[:, cols]) + mm(hidden[1, part, :], wu[:, cols])

        def down_term(c):
            cols = pl.ds(pl.multiple_of(c * COLS, COLS), COLS)
            return mm(hidden[2, part, :], wd[:, cols])

        return [
            ring_reduce(term, rs_out.at[2 * which + j], rs_in.at[2 * which + j], rs_send.at[0], rs_recv.at[2 * which + j])
            for j, term in enumerate((down_term, grad_term))
        ]

    rings = [reducers(which) for which in range(2)]

    def reduce_round(which):
        for ring in rings[which]:
            next(ring)

    def give_back(which):
        for j, (out, inn) in enumerate(((dn_out, dn_in), (rg_out, rg_in))):
            rows = next(rings[which][j]).astype(BF16)
            out[pl.ds(which * SET, SET)] = mm_tn(cmat[...], rows).astype(BF16).reshape(SET, SLOT, COLS)
            if which == 1:
                inn[b] = out[SET]

            def one(i, carry):
                to = step(i, -1)
                send(out.at[i], inn.at[b], a2a_send.at[2 + j], a2a_recv.at[j], to, e)
                return carry

            lax.fori_loop(which * (SET + 1), SET + which * SET, one, 0)

    for k in range(4):
        h_round(k, 0)
        h_round(k, 1)
    h_round(4, 0)
    hidden_units(0)
    reduce_round(0)
    h_round(4, 1)
    hidden_units(1)
    reduce_round(0)
    reduce_round(1)
    reduce_round(0)
    reduce_round(1)
    reduce_round(0)
    reduce_round(1)
    give_back(0)
    reduce_round(1)
    give_back(1)

    a2a_wait(dn_in, a2a_recv.at[0])
    dn = dn_in[...].reshape(NB * SLOT, COLS)
    mine_sum = mm_tn(dg_hi[...], dn) + mm_tn(dg_lo[...], dn)
    pair_out[...] = mine_sum.astype(BF16)
    send(pair_out, pair_in, pair_send.at[0], pair_recv.at[0], b, (1 - y) * NZ + z)

    a2a_wait(rg_in, a2a_recv.at[1])
    token_grad = mm_tn(dmat[...], rg_in[...].reshape(NB * SLOT, COLS)).astype(BF16)
    hg_out[...] = (mm(ga[...], token_grad[:, 0:TOK]) + mm(gb[...], token_grad[:, TOK:COLS])).reshape(NB, 8, TOK)
    a2a_start(hg_out, hg_in, row_send.at[2], row_recv.at[2])

    wait_bytes(pair_in, pair_recv.at[0])
    layer = pair_out[...].astype(F32) + pair_in[...].astype(F32)
    llm_all[z] = (text[...].astype(F32) + layer).astype(BF16)
    llm_ring = ring_gather(llm_all, llm_send.at[0], llm_recv.at[0], 0, TOK // 2)
    next(llm_ring)
    next(llm_ring)
    next(llm_ring)
    a2a_wait(hg_in, row_recv.at[2])
    hg = hg_in[...].reshape(NB * 8, TOK).astype(BF16)
    hg_mine[:, 0:TOK] = mm_tn(sa[...], hg)[0:MR].astype(BF16)
    hg_mine[:, TOK:COLS] = mm_tn(sb[...], hg)[0:MR].astype(BF16)
    hg_all[e] = hg_mine[...]
    to_experts(lambda to: hg_mine, hg_all, e_send.at[3], e_recv.at[3])

    wait_bytes(vis_all.at[pl.ds(0, NZ - 1)], z_recv.at[0])
    wait_bytes(cv_all.at[pl.ds(0, NZ - 1)], z_recv.at[1])
    wait_bytes(hg_all.at[pl.ds(0, NE - 1)], e_recv.at[3])

    gw_sum = jnp.sum(gw_all[...], axis=0)
    ssq = jnp.zeros((MR, COLS), F32)
    cross = jnp.zeros((MR, COLS), F32)
    for c in range(NZ):
        v = vis_all[c].astype(F32)
        ghg = (hg_all[c].astype(F32) + hg_all[NZ + c].astype(F32)) * ng_ref[:, c * COLS : (c + 1) * COLS]
        ssq = ssq + v * v
        cross = cross + ghg * v
    r = lax.rsqrt(jnp.sum(ssq, axis=1, keepdims=True) * (1.0 / WIDTH) + EPS)
    pull = jnp.sum(cross, axis=1, keepdims=True) * (1.0 / WIDTH) * r * r * r
    dot_g = jnp.zeros((MR, COLS), F32)
    dot_v = jnp.zeros((MR, COLS), F32)
    back_scaled = jnp.zeros((4 * HD, TOK), F32)
    for c in range(NZ):
        v = vis_all[c].astype(F32)
        ghg = (hg_all[c].astype(F32) + hg_all[NZ + c].astype(F32)) * ng_ref[:, c * COLS : (c + 1) * COLS]
        vg = (cv_all[c].astype(F32) + (r * ghg - v * pull)).astype(BF16)
        wide = vg.astype(F32)
        dot_g = dot_g + wide * gw_sum[c : c + 1, :]
        dot_v = dot_v + wide * v
        four = jnp.concatenate([vg, vg, vg, vg], axis=0)
        back_scaled = back_scaled + mm_nt(mw[:, c * COLS : (c + 1) * COLS], four)
    next(llm_ring)

    def to_lanes(columns):
        column = jnp.sum(columns, axis=1, keepdims=True)
        column = jnp.concatenate([column, column, column, column], axis=0)
        eye = iota((TOK, TOK), 0) == iota((TOK, TOK), 1)
        return jnp.sum(jnp.where(eye, column, 0.0), axis=0, keepdims=True)

    grad_mean = to_lanes(dot_g) * (1.0 / MERGE)
    cross_mean = to_lanes(dot_v) * (1.0 / MERGE)
    scaled_grad = jnp.zeros((HD, TOK), F32)
    for i in range(4):
        scaled_grad = jnp.where(group == i, back_scaled[i * HD : (i + 1) * HD, :], scaled_grad)
    merged_grad = inv_std * (scaled_grad * gain - grad_mean - normed * cross_mean)
    unfold = jnp.where(pj == 4 * (pi & 31) + (pi >> 5), 1.0, 0.0).astype(BF16)
    part1 = merged_grad.astype(BF16)
    rest = merged_grad - part1.astype(F32)
    part2 = rest.astype(BF16)
    part3 = (rest - part2.astype(F32)).astype(BF16)
    ag_ref[...] = mm(part1, unfold) + mm(part2, unfold) + mm(part3, unfold)
    for _ in llm_ring:
        pass
    for c in range(NZ):
        llm_ref[:, c * COLS : (c + 1) * COLS] = llm_all[c]

    wait_bytes(kvb.at[pl.ds(0, NB - 1)], kv_send.at[0])
    for index, buf in enumerate((cot_out, h_out, dn_out, rg_out)):
        wait_bytes(buf.at[pl.ds(0, NB - 1)], a2a_send.at[index])
    for index, buf in enumerate((cv_out, vi_out, hg_out)):
        wait_bytes(buf.at[pl.ds(0, NB - 1)], row_send.at[index])
    for index, buf in enumerate((gw_all, st_all, vp_all, hg_all)):
        wait_bytes(buf.at[pl.ds(0, NE - 1)], e_send.at[index])
    for index, buf in enumerate((vis_all, cv_all)):
        wait_bytes(buf.at[pl.ds(0, NZ - 1)], z_send.at[index])
    wait_bytes(xc.at[pl.ds(0, NZ - 1)], ring_send.at[0])
    for index in range(2):
        wait_bytes(xh.at[pl.ds(0, NZ - 1), pl.ds(0, HALF)], ring_send.at[1 + index])
    wait_bytes(rs_out.at[:, pl.ds(0, 14)], rs_send.at[0])
    wait_bytes(pair_out, pair_send.at[0])
    wait_bytes(llm_all.at[pl.ds(0, NZ - 1)], llm_send.at[0])


def scratch_shapes():
    V = pltpu.VMEM
    D = pltpu.SemaphoreType.DMA
    routed = [V((NB, SLOT, COLS), BF16)] * 8
    rows = [V((NB, 8, TOK), F32)] * 6
    return (
        [V((HD, TOK), BF16)] * 3
        + [V((1, MR), jnp.int32), V((1, MR), jnp.int32), V((1, 4 * HD), F32), V((1, WIDTH), F32)]
        + [V((8, TOK), jnp.int32), V((8, TOK), F32)]
        + [V((4 * HD, WIDTH), BF16), V((TOK, COLS), BF16), V((TOK, COLS), BF16)]
        + [V((FG, WIDTH), BF16)] * 5
        + [D((15,))]
        + [V((NB, KVR, TOK), BF16), D((1,)), D((NB,))]
        + [V((NB * SLOT, TOK), BF16)] * 3
        + [V((HALF, SET * SLOT), BF16)]
        + [V((NB * 8, TOK), BF16)] * 4
        + routed + [D((4,)), D((2,)), D((2, 2))]
        + rows + [D((3,)), D((3,))]
        + [V((NE, NZ, COLS), F32), V((NE, 8, TOK), F32), V((NZ, MR, COLS), BF16), V((NE, MR, COLS), BF16)]
        + [V((NE, MR, COLS), BF16), V((MR, COLS), BF16), D((4,)), D((4,))]
        + [V((NZ, MR, COLS), BF16)] * 2 + [D((2,)), D((2,))]
        + [V((NZ, ROWS, COLS), BF16)] * 2 + [D((3,)), D((3, 16))]
        + [V((ROWS, FG), F32), V((ROWS, FG), F32), V((ROWS, TOK), F32), V((ROWS, FG), F32), V((3, ROWS, FG), BF16)]
        + [V((4, 20, QUARTER, COLS), BF16)] * 2 + [D((1,)), D((4, 20))]
        + [V((TOK, COLS), BF16)] * 2 + [D((1,)), D((1,))]
        + [V((NZ, TOK, COLS), BF16), D((1,)), D((1, 16))]
    )


def body(
    queries, keys, values, image_ids, placement, merge_gain, merge_weight, text, norm_gain,
    w_gate, w_up, w_down, routes, route_gates, cotangent,
):
    vm = pl.BlockSpec(memory_space=pltpu.VMEM)
    anywhere = pl.BlockSpec(memory_space=pl.ANY)
    llm_out, attn_grad = pl.pallas_call(
        kernel,
        out_shape=(
            jax.ShapeDtypeStruct((TOK, WIDTH), BF16),
            jax.ShapeDtypeStruct((HD, TOK), F32),
        ),
        in_specs=[anywhere] * 15,
        out_specs=(vm, vm),
        scratch_shapes=scratch_shapes(),
        compiler_params=pltpu.CompilerParams(
            collective_id=0, has_side_effects=True, vmem_limit_bytes=VMEM_BYTES
        ),
    )(
        queries, keys, values, image_ids[None, :], placement.T, merge_gain, merge_weight, text, norm_gain[None, :],
        w_gate, w_up, w_down, routes.T, route_gates.T, cotangent,
    )
    return llm_out, attn_grad[None]


def solution(mesh):
    return jax.shard_map(
        body,
        mesh=mesh,
        in_specs=(
            P("expert", None, "blk"),
            P("expert", None, "blk"),
            P("expert", None, "blk"),
            P("blk"),
            P("blk", None),
            P("expert", None),
            P("expert", None, None),
            P("blk", None),
            P(),
            P("blk", "expert", None),
            P("blk", "expert", None),
            P("blk", "expert", None),
            P("blk", None),
            P("blk", None),
            P("blk", None),
        ),
        out_specs=(P("blk", None), P("expert", None, "blk")),
        check_vma=False,
    )
```

```python
import jax
import jax.numpy as jnp
from jax import lax
from jax.experimental import pallas as pl
from jax.experimental.pallas import tpu as pltpu
from jax.sharding import PartitionSpec as P

MESH = pl.DeviceIdType.MESH
F32 = jnp.float32
BF16 = jnp.bfloat16
EPS = 1e-06
NB = 32
NE = 16
NZ = 8
HD = 72
CAPX = 10
SLOT = 16
ROWS = NB * CAPX
HALF = ROWS // 2
QUARTER = HALF // 2
SET = NB // 2
COLS = 256
TOK = 128
MR = 32
WIDTH = 2048
FG = 192
MERGE = 4608
VMEM_BYTES = 63 * 1024 * 1024
KVR = 160
STREAMS = ((1, 0, 4), (1, 1, 3), (-1, 0, 3), (-1, 1, 4))


def mm(a, b):
    return lax.dot_general(a, b, (((1,), (0,)), ((), ())), preferred_element_type=F32)


def mm_nt(a, b):
    return lax.dot_general(a, b, (((1,), (1,)), ((), ())), preferred_element_type=F32)


def mm_tn(a, b):
    return lax.dot_general(a, b, (((0,), (0,)), ((), ())), preferred_element_type=F32)


def iota(shape, dim):
    return lax.broadcasted_iota(jnp.int32, shape, dim)


def wait_bytes(ref, sem):
    pltpu.make_async_copy(ref, ref, sem).wait()


def kernel(
    q_hbm, k_hbm, v_hbm, ids_hbm, place_hbm, gain_hbm, mw_hbm, text_hbm, ng_hbm,
    wg_hbm, wu_hbm, wd_hbm, routes_hbm, gates_hbm, cot_hbm,
    llm_ref, ag_ref,
    q_in, k_in, v_in, ids_in, place_in, gain_in, ng_ref, routes_in, gates_in,
    mw, text, cot, wg, wu, wd, wgs, wus, local_sem,
    kvb, kv_send, kv_recv,
    dmat, dg_hi, dg_lo, cmat, ga, gb, sa, sb,
    cot_out, cot_in, h_out, h_in, rg_out, rg_in, dn_out, dn_in, a2a_send, a2a_recv, set_recv,
    cv_out, cv_in, vi_out, vi_in, hg_out, hg_in, row_send, row_recv,
    gw_all, st_all, vp, vp_all, hg_all, hg_mine, e_send, e_recv,
    vis_all, cv_all, z_send, z_recv,
    xc, xh, ring_send, ring_recv,
    gate_acc, up_acc, ss_acc, act_grad, hidden,
    rs_out, rs_in, rs_send, rs_recv,
    pair_out, pair_in, pair_send, pair_recv,
    llm_all, llm_send, llm_recv,
):
    b = lax.axis_index("blk")
    e = lax.axis_index("expert")
    y = e // NZ
    z = e % NZ
    core = b % 2
    x = (b // 2) % 4
    yh = b // 8

    def blk_of(yy, xx, cc):
        return (yy * 4 + xx) * 2 + cc

    def zdev(zz):
        return y * NZ + zz

    zcols = pl.ds(pl.multiple_of(z * COLS, COLS), COLS)
    pairs = (
        (k_hbm.at[0], k_in), (v_hbm.at[0], v_in), (ids_hbm, ids_in), (place_hbm, place_in), (q_hbm.at[0], q_in),
        (routes_hbm, routes_in), (gates_hbm, gates_in), (gain_hbm, gain_in), (ng_hbm, ng_ref),
        (cot_hbm.at[:, zcols], cot), (mw_hbm.at[0], mw), (text_hbm.at[:, zcols], text),
        (wg_hbm.at[0], wg), (wu_hbm.at[0], wu), (wd_hbm.at[0], wd),
    )
    locals_ = [pltpu.make_async_copy(src, dst, local_sem.at[i]) for i, (src, dst) in enumerate(pairs)]
    for copy in locals_:
        copy.start()

    barrier = pltpu.get_barrier_semaphore()

    def greet_blk(i, carry):
        pl.semaphore_signal(barrier, inc=1, device_id=((b + i) % NB, e), device_id_type=MESH)
        return carry

    def greet_expert(i, carry):
        pl.semaphore_signal(barrier, inc=1, device_id=(b, (e + i) % NE), device_id_type=MESH)
        return carry

    lax.fori_loop(1, NB, greet_blk, 0)
    lax.fori_loop(1, NE, greet_expert, 0)

    for copy in locals_[:4]:
        copy.wait()
    ids16 = jnp.broadcast_to(ids_in[...], (16, MR)).astype(F32).astype(BF16)
    ri = iota((MR, TOK), 0)
    li = iota((MR, TOK), 1)
    row16 = iota((16, TOK), 0)
    patch_ids = mm(ids16, jnp.where(li >> 2 == ri, 1.0, 0.0).astype(BF16))
    place16 = jnp.broadcast_to(place_in[...], (16, MR)).astype(F32).astype(BF16)
    place_row = mm(place16, jnp.where(li == ri, 1.0, 0.0).astype(BF16))[0:1, :]
    place_row = jnp.where(iota((1, TOK), 1) < MR, place_row, -1.0)
    extra = jnp.where(row16 < 3, jnp.where(patch_ids == row16.astype(F32), 1.0, 0.0), 0.0)
    extra = jnp.where(row16 == 3, place_row, extra)
    kvb[b] = jnp.concatenate([k_in[...].astype(F32), v_in[...].astype(F32), extra], axis=0).astype(BF16)
    pl.semaphore_wait(barrier, NB - 1 + NE - 1)

    def send(src, dst, ssem, rsem, db, de):
        pltpu.make_async_remote_copy(
            src_ref=src, dst_ref=dst, send_sem=ssem, recv_sem=rsem, device_id=(db, de), device_id_type=MESH
        ).start()

    def a2a_start(src, dst, ssem, rsem):
        dst[b] = src[b]

        def one(i, carry):
            to = (b + i) % NB
            send(src.at[to], dst.at[b], ssem, rsem, to, e)
            return carry

        lax.fori_loop(1, NB, one, 0)

    def a2a_wait(dst, rsem):
        wait_bytes(dst.at[pl.ds(0, NB - 1)], rsem)

    within = lax.rem(b, 8)

    def steps(which, sign, go):
        for group in (0, 1):
            along = ((1, 3), (0, 2))[which][group]
            base = lax.rem(yh + 4 + sign * along, 4) * 8

            def one(j, carry):
                go(which * SET + group * 8 + j, base + lax.rem(within + 8 + sign * j, 8))
                return carry

            lax.fori_loop(0 if along > 0 else 1, 8, one, 0)

    def dispatch(src, dst, ssem, rsems):
        for which in (0, 1):
            steps(which, 1, lambda i, to: send(src.at[to], dst.at[i], ssem, rsems.at[which], to, e))
        dst[SET] = src[b]

    def dispatch_wait(dst, rsems, which):
        wait_bytes(dst.at[pl.ds(0, SET - which)], rsems.at[which])

    def packed(landed, which):
        rows = landed[pl.ds(which * SET, SET)].reshape(SET * SLOT, COLS)
        return mm(cmat[...], rows).astype(BF16)

    def to_experts(src_of, dst, ssem, rsem):
        def one(i, carry):
            to = (e + i) % NE
            send(src_of(to), dst.at[e], ssem, rsem, b, to)
            return carry

        lax.fori_loop(1, NE, one, 0)

    def to_z(src, dst, ssem, rsem):
        def one(i, carry):
            to = (z + i) % NZ
            send(src, dst.at[z], ssem, rsem, b, zdev(to))
            return carry

        lax.fori_loop(1, NZ, one, 0)

    def ring_gather(buf, ssem, rsems, first, size):
        def piece(src, half):
            return buf.at[src, pl.ds(first + half * size, size)]

        for k in range(5):
            for way, half, far in STREAMS:
                if k > far:
                    continue
                src = (z + 8 - way * k) % NZ
                if k > 0:
                    wait_bytes(piece(src, half), rsems.at[src * 2 + half])
                if k < far:
                    send(piece(src, half), piece(src, half), ssem, rsems.at[src * 2 + half], b, zdev((z + 8 + way) % NZ))
            yield k

    def ring_reduce(term, out, inn, ssem, rsems):
        for d in range(4, 0, -1):
            right = term((z + d) % NZ)
            terms = {1: right, -1: right if d == 4 else term((z + 8 - d) % NZ)}
            for starts in (True, False):
                for index, (way, half, far) in enumerate(STREAMS):
                    if d > far or starts != (d == far):
                        continue
                    value = terms[way][half * QUARTER : (half + 1) * QUARTER]
                    here = index * 5 + d
                    if d < far:
                        wait_bytes(inn.at[here], rsems.at[here])
                        value = value + inn[here].astype(F32)
                    out[here] = value.astype(BF16)
                    send(out.at[here], inn.at[here - 1], ssem, rsems.at[here - 1], b, zdev((z + 8 + way) % NZ))
            yield None
        own = term(z)
        for index in range(4):
            wait_bytes(inn.at[index * 5], rsems.at[index * 5])
        arrived = [inn[half * 5].astype(F32) + inn[(2 + half) * 5].astype(F32) for half in range(2)]
        yield own + jnp.concatenate(arrived, axis=0)

    def kv_go(block, to):
        send(kvb.at[block], kvb.at[block], kv_send.at[0], kv_recv.at[block], to, e)

    def kv_x(block):
        for dx in (1, 3, 2):
            kv_go(block, blk_of(yh, (x + dx) % 4, core))
        kv_go(block, blk_of(yh, x, 1 - core))

    for dy in (1, 3, 2):
        kv_go(b, blk_of((yh + dy) % 4, x, core))
    kv_x(b)

    for copy in locals_[4:9]:
        copy.wait()
    pi = iota((TOK, TOK), 0)
    pj = iota((TOK, TOK), 1)
    fold = jnp.where(pi == 4 * (pj & 31) + (pj >> 5), 1.0, 0.0).astype(BF16)
    row_ids = mm(ids16, jnp.where((li & 31) == ri, 1.0, 0.0).astype(BF16))
    shut = jnp.where((row16 < 3) & (row_ids != row16.astype(F32)), -1e30, 0.0)
    qp = jnp.concatenate([mm(q_in[...], fold), jnp.zeros((HD, TOK), F32), shut], axis=0).astype(BF16)
    unit = (iota((KVR, KVR), 0) == iota((KVR, KVR), 1)).astype(BF16)
    qt = mm_tn(qp, unit).astype(BF16)

    group = iota((HD, TOK), 1) >> 5
    fi = iota((HD, 4 * HD), 0)
    fj = iota((HD, 4 * HD), 1)
    gain = jnp.zeros((HD, TOK), F32)
    for i in range(4):
        column = jnp.sum(jnp.where(fj == fi + i * HD, gain_in[...], 0.0), axis=1, keepdims=True)
        gain = jnp.where(group == i, column, gain)
    gain_hi = gain_in[...].astype(BF16).astype(F32)
    gi = iota((16, 4 * HD), 0)
    gain_rows = jnp.where(gi == 0, gain_hi, jnp.where(gi == 1, gain_in[...] - gain_hi, 0.0)).astype(BF16)

    upper = (iota((TOK, TOK), 0) < iota((TOK, TOK), 1)).astype(BF16)
    ids = 2 * iota((NB, TOK), 0) + y
    hit = jnp.zeros((NB, TOK), F32)
    gate = jnp.zeros((NB, TOK), F32)
    for k in range(8):
        same = routes_in[k : k + 1, :] == ids
        hit = hit + jnp.where(same, 1.0, 0.0)
        gate = gate + jnp.where(same, gates_in[k : k + 1, :], 0.0)
    rank = mm(hit.astype(BF16), upper)
    place = jnp.where(hit > 0.0, rank, -1.0)
    slot3 = iota((NB, SLOT, TOK), 1).astype(F32)
    one_hot = jnp.where(place[:, None, :] == slot3, 1.0, 0.0)
    gated = (one_hot * gate[:, None, :]).reshape(NB * SLOT, TOK)
    dmat[...] = one_hot.reshape(NB * SLOT, TOK).astype(BF16)
    high = gated.astype(BF16)
    dg_hi[...] = high
    dg_lo[...] = (gated - high.astype(F32)).astype(BF16)
    slot_gate = jnp.sum(gated, axis=1, keepdims=True)
    locals_[9].wait()
    back = (mm(dmat[...], cot[...]) * slot_gate).astype(BF16)
    cot_out[...] = back.reshape(NB, SLOT, COLS)
    dispatch(cot_out, cot_in, a2a_send.at[0], set_recv.at[0])

    locals_[10].wait()
    gw = mm(gain_rows, mw[...])
    gw = gw[0:1, :] + gw[1:2, :]
    for c in range(NZ):
        gw_all[e, c : c + 1, :] = gw[:, c * COLS : (c + 1) * COLS]
    to_experts(lambda to: gw_all.at[e], gw_all, e_send.at[0], e_recv.at[0])

    for dy in (1, 3, 2):
        block = blk_of((yh + 4 - dy) % 4, x, core)
        wait_bytes(kvb.at[block], kv_recv.at[block])
        kv_x(block)

    ci = iota((HALF, SET * SLOT), 0)
    cj = iota((HALF, SET * SLOT), 1)
    cmat[...] = jnp.where((ci == (cj >> 4) * CAPX + (cj & 15)) & ((cj & 15) < CAPX), 1.0, 0.0).astype(BF16)

    def kv_arrive(xx, cc):
        for yy in range(4):
            block = blk_of((yh + yy) % 4, xx, cc)
            wait_bytes(kvb.at[block], kv_recv.at[block])

    def kv_pass(dx):
        def one(i, carry):
            block = blk_of((yh + 4 - i) % 4, (x + 4 - dx) % 4, core)
            wait_bytes(kvb.at[block], kv_recv.at[block])
            kv_go(block, blk_of(yh, x, 1 - core))
            return carry

        lax.fori_loop(0, 4, one, 0)

    def attend(state, xx, cc):
        top, total, acc = state
        block = jnp.concatenate([kvb[blk_of(yy, xx, cc)] for yy in range(4)], axis=1)
        s = mm(qt, block)
        new_top = jnp.maximum(top, jnp.max(s, axis=1, keepdims=True))
        shrink = jnp.exp((top - new_top) * (HD ** -0.5))
        w = jnp.exp((s - new_top) * (HD ** -0.5))
        total = total * shrink + jnp.sum(w, axis=1, keepdims=True)
        return new_top, total, acc * shrink + mm_nt(w.astype(BF16), block)

    state = (jnp.full((TOK, 1), -1e30, F32), jnp.zeros((TOK, 1), F32), jnp.zeros((TOK, KVR), F32))
    state = attend(state, x, core)
    kv_pass(1)
    kv_arrive(x, 1 - core)
    state = attend(state, x, 1 - core)
    kv_pass(3)
    state = attend(state, (x + 3) % 4, core)
    kv_pass(2)
    for which in range(2):
        dispatch_wait(cot_in, set_recv.at[0], which)
        xc[z, pl.ds(which * HALF, HALF), :] = packed(cot_in, which)
    cot_ring = ring_gather(xc, ring_send.at[0], ring_recv.at[0], 0, HALF)
    next(cot_ring)
    kv_arrive((x + 3) % 4, 1 - core)
    state = attend(state, (x + 3) % 4, 1 - core)
    state = attend(state, (x + 1) % 4, core)
    kv_arrive((x + 1) % 4, 1 - core)
    state = attend(state, (x + 1) % 4, 1 - core)
    state = attend(state, (x + 2) % 4, core)
    kv_arrive((x + 2) % 4, 1 - core)
    _, total, acc = attend(state, (x + 2) % 4, 1 - core)
    pick = (iota((HD, KVR), 1) == iota((HD, KVR), 0) + HD).astype(BF16)
    attn = mm_nt(pick, (acc / total).astype(BF16))

    def over_i(row):
        row = row + pltpu.roll(row, 32, 1)
        return row + pltpu.roll(row, 64, 1)

    local_mean = over_i(jnp.broadcast_to(jnp.sum(attn, axis=0, keepdims=True), (8, TOK)))[0:1, :] * (1.0 / (4 * HD))
    centred = attn - local_mean
    squares = over_i(jnp.broadcast_to(jnp.sum(centred * centred, axis=0, keepdims=True), (8, TOK)))
    st_all[e] = jnp.where(iota((8, TOK), 0) == 0, local_mean, squares)
    to_experts(lambda to: st_all.at[e], st_all, e_send.at[1], e_recv.at[1])
    scaled = centred * gain
    left = jnp.concatenate([jnp.where(group == i, scaled, 0.0) for i in range(4)], axis=0).astype(BF16)

    unit128 = (pi == pj).astype(BF16)
    left = mm_nt(unit128, left).astype(BF16)

    def merge_pair(j):
        cols = pl.ds(pl.multiple_of(j * (2 * COLS), 2 * COLS), 2 * COLS)
        v = mm(left, mw[:, cols])
        v = (v[0:32] + v[32:64] + v[64:96] + v[96:128]).astype(BF16)
        vp[2 * j] = v[:, 0:COLS]
        vp[2 * j + 1] = v[:, COLS : 2 * COLS]

    def merge_send(c, member):
        send(vp.at[c], vp_all.at[e], e_send.at[2], e_recv.at[2], b, member * NZ + c)

    def merge_others(i, carry):
        j = (z // 2 + 1 + i) % 4
        merge_pair(j)
        for c in (2 * j, 2 * j + 1):
            merge_send(c, 0)
            merge_send(c, 1)
        return carry

    lax.fori_loop(0, 3, merge_others, 0)
    merge_pair(z // 2)
    merge_send(z + 1 - 2 * (z % 2), 0)
    merge_send(z + 1 - 2 * (z % 2), 1)
    merge_send(z, 1 - y)
    vp_all[e] = vp[z]

    places = kvb[:, 144:160, :].astype(F32)
    places = jnp.sum(jnp.where(iota((NB, 16, TOK), 1) == 3, places, 0.0), axis=1)
    named = jnp.where(places == b.astype(F32), 1.0, 0.0)
    count = jnp.broadcast_to(jnp.sum(named, axis=1, keepdims=True), (NB, TOK))
    below = (iota((NB, NB), 1) < iota((NB, NB), 0)).astype(BF16)
    base = mm(below, count.astype(BF16))
    placed = jnp.sum(count, axis=0, keepdims=True)[:, 0:1]
    q3 = iota((NB, 8, TOK), 1).astype(F32)
    k3 = jnp.where(q3 < 4.0, q3, q3 - 4.0)
    lane3 = iota((NB, 8, TOK), 2).astype(F32)
    mine = jnp.where((lane3 == base[:, None, :] + k3) & (k3 < count[:, None, :]), 1.0, 0.0)
    ga[...] = jnp.where(q3 < 4.0, mine, 0.0).reshape(NB * 8, TOK).astype(BF16)
    gb[...] = jnp.where(q3 < 4.0, 0.0, mine).reshape(NB * 8, TOK).astype(BF16)
    to_shard = jnp.where(place_row == iota((NB, TOK), 0).astype(F32), 1.0, 0.0)
    order = mm(to_shard.astype(BF16), upper)
    order = jnp.where(to_shard > 0.0, order, -1.0)
    theirs = jnp.where(order[:, None, :] == k3, 1.0, 0.0)
    sa[...] = jnp.where(q3 < 4.0, theirs, 0.0).reshape(NB * 8, TOK).astype(BF16)
    sb[...] = jnp.where(q3 < 4.0, 0.0, theirs).reshape(NB * 8, TOK).astype(BF16)

    cv_out[...] = (mm(ga[...], cot[:, 0:TOK]) + mm(gb[...], cot[:, TOK:COLS])).reshape(NB, 8, TOK)
    a2a_start(cv_out, cv_in, row_send.at[0], row_recv.at[0])

    wait_bytes(gw_all.at[pl.ds(0, NE - 1)], e_recv.at[0])
    wait_bytes(st_all.at[pl.ds(0, NE - 1)], e_recv.at[1])
    row_stats = st_all[...]
    first = iota((NE, 8, TOK), 1) == 0
    means = jnp.sum(jnp.where(first, row_stats, 0.0), axis=1)
    mean = jnp.sum(means, axis=0, keepdims=True) * (1.0 / NE)
    spread = means - mean
    inner = jnp.sum(row_stats[:, 1:2, :], axis=0)
    variance = (inner + jnp.sum(spread * spread, axis=0, keepdims=True) * (4.0 * HD)) * (1.0 / MERGE)
    inv_std = lax.rsqrt(variance + EPS)
    normed = (attn - mean) * inv_std
    here_z = iota((NE, NZ, COLS), 1) == z
    gw_slice = jnp.sum(jnp.where(here_z, gw_all[...], 0.0), axis=1)
    shift = lax.dot_general(
        spread, gw_slice, (((0,), (0,)), ((), ())), preferred_element_type=F32, precision=lax.Precision.HIGHEST
    )[0:MR]
    inv_column = jnp.sum(jnp.where(pi == pj, inv_std, 0.0), axis=1, keepdims=True)[0:MR]
    wait_bytes(vp_all.at[pl.ds(0, NE - 1)], e_recv.at[2])
    next(cot_ring)
    vision = ((jnp.sum(vp_all[...].astype(F32), axis=0) + shift) * inv_column).astype(BF16)
    vis_all[z] = vision
    fill = jnp.zeros((TOK - MR, COLS), BF16)
    padded = jnp.concatenate([vision, fill], axis=0)
    vi_out[...] = (mm(sa[...], padded[:, 0:TOK]) + mm(sb[...], padded[:, TOK:COLS])).reshape(NB, 8, TOK)
    a2a_start(vi_out, vi_in, row_send.at[1], row_recv.at[1])
    to_z(vis_all.at[z], vis_all, z_send.at[0], z_recv.at[0])

    locals_[12].wait()
    locals_[13].wait()

    def gain_chunk(c, carry):
        cols = pl.ds(pl.multiple_of(c * COLS, COLS), COLS)
        g = ng_ref[:, cols]
        wgs[:, cols] = (wg[:, cols].astype(F32) * g).astype(BF16)
        wus[:, cols] = (wu[:, cols].astype(F32) * g).astype(BF16)
        return carry

    lax.fori_loop(0, NZ, gain_chunk, 0)
    next(cot_ring)
    a2a_wait(cv_in, row_recv.at[0])
    cv = cv_in[...].reshape(NB * 8, TOK).astype(BF16)
    cv_all[z, :, 0:TOK] = mm_tn(sa[...], cv)[0:MR].astype(BF16)
    cv_all[z, :, TOK:COLS] = mm_tn(sb[...], cv)[0:MR].astype(BF16)
    to_z(cv_all.at[z], cv_all, z_send.at[1], z_recv.at[1])

    locals_[11].wait()
    a2a_wait(vi_in, row_recv.at[1])
    arrived = vi_in[...].reshape(NB * 8, TOK).astype(BF16)
    taken = iota((TOK, TOK), 0).astype(F32) < placed
    llm_a = jnp.where(taken, mm_tn(ga[...], arrived), text[:, 0:TOK].astype(F32))
    llm_b = jnp.where(taken, mm_tn(gb[...], arrived), text[:, TOK:COLS].astype(F32))
    text[:, 0:TOK] = llm_a.astype(BF16)
    text[:, TOK:COLS] = llm_b.astype(BF16)
    h_out[...] = mm(dmat[...], text[...]).astype(BF16).reshape(NB, SLOT, COLS)
    dispatch(h_out, h_in, a2a_send.at[1], set_recv.at[1])

    for _ in cot_ring:
        pass
    locals_[14].wait()
    act_grad[...] = jnp.zeros_like(act_grad)
    gate_acc[...] = jnp.zeros_like(gate_acc)
    up_acc[...] = jnp.zeros_like(up_acc)
    ss_acc[...] = jnp.zeros_like(ss_acc)

    def act_chunk(c, carry):
        cols = pl.ds(pl.multiple_of(c * COLS, COLS), COLS)
        act_grad[...] += mm_nt(xc[c], wd[:, cols])
        return carry

    def project(c, which):
        cols = pl.ds(pl.multiple_of(c * COLS, COLS), COLS)
        part = pl.ds(which * HALF, HALF)
        rows = xh[c, part, :]
        gate_acc[part, :] += mm_nt(rows, wgs[:, cols])
        up_acc[part, :] += mm_nt(rows, wus[:, cols])
        wide = rows.astype(F32)
        ss_acc[part, :] += wide[:, 0:TOK] * wide[:, 0:TOK] + wide[:, TOK:COLS] * wide[:, TOK:COLS]

    h_rings = [
        ring_gather(xh, ring_send.at[1 + which], ring_recv.at[1 + which], which * HALF, QUARTER) for which in range(2)
    ]

    def h_round(k, which):
        if k == 0:
            dispatch_wait(h_in, set_recv.at[1], which)
            xh[z, pl.ds(which * HALF, HALF), :] = packed(h_in, which)
        next(h_rings[which])
        project((z + k) % NZ, which)
        if 0 < k < 4:
            project((z + 8 - k) % NZ, which)

    def hidden_units(which):
        part = pl.ds(which * HALF, HALF)
        inv = lax.rsqrt(jnp.sum(ss_acc[part, :], axis=1, keepdims=True) * (1.0 / WIDTH) + EPS)
        gate_pre = gate_acc[part, :] * inv
        up_proj = up_acc[part, :] * inv
        sig = 1.0 / (1.0 + jnp.exp(-gate_pre))
        grad = act_grad[part, :]
        hidden[0, part, :] = (grad * up_proj * sig * (1.0 + gate_pre * (1.0 - sig))).astype(BF16)
        hidden[1, part, :] = (grad * gate_pre * sig).astype(BF16)
        hidden[2, part, :] = (gate_pre * sig * up_proj).astype(BF16)

    def reducers(which):
        part = pl.ds(which * HALF, HALF)

        def grad_term(c):
            cols = pl.ds(pl.multiple_of(c * COLS, COLS), COLS)
            return mm(hidden[0, part, :], wg[:, cols]) + mm(hidden[1, part, :], wu[:, cols])

        def down_term(c):
            cols = pl.ds(pl.multiple_of(c * COLS, COLS), COLS)
            return mm(hidden[2, part, :], wd[:, cols])

        return [
            ring_reduce(term, rs_out.at[2 * which + j], rs_in.at[2 * which + j], rs_send.at[0], rs_recv.at[2 * which + j])
            for j, term in enumerate((grad_term, down_term))
        ]

    rings = [reducers(which) for which in range(2)]

    def reduce_round(which):
        for ring in rings[which]:
            next(ring)

    def give_back(which):
        for j, (out, inn) in enumerate(((rg_out, rg_in), (dn_out, dn_in))):
            rows = next(rings[which][j]).astype(BF16)
            out[pl.ds(which * SET, SET)] = mm_tn(cmat[...], rows).astype(BF16).reshape(SET, SLOT, COLS)
            if which == 1:
                inn[b] = out[SET]
            steps(which, -1, lambda i, to: send(out.at[i], inn.at[b], a2a_send.at[2 + j], a2a_recv.at[j], to, e))

    h_round(0, 0)
    h_round(0, 1)
    lax.fori_loop(0, NZ, act_chunk, 0)
    for k in range(1, 4):
        h_round(k, 0)
        h_round(k, 1)
    h_round(4, 0)
    hidden_units(0)
    reduce_round(0)
    h_round(4, 1)
    hidden_units(1)
    for which in (0, 1, 0, 1, 0, 1):
        reduce_round(which)
    give_back(0)
    reduce_round(1)
    give_back(1)

    a2a_wait(rg_in, a2a_recv.at[0])
    token_grad = mm_tn(dmat[...], rg_in[...].reshape(NB * SLOT, COLS)).astype(BF16)
    hg_out[...] = (mm(ga[...], token_grad[:, 0:TOK]) + mm(gb[...], token_grad[:, TOK:COLS])).reshape(NB, 8, TOK)
    a2a_start(hg_out, hg_in, row_send.at[2], row_recv.at[2])

    a2a_wait(dn_in, a2a_recv.at[1])
    dn = dn_in[...].reshape(NB * SLOT, COLS)
    mine_sum = mm_tn(dg_hi[...], dn) + mm_tn(dg_lo[...], dn)
    pair_out[...] = mine_sum.astype(BF16)
    own_half = pl.ds(pl.multiple_of(y * (TOK // 2), TOK // 2), TOK // 2)
    other_half = pl.ds(pl.multiple_of((1 - y) * (TOK // 2), TOK // 2), TOK // 2)
    other = (1 - y) * NZ + z
    send(pair_out.at[other_half], pair_in, pair_send.at[0], pair_recv.at[0], b, other)

    def llm_cross(src):
        send(llm_all.at[src, own_half], llm_all.at[src, own_half], llm_send.at[1], llm_recv.at[1, src], b, other)

    wait_bytes(pair_in, pair_recv.at[0])
    layer = pair_out[own_half, :].astype(F32) + pair_in[...].astype(F32)
    llm_all[z, own_half, :] = (text[own_half, :].astype(F32) + layer).astype(BF16)
    def llm_along(src, to):
        part = llm_all.at[src, own_half]
        send(part, part, llm_send.at[0], llm_recv.at[0, src], b, zdev(lax.rem(z + to, NZ)))

    def llm_arrive(distance):
        src = lax.rem(z + distance, NZ)
        wait_bytes(llm_all.at[src, own_half], llm_recv.at[0, src])
        return src

    for to in (2, 6, 1, 7):
        llm_along(z, to)
    llm_cross(z)
    a2a_wait(hg_in, row_recv.at[2])
    hg = hg_in[...].reshape(NB * 8, TOK).astype(BF16)
    hg_mine[:, 0:TOK] = mm_tn(sa[...], hg)[0:MR].astype(BF16)
    hg_mine[:, TOK:COLS] = mm_tn(sb[...], hg)[0:MR].astype(BF16)
    hg_all[e] = hg_mine[...]
    to_experts(lambda to: hg_mine, hg_all, e_send.at[3], e_recv.at[3])

    for distance, onward in ((6, (1, 2)), (2, (7,)), (7, ()), (1, ()), (5, ()), (3, ()), (4, ())):
        src = llm_arrive(distance)
        for to in onward:
            llm_along(src, to)
        llm_cross(src)

    wait_bytes(vis_all.at[pl.ds(0, NZ - 1)], z_recv.at[0])
    wait_bytes(cv_all.at[pl.ds(0, NZ - 1)], z_recv.at[1])
    wait_bytes(hg_all.at[pl.ds(0, NE - 1)], e_recv.at[3])

    gw_sum = jnp.sum(gw_all[...], axis=0)
    ssq = jnp.zeros((MR, COLS), F32)
    cross = jnp.zeros((MR, COLS), F32)
    for c in range(NZ):
        v = vis_all[c].astype(F32)
        ghg = (hg_all[c].astype(F32) + hg_all[NZ + c].astype(F32)) * ng_ref[:, c * COLS : (c + 1) * COLS]
        ssq = ssq + v * v
        cross = cross + ghg * v
    r = lax.rsqrt(jnp.sum(ssq, axis=1, keepdims=True) * (1.0 / WIDTH) + EPS)
    pull = jnp.sum(cross, axis=1, keepdims=True) * (1.0 / WIDTH) * r * r * r
    dot_g = jnp.zeros((MR, COLS), F32)
    dot_v = jnp.zeros((MR, COLS), F32)
    back_scaled = jnp.zeros((4 * HD, TOK), F32)
    for c in range(NZ):
        v = vis_all[c].astype(F32)
        ghg = (hg_all[c].astype(F32) + hg_all[NZ + c].astype(F32)) * ng_ref[:, c * COLS : (c + 1) * COLS]
        vg = (cv_all[c].astype(F32) + (r * ghg - v * pull)).astype(BF16)
        wide = vg.astype(F32)
        dot_g = dot_g + wide * gw_sum[c : c + 1, :]
        dot_v = dot_v + wide * v
        four = jnp.concatenate([vg, vg, vg, vg], axis=0)
        back_scaled = back_scaled + mm_nt(mw[:, c * COLS : (c + 1) * COLS], four)

    def to_lanes(columns):
        column = jnp.sum(columns, axis=1, keepdims=True)
        column = jnp.concatenate([column, column, column, column], axis=0)
        eye = iota((TOK, TOK), 0) == iota((TOK, TOK), 1)
        return jnp.sum(jnp.where(eye, column, 0.0), axis=0, keepdims=True)

    grad_mean = to_lanes(dot_g) * (1.0 / MERGE)
    cross_mean = to_lanes(dot_v) * (1.0 / MERGE)
    scaled_grad = jnp.zeros((HD, TOK), F32)
    for i in range(4):
        scaled_grad = jnp.where(group == i, back_scaled[i * HD : (i + 1) * HD, :], scaled_grad)
    merged_grad = inv_std * (scaled_grad * gain - grad_mean - normed * cross_mean)
    unfold = jnp.where(pj == 4 * (pi & 31) + (pi >> 5), 1.0, 0.0).astype(BF16)
    part1 = merged_grad.astype(BF16)
    rest = merged_grad - part1.astype(F32)
    part2 = rest.astype(BF16)
    part3 = (rest - part2.astype(F32)).astype(BF16)
    ag_ref[...] = mm(part1, unfold) + mm(part2, unfold) + mm(part3, unfold)
    for src in range(NZ):
        wait_bytes(llm_all.at[src, other_half], llm_recv.at[1, src])
    for c in range(NZ):
        llm_ref[:, c * COLS : (c + 1) * COLS] = llm_all[c]

    wait_bytes(kvb.at[pl.ds(0, NB - 1)], kv_send.at[0])
    for index, buf in enumerate((cot_out, h_out, rg_out, dn_out)):
        wait_bytes(buf.at[pl.ds(0, NB - 1)], a2a_send.at[index])
    for index, buf in enumerate((cv_out, vi_out, hg_out)):
        wait_bytes(buf.at[pl.ds(0, NB - 1)], row_send.at[index])
    for index, buf in enumerate((gw_all, st_all, vp_all, hg_all)):
        wait_bytes(buf.at[pl.ds(0, NE - 1)], e_send.at[index])
    for index, buf in enumerate((vis_all, cv_all)):
        wait_bytes(buf.at[pl.ds(0, NZ - 1)], z_send.at[index])
    wait_bytes(xc.at[pl.ds(0, NZ - 1)], ring_send.at[0])
    for index in range(2):
        wait_bytes(xh.at[pl.ds(0, NZ - 1), pl.ds(0, HALF)], ring_send.at[1 + index])
    wait_bytes(rs_out.at[:, pl.ds(0, 14)], rs_send.at[0])
    wait_bytes(pair_in, pair_send.at[0])
    wait_bytes(llm_all.at[pl.ds(0, NZ - 1), own_half], llm_send.at[0])
    wait_bytes(llm_all.at[:, own_half], llm_send.at[1])


def scratch_shapes():
    V = pltpu.VMEM
    D = pltpu.SemaphoreType.DMA
    routed = [V((NB, SLOT, COLS), BF16)] * 8
    rows = [V((NB, 8, TOK), F32)] * 6
    return (
        [V((HD, TOK), BF16)] * 3
        + [V((1, MR), jnp.int32), V((1, MR), jnp.int32), V((1, 4 * HD), F32), V((1, WIDTH), F32)]
        + [V((8, TOK), jnp.int32), V((8, TOK), F32)]
        + [V((4 * HD, WIDTH), BF16), V((TOK, COLS), BF16), V((TOK, COLS), BF16)]
        + [V((FG, WIDTH), BF16)] * 5
        + [D((15,))]
        + [V((NB, KVR, TOK), BF16), D((1,)), D((NB,))]
        + [V((NB * SLOT, TOK), BF16)] * 3
        + [V((HALF, SET * SLOT), BF16)]
        + [V((NB * 8, TOK), BF16)] * 4
        + routed + [D((4,)), D((2,)), D((2, 2))]
        + rows + [D((3,)), D((3,))]
        + [V((NE, NZ, COLS), F32), V((NE, 8, TOK), F32), V((NZ, MR, COLS), BF16), V((NE, MR, COLS), BF16)]
        + [V((NE, MR, COLS), BF16), V((MR, COLS), BF16), D((4,)), D((4,))]
        + [V((NZ, MR, COLS), BF16)] * 2 + [D((2,)), D((2,))]
        + [V((NZ, ROWS, COLS), BF16)] * 2 + [D((3,)), D((3, 16))]
        + [V((ROWS, FG), F32), V((ROWS, FG), F32), V((ROWS, TOK), F32), V((ROWS, FG), F32), V((3, ROWS, FG), BF16)]
        + [V((4, 20, QUARTER, COLS), BF16)] * 2 + [D((1,)), D((4, 20))]
        + [V((TOK, COLS), BF16), V((TOK // 2, COLS), BF16), D((1,)), D((1,))]
        + [V((NZ, TOK, COLS), BF16), D((2,)), D((2, NZ))]
    )


def body(
    queries, keys, values, image_ids, placement, merge_gain, merge_weight, text, norm_gain,
    w_gate, w_up, w_down, routes, route_gates, cotangent,
):
    vm = pl.BlockSpec(memory_space=pltpu.VMEM)
    anywhere = pl.BlockSpec(memory_space=pl.ANY)
    llm_out, attn_grad = pl.pallas_call(
        kernel,
        out_shape=(
            jax.ShapeDtypeStruct((TOK, WIDTH), BF16),
            jax.ShapeDtypeStruct((HD, TOK), F32),
        ),
        in_specs=[anywhere] * 15,
        out_specs=(vm, vm),
        scratch_shapes=scratch_shapes(),
        compiler_params=pltpu.CompilerParams(
            collective_id=0, has_side_effects=True, vmem_limit_bytes=VMEM_BYTES
        ),
    )(
        queries, keys, values, image_ids[None, :], placement.T, merge_gain, merge_weight, text, norm_gain[None, :],
        w_gate, w_up, w_down, routes.T, route_gates.T, cotangent,
    )
    return llm_out, attn_grad[None]


def solution(mesh):
    return jax.shard_map(
        body,
        mesh=mesh,
        in_specs=(
            P("expert", None, "blk"),
            P("expert", None, "blk"),
            P("expert", None, "blk"),
            P("blk"),
            P("blk", None),
            P("expert", None),
            P("expert", None, None),
            P("blk", None),
            P(),
            P("blk", "expert", None),
            P("blk", "expert", None),
            P("blk", "expert", None),
            P("blk", None),
            P("blk", None),
            P("blk", None),
        ),
        out_specs=(P("blk", None), P("expert", None, "blk")),
        check_vma=False,
    )
```

```python
import jax
import jax.numpy as jnp
from jax import lax
from jax.experimental import pallas as pl
from jax.experimental.pallas import tpu as pltpu
from jax.sharding import PartitionSpec as P

MESH = pl.DeviceIdType.MESH
F32 = jnp.float32
BF16 = jnp.bfloat16
EPS = 1e-06
NB = 32
NE = 16
NZ = 8
HD = 72
CAPX = 10
SLOT = 16
ROWS = NB * CAPX
HALF = ROWS // 2
QUARTER = HALF // 2
SET = NB // 2
COLS = 256
TOK = 128
MR = 32
WIDTH = 2048
FG = 192
MERGE = 4608
VMEM_BYTES = 63 * 1024 * 1024
KVR = 160
STREAMS = ((1, 0, 4), (1, 1, 3), (-1, 0, 3), (-1, 1, 4))


def mm(a, b):
    return lax.dot_general(a, b, (((1,), (0,)), ((), ())), preferred_element_type=F32)


def mm_nt(a, b):
    return lax.dot_general(a, b, (((1,), (1,)), ((), ())), preferred_element_type=F32)


def mm_tn(a, b):
    return lax.dot_general(a, b, (((0,), (0,)), ((), ())), preferred_element_type=F32)


def iota(shape, dim):
    return lax.broadcasted_iota(jnp.int32, shape, dim)


def wait_bytes(ref, sem):
    pltpu.make_async_copy(ref, ref, sem).wait()


def kernel(
    q_hbm, k_hbm, v_hbm, ids_hbm, place_hbm, gain_hbm, mw_hbm, text_hbm, ng_hbm,
    wg_hbm, wu_hbm, wd_hbm, routes_hbm, gates_hbm, cot_hbm,
    llm_ref, ag_ref,
    q_in, k_in, v_in, ids_in, place_in, gain_in, ng_ref, routes_in, gates_in,
    mw, text, cot, wg, wu, wd, wgs, wus, local_sem,
    kvb, kv_send, kv_recv,
    dmat, dg_hi, dg_lo, cmat, ga, gb, sa, sb,
    cot_out, cot_in, h_out, h_in, dn_out, dn_in, a2a_send, a2a_recv, set_recv,
    by_row, core_out, core_in, x_out, x_in, y_out, y_in, sum_send, core_recv, x_recv, y_recv,
    cv_out, cv_in, row_send, row_recv, vblk, vi_send, vi_recv, vt, pick_rows, info_out, info_in, info_send, place_all, place_recv,
    gw_all, st_all, vp, vp_all, hg_all, hg_mine, hg_other, e_send, e_recv,
    vis_all, cv_all, z_send, z_recv,
    xc, xh, ring_send, ring_recv,
    gate_acc, up_acc, ss_acc, act_grad, hidden,
    rs_out, rs_in, rs_send, rs_recv,
    pair_out, pair_in, pair_send, pair_recv,
    llm_all, llm_send, llm_recv,
):
    b = lax.axis_index("blk")
    e = lax.axis_index("expert")
    y = e // NZ
    z = e % NZ
    core = b % 2
    x = (b // 2) % 4
    yh = b // 8

    def blk_of(yy, xx, cc):
        return (yy * 4 + xx) * 2 + cc

    def zdev(zz):
        return y * NZ + zz

    zcols = pl.ds(pl.multiple_of(z * COLS, COLS), COLS)
    pairs = (
        (k_hbm.at[0], k_in), (v_hbm.at[0], v_in), (ids_hbm, ids_in), (place_hbm, place_in), (q_hbm.at[0], q_in),
        (routes_hbm, routes_in), (gates_hbm, gates_in), (gain_hbm, gain_in), (ng_hbm, ng_ref),
        (cot_hbm.at[:, zcols], cot), (mw_hbm.at[0], mw), (text_hbm.at[:, zcols], text),
        (wg_hbm.at[0], wg), (wu_hbm.at[0], wu), (wd_hbm.at[0], wd),
    )
    locals_ = [pltpu.make_async_copy(src, dst, local_sem.at[i]) for i, (src, dst) in enumerate(pairs)]
    for copy in locals_:
        copy.start()

    barrier = pltpu.get_barrier_semaphore()

    def greet_blk(i, carry):
        pl.semaphore_signal(barrier, inc=1, device_id=((b + i) % NB, e), device_id_type=MESH)
        return carry

    def greet_expert(i, carry):
        pl.semaphore_signal(barrier, inc=1, device_id=(b, (e + i) % NE), device_id_type=MESH)
        return carry

    lax.fori_loop(1, NB, greet_blk, 0)
    lax.fori_loop(1, NE, greet_expert, 0)

    for copy in locals_[:4]:
        copy.wait()
    ids16 = jnp.broadcast_to(ids_in[...], (16, MR)).astype(F32).astype(BF16)
    ri = iota((MR, TOK), 0)
    li = iota((MR, TOK), 1)
    row16 = iota((16, TOK), 0)
    patch_ids = mm(ids16, jnp.where(li >> 2 == ri, 1.0, 0.0).astype(BF16))
    place16 = jnp.broadcast_to(place_in[...], (16, MR)).astype(F32).astype(BF16)
    place_row = mm(place16, jnp.where(li == ri, 1.0, 0.0).astype(BF16))[0:1, :]
    place_row = jnp.where(iota((1, TOK), 1) < MR, place_row, -1.0)
    extra = jnp.where(row16 < 3, jnp.where(patch_ids == row16.astype(F32), 1.0, 0.0), 0.0)
    place_all[b] = place_row.astype(jnp.int32)
    kvb[b] = jnp.concatenate([k_in[...].astype(F32), v_in[...].astype(F32), extra], axis=0).astype(BF16)
    pl.semaphore_wait(barrier, NB - 1 + NE - 1)

    def send(src, dst, ssem, rsem, db, de):
        pltpu.make_async_remote_copy(
            src_ref=src, dst_ref=dst, send_sem=ssem, recv_sem=rsem, device_id=(db, de), device_id_type=MESH
        ).start()

    def a2a_start(src, dst, ssem, rsem):
        dst[b] = src[b]

        def one(i, carry):
            to = (b + i) % NB
            send(src.at[to], dst.at[b], ssem, rsem, to, e)
            return carry

        lax.fori_loop(1, NB, one, 0)

    def a2a_wait(dst, rsem):
        wait_bytes(dst.at[pl.ds(0, NB - 1)], rsem)

    within = lax.rem(b, 8)

    def steps(which, sign, go):
        for group in (0, 1):
            along = ((1, 3), (0, 2))[which][group]
            base = lax.rem(yh + 4 + sign * along, 4) * 8

            def one(j, carry):
                go(which * SET + group * 8 + j, base + lax.rem(within + 8 + sign * j, 8))
                return carry

            lax.fori_loop(0 if along > 0 else 1, 8, one, 0)

    def dispatch(src, dst, ssem, rsems):
        for which in (0, 1):
            steps(which, 1, lambda i, to: send(src.at[to], dst.at[i], ssem, rsems.at[which], to, e))
        dst[SET] = src[b]

    def dispatch_wait(dst, rsems, which):
        wait_bytes(dst.at[pl.ds(0, SET - which)], rsems.at[which])

    def packed(landed, which):
        rows = landed[pl.ds(which * SET, SET)].reshape(SET * SLOT, landed.shape[2])
        return mm(cmat[...], rows)

    def to_experts(src_of, dst, ssem, rsem):
        def one(i, carry):
            to = (e + i) % NE
            send(src_of(to), dst.at[e], ssem, rsem, b, to)
            return carry

        lax.fori_loop(1, NE, one, 0)

    def to_z(src, dst, ssem, rsem):
        def one(i, carry):
            to = (z + i) % NZ
            send(src, dst.at[z], ssem, rsem, b, zdev(to))
            return carry

        lax.fori_loop(1, NZ, one, 0)

    def ring_gather(buf, ssem, rsems, first, size):
        def piece(src, half):
            return buf.at[src, pl.ds(first + half * size, size)]

        for k in range(5):
            for way, half, far in STREAMS:
                if k > far:
                    continue
                src = (z + 8 - way * k) % NZ
                if k > 0:
                    wait_bytes(piece(src, half), rsems.at[src * 2 + half])
                if k < far:
                    send(piece(src, half), piece(src, half), ssem, rsems.at[src * 2 + half], b, zdev((z + 8 + way) % NZ))
            yield k

    def ring_reduce(term, out, inn, ssem, rsems):
        for d in range(4, 0, -1):
            right = term((z + d) % NZ)
            terms = {1: right, -1: right if d == 4 else term((z + 8 - d) % NZ)}
            for starts in (True, False):
                for index, (way, half, far) in enumerate(STREAMS):
                    if d > far or starts != (d == far):
                        continue
                    value = terms[way][half * QUARTER : (half + 1) * QUARTER]
                    here = index * 5 + d
                    if d < far:
                        wait_bytes(inn.at[here], rsems.at[here])
                        value = value + inn[here].astype(F32)
                    out[here] = value.astype(BF16)
                    send(out.at[here], inn.at[here - 1], ssem, rsems.at[here - 1], b, zdev((z + 8 + way) % NZ))
            yield None
        own = term(z)
        for index in range(4):
            wait_bytes(inn.at[index * 5], rsems.at[index * 5])
        arrived = [inn[half * 5].astype(F32) + inn[(2 + half) * 5].astype(F32) for half in range(2)]
        yield own + jnp.concatenate(arrived, axis=0)

    def kv_go(block, to):
        send(kvb.at[block], kvb.at[block], kv_send.at[0], kv_recv.at[block], to, e)

    def vi_go(block, to):
        send(vblk.at[block], vblk.at[block], vi_send.at[0], vi_recv.at[block], to, e)

    def along_x(go, block):
        for dx in (1, 3, 2):
            go(block, blk_of(yh, (x + dx) % 4, core))
        go(block, blk_of(yh, x, 1 - core))

    def along_y(go):
        for dy in (1, 3, 2):
            go(b, blk_of((yh + dy) % 4, x, core))
        along_x(go, b)

    def onward_x(go, buf, rsems):
        for dy in (1, 3, 2):
            block = blk_of((yh + 4 - dy) % 4, x, core)
            wait_bytes(buf.at[block], rsems.at[block])
            along_x(go, block)

    def onward_core(go, buf, rsems, dx):
        def one(i, carry):
            block = blk_of((yh + 4 - i) % 4, (x + 4 - dx) % 4, core)
            wait_bytes(buf.at[block], rsems.at[block])
            go(block, blk_of(yh, x, 1 - core))
            return carry

        lax.fori_loop(0, 4, one, 0)

    along_y(kv_go)

    def tell_place(i, carry):
        send(place_all.at[b], place_all.at[b], info_send.at[1], place_recv.at[0], lax.rem(b + i, NB), e)
        return carry

    lax.fori_loop(1, NB, tell_place, 0)

    for copy in locals_[4:9]:
        copy.wait()
    pi = iota((TOK, TOK), 0)
    pj = iota((TOK, TOK), 1)
    fold = jnp.where(pi == 4 * (pj & 31) + (pj >> 5), 1.0, 0.0).astype(BF16)
    row_ids = mm(ids16, jnp.where((li & 31) == ri, 1.0, 0.0).astype(BF16))
    shut = jnp.where((row16 < 3) & (row_ids != row16.astype(F32)), -1e30, 0.0)
    qp = jnp.concatenate([mm(q_in[...], fold), jnp.zeros((HD, TOK), F32), shut], axis=0).astype(BF16)
    unit = (iota((KVR, KVR), 0) == iota((KVR, KVR), 1)).astype(BF16)
    qt = mm_tn(qp, unit).astype(BF16)

    group = iota((HD, TOK), 1) >> 5
    fi = iota((HD, 4 * HD), 0)
    fj = iota((HD, 4 * HD), 1)
    gain = jnp.zeros((HD, TOK), F32)
    for i in range(4):
        column = jnp.sum(jnp.where(fj == fi + i * HD, gain_in[...], 0.0), axis=1, keepdims=True)
        gain = jnp.where(group == i, column, gain)
    gain_hi = gain_in[...].astype(BF16).astype(F32)
    gi = iota((16, 4 * HD), 0)
    gain_rows = jnp.where(gi == 0, gain_hi, jnp.where(gi == 1, gain_in[...] - gain_hi, 0.0)).astype(BF16)

    upper = (iota((TOK, TOK), 0) < iota((TOK, TOK), 1)).astype(BF16)
    ids = 2 * iota((NB, TOK), 0) + y
    hit = jnp.zeros((NB, TOK), F32)
    gate = jnp.zeros((NB, TOK), F32)
    for k in range(8):
        same = routes_in[k : k + 1, :] == ids
        hit = hit + jnp.where(same, 1.0, 0.0)
        gate = gate + jnp.where(same, gates_in[k : k + 1, :], 0.0)
    rank = mm(hit.astype(BF16), upper)
    place = jnp.where(hit > 0.0, rank, -1.0)
    slot3 = iota((NB, SLOT, TOK), 1).astype(F32)
    one_hot = jnp.where(place[:, None, :] == slot3, 1.0, 0.0)
    gated = (one_hot * gate[:, None, :]).reshape(NB * SLOT, TOK)
    dmat[...] = one_hot.reshape(NB * SLOT, TOK).astype(BF16)
    high = gated.astype(BF16)
    dg_hi[...] = high
    dg_lo[...] = (gated - high.astype(F32)).astype(BF16)
    slot_gate = jnp.sum(gated, axis=1, keepdims=True)
    locals_[9].wait()
    back = (mm(dmat[...], cot[...]) * slot_gate).astype(BF16)
    cot_out[...] = back.reshape(NB, SLOT, COLS)
    dispatch(cot_out, cot_in, a2a_send.at[0], set_recv.at[0])

    locals_[10].wait()
    gw = mm(gain_rows, mw[...])
    gw = gw[0:1, :] + gw[1:2, :]
    for c in range(NZ):
        gw_all[e, c : c + 1, :] = gw[:, c * COLS : (c + 1) * COLS]
    to_experts(lambda to: gw_all.at[e], gw_all, e_send.at[0], e_recv.at[0])

    onward_x(kv_go, kvb, kv_recv)

    wait_bytes(place_all.at[pl.ds(0, NB - 1)], place_recv.at[0])
    places = jnp.sum(place_all[...].astype(F32), axis=1)
    named = jnp.where(places == b.astype(F32), 1.0, 0.0)
    count = jnp.broadcast_to(jnp.sum(named, axis=1, keepdims=True), (NB, TOK))
    below = (iota((NB, NB), 1) < iota((NB, NB), 0)).astype(BF16)
    base = mm(below, count.astype(BF16))
    placed = jnp.sum(count, axis=0, keepdims=True)[:, 0:1]
    q3 = iota((NB, 8, TOK), 1).astype(F32)
    k3 = jnp.where(q3 < 4.0, q3, q3 - 4.0)
    lane3 = iota((NB, 8, TOK), 2).astype(F32)
    mine = jnp.where((lane3 == base[:, None, :] + k3) & (k3 < count[:, None, :]), 1.0, 0.0)
    ga[...] = jnp.where(q3 < 4.0, mine, 0.0).reshape(NB * 8, TOK).astype(BF16)
    gb[...] = jnp.where(q3 < 4.0, 0.0, mine).reshape(NB * 8, TOK).astype(BF16)
    to_shard = jnp.where(place_row == iota((NB, TOK), 0).astype(F32), 1.0, 0.0)
    order = mm(to_shard.astype(BF16), upper)
    order = jnp.where(to_shard > 0.0, order, -1.0)
    theirs = jnp.where(order[:, None, :] == k3, 1.0, 0.0)
    sa[...] = jnp.where(q3 < 4.0, theirs, 0.0).reshape(NB * 8, TOK).astype(BF16)
    sb[...] = jnp.where(q3 < 4.0, 0.0, theirs).reshape(NB * 8, TOK).astype(BF16)

    row_slot = jnp.where(named > 0.0, base + mm(named.astype(BF16), upper), -1.0)
    row3 = iota((NB, MR, TOK), 1)
    slot_lane3 = iota((NB, MR, TOK), 2)
    row_slot = jnp.sum(jnp.where(row3 == slot_lane3, row_slot[:, None, :], 0.0), axis=2, keepdims=True)
    vt[...] = jnp.where(row_slot == slot_lane3.astype(F32), 1.0, 0.0).reshape(NB * MR, TOK).astype(BF16)
    fact = iota((TOK, NB * MR), 0)
    row_id = iota((TOK, NB * MR), 1)
    fact = jnp.where(fact == 0, row_id >> 5, jnp.where(fact == 1, row_id & 31, jnp.where(fact == 2, 1, 0)))
    token_facts = mm(fact.astype(F32).astype(BF16), vt[...]).astype(BF16)

    locals_[11].wait()
    taken = iota((TOK, COLS), 0).astype(F32) < placed
    text_only = jnp.where(taken, 0.0, text[...].astype(F32)).astype(BF16)
    h_out[...] = mm(dmat[...], text_only).astype(BF16).reshape(NB, SLOT, COLS)
    dispatch(h_out, h_in, a2a_send.at[1], set_recv.at[1])
    info_out[...] = mm_nt(dmat[...], token_facts).astype(BF16).reshape(NB, SLOT, TOK)
    dispatch(info_out, info_in, info_send.at[0], set_recv.at[2])


    ci = iota((HALF, SET * SLOT), 0)
    cj = iota((HALF, SET * SLOT), 1)
    cmat[...] = jnp.where((ci == (cj >> 4) * CAPX + (cj & 15)) & ((cj & 15) < CAPX), 1.0, 0.0).astype(BF16)

    def kv_arrive(xx, cc):
        for yy in range(4):
            block = blk_of((yh + yy) % 4, xx, cc)
            wait_bytes(kvb.at[block], kv_recv.at[block])

    def attend(state, xx, cc):
        top, total, acc = state
        block = jnp.concatenate([kvb[blk_of(yy, xx, cc)] for yy in range(4)], axis=1)
        s = mm(qt, block)
        new_top = jnp.maximum(top, jnp.max(s, axis=1, keepdims=True))
        shrink = jnp.exp((top - new_top) * (HD ** -0.5))
        w = jnp.exp((s - new_top) * (HD ** -0.5))
        total = total * shrink + jnp.sum(w, axis=1, keepdims=True)
        return new_top, total, acc * shrink + mm_nt(w.astype(BF16), block)

    state = (jnp.full((TOK, 1), -1e30, F32), jnp.zeros((TOK, 1), F32), jnp.zeros((TOK, KVR), F32))
    state = attend(state, x, core)
    onward_core(kv_go, kvb, kv_recv, 1)
    kv_arrive(x, 1 - core)
    state = attend(state, x, 1 - core)
    onward_core(kv_go, kvb, kv_recv, 3)
    state = attend(state, (x + 3) % 4, core)
    onward_core(kv_go, kvb, kv_recv, 2)
    for which in range(2):
        dispatch_wait(cot_in, set_recv.at[0], which)
        xc[z, pl.ds(which * HALF, HALF), :] = packed(cot_in, which).astype(BF16)
    cot_ring = ring_gather(xc, ring_send.at[0], ring_recv.at[0], 0, HALF)
    next(cot_ring)
    kv_arrive((x + 3) % 4, 1 - core)
    state = attend(state, (x + 3) % 4, 1 - core)
    state = attend(state, (x + 1) % 4, core)
    kv_arrive((x + 1) % 4, 1 - core)
    state = attend(state, (x + 1) % 4, 1 - core)
    state = attend(state, (x + 2) % 4, core)
    kv_arrive((x + 2) % 4, 1 - core)
    _, total, acc = attend(state, (x + 2) % 4, 1 - core)
    pick = (iota((HD, KVR), 1) == iota((HD, KVR), 0) + HD).astype(BF16)
    attn = mm_nt(pick, (acc / total).astype(BF16))

    def over_i(row):
        row = row + pltpu.roll(row, 32, 1)
        return row + pltpu.roll(row, 64, 1)

    local_mean = over_i(jnp.broadcast_to(jnp.sum(attn, axis=0, keepdims=True), (8, TOK)))[0:1, :] * (1.0 / (4 * HD))
    centred = attn - local_mean
    squares = over_i(jnp.broadcast_to(jnp.sum(centred * centred, axis=0, keepdims=True), (8, TOK)))
    st_all[e] = jnp.where(iota((8, TOK), 0) == 0, local_mean, squares)
    to_experts(lambda to: st_all.at[e], st_all, e_send.at[1], e_recv.at[1])
    scaled = centred * gain
    left = jnp.concatenate([jnp.where(group == i, scaled, 0.0) for i in range(4)], axis=0).astype(BF16)

    unit128 = (pi == pj).astype(BF16)
    left = mm_nt(unit128, left).astype(BF16)

    def merge_pair(j):
        cols = pl.ds(pl.multiple_of(j * (2 * COLS), 2 * COLS), 2 * COLS)
        v = mm(left, mw[:, cols])
        v = (v[0:32] + v[32:64] + v[64:96] + v[96:128]).astype(BF16)
        vp[2 * j] = v[:, 0:COLS]
        vp[2 * j + 1] = v[:, COLS : 2 * COLS]

    def merge_send(c, member):
        send(vp.at[c], vp_all.at[e], e_send.at[2], e_recv.at[2], b, member * NZ + c)

    def merge_others(i, carry):
        j = (z // 2 + 1 + i) % 4
        merge_pair(j)
        for c in (2 * j, 2 * j + 1):
            merge_send(c, 0)
            merge_send(c, 1)
        return carry

    lax.fori_loop(0, 3, merge_others, 0)
    merge_pair(z // 2)
    merge_send(z + 1 - 2 * (z % 2), 0)
    merge_send(z + 1 - 2 * (z % 2), 1)
    merge_send(z, 1 - y)
    vp_all[e] = vp[z]

    next(cot_ring)

    cv_out[...] = (mm(ga[...], cot[:, 0:TOK]) + mm(gb[...], cot[:, TOK:COLS])).reshape(NB, 8, TOK)
    a2a_start(cv_out, cv_in, row_send.at[0], row_recv.at[0])

    locals_[12].wait()
    locals_[13].wait()

    def gain_chunk(c, carry):
        cols = pl.ds(pl.multiple_of(c * COLS, COLS), COLS)
        g = ng_ref[:, cols]
        wgs[:, cols] = (wg[:, cols].astype(F32) * g).astype(BF16)
        wus[:, cols] = (wu[:, cols].astype(F32) * g).astype(BF16)
        return carry

    lax.fori_loop(0, NZ, gain_chunk, 0)

    for which in range(2):
        dispatch_wait(info_in, set_recv.at[2], which)
        facts = packed(info_in, which)
        row_of = facts[:, 0:1] * 32.0 + facts[:, 1:2] + (facts[:, 2:3] - 1.0)
        hits = jnp.where(row_of == iota((HALF, NB * MR), 1).astype(F32), 1.0, 0.0)
        pick_rows[which] = hits.astype(BF16)

    wait_bytes(gw_all.at[pl.ds(0, NE - 1)], e_recv.at[0])
    wait_bytes(st_all.at[pl.ds(0, NE - 1)], e_recv.at[1])
    row_stats = st_all[...]
    first = iota((NE, 8, TOK), 1) == 0
    means = jnp.sum(jnp.where(first, row_stats, 0.0), axis=1)
    mean = jnp.sum(means, axis=0, keepdims=True) * (1.0 / NE)
    spread = means - mean
    inner = jnp.sum(row_stats[:, 1:2, :], axis=0)
    variance = (inner + jnp.sum(spread * spread, axis=0, keepdims=True) * (4.0 * HD)) * (1.0 / MERGE)
    inv_std = lax.rsqrt(variance + EPS)
    normed = (attn - mean) * inv_std
    here_z = iota((NE, NZ, COLS), 1) == z
    gw_slice = jnp.sum(jnp.where(here_z, gw_all[...], 0.0), axis=1)
    shift = lax.dot_general(
        spread, gw_slice, (((0,), (0,)), ((), ())), preferred_element_type=F32, precision=lax.Precision.HIGHEST
    )[0:MR]
    inv_column = jnp.sum(jnp.where(pi == pj, inv_std, 0.0), axis=1, keepdims=True)[0:MR]
    wait_bytes(vp_all.at[pl.ds(0, NE - 1)], e_recv.at[2])
    vision = ((jnp.sum(vp_all[...].astype(F32), axis=0) + shift) * inv_column).astype(BF16)
    vis_all[z] = vision
    vblk[b] = vision
    along_y(vi_go)

    onward_x(vi_go, vblk, vi_recv)
    for dx in (1, 3, 2):
        onward_core(vi_go, vblk, vi_recv, dx)
    next(cot_ring)
    a2a_wait(cv_in, row_recv.at[0])
    cv = cv_in[...].reshape(NB * 8, TOK).astype(BF16)
    cv_all[z, :, 0:TOK] = mm_tn(sa[...], cv)[0:MR].astype(BF16)
    cv_all[z, :, TOK:COLS] = mm_tn(sb[...], cv)[0:MR].astype(BF16)

    def vi_from_core(i, carry):
        block = 2 * i + (1 - core)
        wait_bytes(vblk.at[block], vi_recv.at[block])
        return carry

    lax.fori_loop(0, NB // 2, vi_from_core, 0)

    locals_[14].wait()
    act_grad[...] = jnp.zeros_like(act_grad)
    gate_acc[...] = jnp.zeros_like(gate_acc)
    up_acc[...] = jnp.zeros_like(up_acc)
    ss_acc[...] = jnp.zeros_like(ss_acc)

    def act_chunk(c, carry):
        cols = pl.ds(pl.multiple_of(c * COLS, COLS), COLS)
        act_grad[...] += mm_nt(xc[c], wd[:, cols])
        return carry

    def project(c, which):
        cols = pl.ds(pl.multiple_of(c * COLS, COLS), COLS)
        part = pl.ds(which * HALF, HALF)
        rows = xh[c, part, :]
        gate_acc[part, :] += mm_nt(rows, wgs[:, cols])
        up_acc[part, :] += mm_nt(rows, wus[:, cols])
        wide = rows.astype(F32)
        ss_acc[part, :] += wide[:, 0:TOK] * wide[:, 0:TOK] + wide[:, TOK:COLS] * wide[:, TOK:COLS]

    h_rings = [
        ring_gather(xh, ring_send.at[1 + which], ring_recv.at[1 + which], which * HALF, QUARTER) for which in range(2)
    ]

    def h_round(k, which):
        if k == 0:
            dispatch_wait(h_in, set_recv.at[1], which)
            placed_rows = mm(pick_rows[which], vblk[...].reshape(NB * MR, COLS))
            xh[z, pl.ds(which * HALF, HALF), :] = (packed(h_in, which) + placed_rows).astype(BF16)
        next(h_rings[which])
        project((z + k) % NZ, which)
        if 0 < k < 4:
            project((z + 8 - k) % NZ, which)

    def hidden_units(which):
        part = pl.ds(which * HALF, HALF)
        inv = lax.rsqrt(jnp.sum(ss_acc[part, :], axis=1, keepdims=True) * (1.0 / WIDTH) + EPS)
        gate_pre = gate_acc[part, :] * inv
        up_proj = up_acc[part, :] * inv
        sig = 1.0 / (1.0 + jnp.exp(-gate_pre))
        grad = act_grad[part, :]
        hidden[0, part, :] = (grad * up_proj * sig * (1.0 + gate_pre * (1.0 - sig))).astype(BF16)
        hidden[1, part, :] = (grad * gate_pre * sig).astype(BF16)
        hidden[2, part, :] = (gate_pre * sig * up_proj).astype(BF16)

    def reducers(which):
        part = pl.ds(which * HALF, HALF)

        def grad_term(c):
            cols = pl.ds(pl.multiple_of(c * COLS, COLS), COLS)
            return mm(hidden[0, part, :], wg[:, cols]) + mm(hidden[1, part, :], wu[:, cols])

        def down_term(c):
            cols = pl.ds(pl.multiple_of(c * COLS, COLS), COLS)
            return mm(hidden[2, part, :], wd[:, cols])

        return [
            ring_reduce(term, rs_out.at[2 * which + j], rs_in.at[2 * which + j], rs_send.at[0], rs_recv.at[2 * which + j])
            for j, term in enumerate((grad_term, down_term))
        ]

    rings = [reducers(which) for which in range(2)]

    def reduce_round(which):
        for ring in rings[which]:
            next(ring)

    def place_grad(which):
        rows = next(rings[which][0]).astype(BF16)
        placed_grad = mm_tn(pick_rows[which], rows).reshape(NB, MR, COLS)
        if which == 0:
            by_row[...] = placed_grad
        else:
            by_row[...] = by_row[...] + placed_grad

    def give_back(which):
        rows = next(rings[which][1]).astype(BF16)
        dn_out[pl.ds(which * SET, SET)] = mm_tn(cmat[...], rows).astype(BF16).reshape(SET, SLOT, COLS)
        if which == 1:
            dn_in[b] = dn_out[SET]
        steps(which, -1, lambda i, to: send(dn_out.at[i], dn_in.at[b], a2a_send.at[2], a2a_recv.at[0], to, e))

    def sum_over_cores():
        for dx in (1, 3, 2, 0):
            xx = lax.rem(x + dx, 4)
            for yy in range(4):
                core_out[xx, yy] = by_row[blk_of(yy, xx, 1 - core)].astype(BF16)
            send(core_out.at[xx], core_in.at[xx], sum_send.at[0], core_recv.at[xx], blk_of(yh, x, 1 - core), e)

    def sum_along_x():
        for dx in (1, 3, 2, 0):
            xx = lax.rem(x + dx, 4)
            wait_bytes(core_in.at[xx], core_recv.at[xx])
            for yy in range(4):
                block = blk_of(yy, xx, core)
                value = by_row[block] + core_in[xx, yy].astype(F32)
                if dx > 0:
                    x_out[dx - 1, yy] = value.astype(BF16)
                else:
                    by_row[block] = value
            if dx > 0:
                send(x_out.at[dx - 1], x_in.at[dx - 1], sum_send.at[1], x_recv.at[dx - 1], blk_of(yh, xx, core), e)

    def sum_along_y():
        for d in (0, 2, 1):
            wait_bytes(x_in.at[d], x_recv.at[d])
        for dy in (2, 1, 3, 0):
            yy = lax.rem(yh + dy, 4)
            block = blk_of(yy, x, core)
            value = by_row[block]
            for d in range(3):
                value = value + x_in[d, yy].astype(F32)
            if dy > 0:
                y_out[dy - 1] = value.astype(BF16)
                send(y_out.at[dy - 1], y_in.at[dy - 1], sum_send.at[2], y_recv.at[dy - 1], blk_of(yy, x, core), e)
            else:
                by_row[block] = value

    h_round(0, 0)
    h_round(0, 1)
    next(cot_ring)
    llm_in = jnp.where(taken, mm_tn(vt[...], vblk[...].reshape(NB * MR, COLS)), text[...].astype(F32))
    text[...] = llm_in.astype(BF16)
    h_round(1, 0)
    h_round(1, 1)
    next(cot_ring)
    lax.fori_loop(0, NZ, act_chunk, 0)
    for k in range(2, 4):
        h_round(k, 0)
        h_round(k, 1)
    h_round(4, 0)
    hidden_units(0)
    reduce_round(0)
    h_round(4, 1)
    hidden_units(1)
    for which in (0, 1, 0, 1, 0, 1):
        reduce_round(which)
    place_grad(0)
    give_back(0)
    reduce_round(1)
    place_grad(1)
    sum_over_cores()
    give_back(1)
    sum_along_x()
    to_z(vis_all.at[z], vis_all, z_send.at[0], z_recv.at[0])
    to_z(cv_all.at[z], cv_all, z_send.at[1], z_recv.at[1])

    sum_along_y()

    a2a_wait(dn_in, a2a_recv.at[0])
    dn = dn_in[...].reshape(NB * SLOT, COLS)
    mine_sum = mm_tn(dg_hi[...], dn) + mm_tn(dg_lo[...], dn)
    pair_out[...] = mine_sum.astype(BF16)
    own_half = pl.ds(pl.multiple_of(y * (TOK // 2), TOK // 2), TOK // 2)
    other_half = pl.ds(pl.multiple_of((1 - y) * (TOK // 2), TOK // 2), TOK // 2)
    other = (1 - y) * NZ + z
    send(pair_out.at[other_half], pair_in, pair_send.at[0], pair_recv.at[0], b, other)

    def llm_cross(src):
        send(llm_all.at[src, own_half], llm_all.at[src, own_half], llm_send.at[1], llm_recv.at[1, src], b, other)

    for d in range(3):
        wait_bytes(y_in.at[d], y_recv.at[d])
    row_grad = by_row[b] + (y_in[0].astype(F32) + y_in[1].astype(F32) + y_in[2].astype(F32))
    hg_mine[...] = row_grad.astype(BF16)
    send(hg_mine, hg_other, pair_send.at[1], pair_recv.at[1], b, other)

    wait_bytes(pair_in, pair_recv.at[0])
    layer = pair_out[own_half, :].astype(F32) + pair_in[...].astype(F32)
    llm_all[z, own_half, :] = (text[own_half, :].astype(F32) + layer).astype(BF16)
    def llm_along(src, to):
        part = llm_all.at[src, own_half]
        send(part, part, llm_send.at[0], llm_recv.at[0, src], b, zdev(lax.rem(z + to, NZ)))

    def llm_arrive(distance):
        src = lax.rem(z + distance, NZ)
        wait_bytes(llm_all.at[src, own_half], llm_recv.at[0, src])
        return src

    for to in (2, 6, 1, 7):
        llm_along(z, to)
    llm_cross(z)

    wait_bytes(hg_other, pair_recv.at[1])
    hg_all[z] = (hg_mine[...].astype(F32) + hg_other[...].astype(F32)).astype(BF16)
    to_z(hg_all.at[z], hg_all, z_send.at[2], z_recv.at[2])

    for distance, onward in ((6, (1, 2)), (2, (7,)), (7, ()), (1, ()), (5, ()), (3, ()), (4, ())):
        src = llm_arrive(distance)
        for to in onward:
            llm_along(src, to)
        llm_cross(src)

    wait_bytes(vis_all.at[pl.ds(0, NZ - 1)], z_recv.at[0])
    wait_bytes(cv_all.at[pl.ds(0, NZ - 1)], z_recv.at[1])
    wait_bytes(hg_all.at[pl.ds(0, NZ - 1)], z_recv.at[2])

    gw_sum = jnp.sum(gw_all[...], axis=0)
    ssq = jnp.zeros((MR, COLS), F32)
    cross = jnp.zeros((MR, COLS), F32)
    for c in range(NZ):
        v = vis_all[c].astype(F32)
        ghg = hg_all[c].astype(F32) * ng_ref[:, c * COLS : (c + 1) * COLS]
        ssq = ssq + v * v
        cross = cross + ghg * v
    r = lax.rsqrt(jnp.sum(ssq, axis=1, keepdims=True) * (1.0 / WIDTH) + EPS)
    pull = jnp.sum(cross, axis=1, keepdims=True) * (1.0 / WIDTH) * r * r * r
    dot_g = jnp.zeros((MR, COLS), F32)
    dot_v = jnp.zeros((MR, COLS), F32)
    back_scaled = jnp.zeros((4 * HD, TOK), F32)
    for c in range(NZ):
        v = vis_all[c].astype(F32)
        ghg = hg_all[c].astype(F32) * ng_ref[:, c * COLS : (c + 1) * COLS]
        vg = (cv_all[c].astype(F32) + (r * ghg - v * pull)).astype(BF16)
        wide = vg.astype(F32)
        dot_g = dot_g + wide * gw_sum[c : c + 1, :]
        dot_v = dot_v + wide * v
        four = jnp.concatenate([vg, vg, vg, vg], axis=0)
        back_scaled = back_scaled + mm_nt(mw[:, c * COLS : (c + 1) * COLS], four)

    def to_lanes(columns):
        column = jnp.sum(columns, axis=1, keepdims=True)
        column = jnp.concatenate([column, column, column, column], axis=0)
        eye = iota((TOK, TOK), 0) == iota((TOK, TOK), 1)
        return jnp.sum(jnp.where(eye, column, 0.0), axis=0, keepdims=True)

    grad_mean = to_lanes(dot_g) * (1.0 / MERGE)
    cross_mean = to_lanes(dot_v) * (1.0 / MERGE)
    scaled_grad = jnp.zeros((HD, TOK), F32)
    for i in range(4):
        scaled_grad = jnp.where(group == i, back_scaled[i * HD : (i + 1) * HD, :], scaled_grad)
    merged_grad = inv_std * (scaled_grad * gain - grad_mean - normed * cross_mean)
    unfold = jnp.where(pj == 4 * (pi & 31) + (pi >> 5), 1.0, 0.0).astype(BF16)
    part1 = merged_grad.astype(BF16)
    rest = merged_grad - part1.astype(F32)
    part2 = rest.astype(BF16)
    part3 = (rest - part2.astype(F32)).astype(BF16)
    ag_ref[...] = mm(part1, unfold) + mm(part2, unfold) + mm(part3, unfold)
    for src in range(NZ):
        wait_bytes(llm_all.at[src, other_half], llm_recv.at[1, src])
    for c in range(NZ):
        llm_ref[:, c * COLS : (c + 1) * COLS] = llm_all[c]

    wait_bytes(kvb.at[pl.ds(0, NB - 1)], kv_send.at[0])
    for index, buf in enumerate((cot_out, h_out, dn_out)):
        wait_bytes(buf.at[pl.ds(0, NB - 1)], a2a_send.at[index])
    wait_bytes(vblk.at[pl.ds(0, NB - 1)], vi_send.at[0])
    wait_bytes(info_out.at[pl.ds(0, NB - 1)], info_send.at[0])
    wait_bytes(place_all.at[pl.ds(0, NB - 1)], info_send.at[1])
    wait_bytes(cv_out.at[pl.ds(0, NB - 1)], row_send.at[0])
    for index, buf in enumerate((core_out, x_out, y_out)):
        wait_bytes(buf, sum_send.at[index])
    for index, buf in enumerate((gw_all, st_all, vp_all)):
        wait_bytes(buf.at[pl.ds(0, NE - 1)], e_send.at[index])
    for index, buf in enumerate((vis_all, cv_all, hg_all)):
        wait_bytes(buf.at[pl.ds(0, NZ - 1)], z_send.at[index])
    wait_bytes(xc.at[pl.ds(0, NZ - 1)], ring_send.at[0])
    for index in range(2):
        wait_bytes(xh.at[pl.ds(0, NZ - 1), pl.ds(0, HALF)], ring_send.at[1 + index])
    wait_bytes(rs_out.at[:, pl.ds(0, 14)], rs_send.at[0])
    wait_bytes(pair_in, pair_send.at[0])
    wait_bytes(hg_other, pair_send.at[1])
    wait_bytes(llm_all.at[pl.ds(0, NZ - 1), own_half], llm_send.at[0])
    wait_bytes(llm_all.at[:, own_half], llm_send.at[1])


def scratch_shapes():
    V = pltpu.VMEM
    D = pltpu.SemaphoreType.DMA
    routed = [V((NB, SLOT, COLS), BF16)] * 6
    rows = [V((NB, 8, TOK), F32)] * 2
    return (
        [V((HD, TOK), BF16)] * 3
        + [V((1, MR), jnp.int32), V((1, MR), jnp.int32), V((1, 4 * HD), F32), V((1, WIDTH), F32)]
        + [V((8, TOK), jnp.int32), V((8, TOK), F32)]
        + [V((4 * HD, WIDTH), BF16), V((TOK, COLS), BF16), V((TOK, COLS), BF16)]
        + [V((FG, WIDTH), BF16)] * 5
        + [D((15,))]
        + [V((NB, KVR, TOK), BF16), D((1,)), D((NB,))]
        + [V((NB * SLOT, TOK), BF16)] * 3
        + [V((HALF, SET * SLOT), BF16)]
        + [V((NB * 8, TOK), BF16)] * 4
        + routed + [D((3,)), D((1,)), D((3, 2))]
        + [V((NB, MR, COLS), F32)] + [V((4, 4, MR, COLS), BF16)] * 2 + [V((3, 4, MR, COLS), BF16)] * 2
        + [V((3, MR, COLS), BF16)] * 2 + [D((3,)), D((4,)), D((3,)), D((3,))]
        + rows + [D((1,)), D((1,))]
        + [V((NB, MR, COLS), BF16), D((1,)), D((NB,)), V((NB * MR, TOK), BF16), V((2, HALF, NB * MR), BF16)]
        + [V((NB, SLOT, TOK), BF16)] * 2 + [D((2,)), V((NB, 1, TOK), jnp.int32), D((1,))]
        + [V((NE, NZ, COLS), F32), V((NE, 8, TOK), F32), V((NZ, MR, COLS), BF16), V((NE, MR, COLS), BF16)]
        + [V((NZ, MR, COLS), BF16), V((MR, COLS), BF16), V((MR, COLS), BF16), D((3,)), D((3,))]
        + [V((NZ, MR, COLS), BF16)] * 2 + [D((3,)), D((3,))]
        + [V((NZ, ROWS, COLS), BF16)] * 2 + [D((3,)), D((3, 16))]
        + [V((ROWS, FG), F32), V((ROWS, FG), F32), V((ROWS, TOK), F32), V((ROWS, FG), F32), V((3, ROWS, FG), BF16)]
        + [V((4, 20, QUARTER, COLS), BF16)] * 2 + [D((1,)), D((4, 20))]
        + [V((TOK, COLS), BF16), V((TOK // 2, COLS), BF16), D((2,)), D((2,))]
        + [V((NZ, TOK, COLS), BF16), D((2,)), D((2, NZ))]
    )


def body(
    queries, keys, values, image_ids, placement, merge_gain, merge_weight, text, norm_gain,
    w_gate, w_up, w_down, routes, route_gates, cotangent,
):
    vm = pl.BlockSpec(memory_space=pltpu.VMEM)
    anywhere = pl.BlockSpec(memory_space=pl.ANY)
    llm_out, attn_grad = pl.pallas_call(
        kernel,
        out_shape=(
            jax.ShapeDtypeStruct((TOK, WIDTH), BF16),
            jax.ShapeDtypeStruct((HD, TOK), F32),
        ),
        in_specs=[anywhere] * 15,
        out_specs=(vm, vm),
        scratch_shapes=scratch_shapes(),
        compiler_params=pltpu.CompilerParams(
            collective_id=0, has_side_effects=True, vmem_limit_bytes=VMEM_BYTES
        ),
    )(
        queries, keys, values, image_ids[None, :], placement.T, merge_gain, merge_weight, text, norm_gain[None, :],
        w_gate, w_up, w_down, routes.T, route_gates.T, cotangent,
    )
    return llm_out, attn_grad[None]


def solution(mesh):
    return jax.shard_map(
        body,
        mesh=mesh,
        in_specs=(
            P("expert", None, "blk"),
            P("expert", None, "blk"),
            P("expert", None, "blk"),
            P("blk"),
            P("blk", None),
            P("expert", None),
            P("expert", None, None),
            P("blk", None),
            P(),
            P("blk", "expert", None),
            P("blk", "expert", None),
            P("blk", "expert", None),
            P("blk", None),
            P("blk", None),
            P("blk", None),
        ),
        out_specs=(P("blk", None), P("expert", None, "blk")),
        check_vma=False,
    )
```

```python
import jax
import jax.numpy as jnp
from jax import lax
from jax.experimental import pallas as pl
from jax.experimental.pallas import tpu as pltpu
from jax.sharding import PartitionSpec as P

MESH = pl.DeviceIdType.MESH
F32 = jnp.float32
BF16 = jnp.bfloat16
EPS = 1e-06
NB = 32
NE = 16
NZ = 8
HD = 72
CAPX = 10
SLOT = 16
ROWS = NB * CAPX
HALF = ROWS // 2
QUARTER = HALF // 2
SET = NB // 2
COLS = 256
TOK = 128
MR = 32
WIDTH = 2048
FG = 192
MERGE = 4608
VMEM_BYTES = 63 * 1024 * 1024
KVR = 160
STREAMS = ((1, 0, 4), (1, 1, 3), (-1, 0, 3), (-1, 1, 4))


def mm(a, b):
    return lax.dot_general(a, b, (((1,), (0,)), ((), ())), preferred_element_type=F32)


def mm_nt(a, b):
    return lax.dot_general(a, b, (((1,), (1,)), ((), ())), preferred_element_type=F32)


def mm_tn(a, b):
    return lax.dot_general(a, b, (((0,), (0,)), ((), ())), preferred_element_type=F32)


def iota(shape, dim):
    return lax.broadcasted_iota(jnp.int32, shape, dim)


def wait_bytes(ref, sem):
    pltpu.make_async_copy(ref, ref, sem).wait()


def kernel(
    q_hbm, k_hbm, v_hbm, ids_hbm, place_hbm, gain_hbm, mw_hbm, text_hbm, ng_hbm,
    wg_hbm, wu_hbm, wd_hbm, routes_hbm, gates_hbm, cot_hbm,
    llm_ref, ag_ref,
    q_in, k_in, v_in, ids_in, place_in, gain_in, ng_ref, routes_in, gates_in,
    mw, text, cot, wg, wu, wd, wgs, wus, local_sem,
    kvb, kv_send, kv_recv,
    dmat, dg_hi, dg_lo, cmat, ga, gb, sa, sb,
    cot_out, cot_in, h_out, h_in, dn_out, dn_in, a2a_send, a2a_recv, set_recv,
    by_row, core_out, core_in, x_out, x_in, y_out, y_in, sum_send, core_recv, x_recv, y_recv,
    cv_out, cv_in, row_send, row_recv, vblk, vi_send, vi_recv, vt, pick_rows, pick_slots, info_out, info_in, info_send, place_all, place_recv,
    gw_all, st_all, vp, vp_all, hg_all, hg_mine, hg_other, e_send, e_recv,
    vis_all, cv_all, z_send, z_recv,
    xc, xh, ring_send, ring_recv,
    gate_acc, up_acc, ss_acc, act_grad, hidden,
    rs_out, rs_in, rs_send, rs_recv,
    pair_out, pair_in, pair_send, pair_recv,
    llm_all, llm_send, llm_recv,
):
    b = lax.axis_index("blk")
    e = lax.axis_index("expert")
    y = e // NZ
    z = e % NZ
    core = b % 2
    x = (b // 2) % 4
    yh = b // 8

    def blk_of(yy, xx, cc):
        return (yy * 4 + xx) * 2 + cc

    def zdev(zz):
        return y * NZ + zz

    zcols = pl.ds(pl.multiple_of(z * COLS, COLS), COLS)
    pairs = (
        (k_hbm.at[0], k_in), (v_hbm.at[0], v_in), (ids_hbm, ids_in), (place_hbm, place_in), (q_hbm.at[0], q_in),
        (routes_hbm, routes_in), (gates_hbm, gates_in), (gain_hbm, gain_in), (ng_hbm, ng_ref),
        (cot_hbm.at[:, zcols], cot), (mw_hbm.at[0], mw), (text_hbm.at[:, zcols], text),
        (wg_hbm.at[0], wg), (wu_hbm.at[0], wu), (wd_hbm.at[0], wd),
    )
    locals_ = [pltpu.make_async_copy(src, dst, local_sem.at[i]) for i, (src, dst) in enumerate(pairs)]
    for copy in locals_:
        copy.start()

    barrier = pltpu.get_barrier_semaphore()

    def greet_blk(i, carry):
        pl.semaphore_signal(barrier, inc=1, device_id=((b + i) % NB, e), device_id_type=MESH)
        return carry

    def greet_expert(i, carry):
        pl.semaphore_signal(barrier, inc=1, device_id=(b, (e + i) % NE), device_id_type=MESH)
        return carry

    lax.fori_loop(1, NB, greet_blk, 0)
    lax.fori_loop(1, NE, greet_expert, 0)

    for copy in locals_[:4]:
        copy.wait()
    ids16 = jnp.broadcast_to(ids_in[...], (16, MR)).astype(F32).astype(BF16)
    ri = iota((MR, TOK), 0)
    li = iota((MR, TOK), 1)
    row16 = iota((16, TOK), 0)
    patch_ids = mm(ids16, jnp.where(li >> 2 == ri, 1.0, 0.0).astype(BF16))
    place16 = jnp.broadcast_to(place_in[...], (16, MR)).astype(F32).astype(BF16)
    place_row = mm(place16, jnp.where(li == ri, 1.0, 0.0).astype(BF16))[0:1, :]
    place_row = jnp.where(iota((1, TOK), 1) < MR, place_row, -1.0)
    extra = jnp.where(row16 < 3, jnp.where(patch_ids == row16.astype(F32), 1.0, 0.0), 0.0)
    place_all[b] = place_row.astype(jnp.int32)
    kvb[b] = jnp.concatenate([k_in[...].astype(F32), v_in[...].astype(F32), extra], axis=0).astype(BF16)
    pl.semaphore_wait(barrier, NB - 1 + NE - 1)

    def send(src, dst, ssem, rsem, db, de):
        pltpu.make_async_remote_copy(
            src_ref=src, dst_ref=dst, send_sem=ssem, recv_sem=rsem, device_id=(db, de), device_id_type=MESH
        ).start()

    def a2a_start(src, dst, ssem, rsem):
        dst[b] = src[b]

        def one(i, carry):
            to = (b + i) % NB
            send(src.at[to], dst.at[b], ssem, rsem, to, e)
            return carry

        lax.fori_loop(1, NB, one, 0)

    def a2a_wait(dst, rsem):
        wait_bytes(dst.at[pl.ds(0, NB - 1)], rsem)

    within = lax.rem(b, 8)

    def steps(which, sign, go):
        for group in (0, 1):
            along = ((1, 3), (0, 2))[which][group]
            base = lax.rem(yh + 4 + sign * along, 4) * 8

            def one(j, carry):
                go(which * SET + group * 8 + j, base + lax.rem(within + 8 + sign * j, 8))
                return carry

            lax.fori_loop(0 if along > 0 else 1, 8, one, 0)

    def dispatch(src, dst, ssem, rsems):
        for which in (0, 1):
            steps(which, 1, lambda i, to: send(src.at[to], dst.at[i], ssem, rsems.at[which], to, e))
        dst[SET] = src[b]

    def dispatch_wait(dst, rsems, which):
        wait_bytes(dst.at[pl.ds(0, SET - which)], rsems.at[which])

    def packed(landed, which):
        rows = landed[pl.ds(which * SET, SET)].reshape(SET * SLOT, landed.shape[2])
        return mm(cmat[...], rows)

    def to_experts(src_of, dst, ssem, rsem):
        def one(i, carry):
            to = (e + i) % NE
            send(src_of(to), dst.at[e], ssem, rsem, b, to)
            return carry

        lax.fori_loop(1, NE, one, 0)

    def to_z(src, dst, ssem, rsem):
        def one(i, carry):
            to = (z + i) % NZ
            send(src, dst.at[z], ssem, rsem, b, zdev(to))
            return carry

        lax.fori_loop(1, NZ, one, 0)

    def ring_gather(buf, ssem, rsems, first, size):
        def piece(src, half):
            return buf.at[src, pl.ds(first + half * size, size)]

        for k in range(5):
            for way, half, far in STREAMS:
                if k > far:
                    continue
                src = (z + 8 - way * k) % NZ
                if k > 0:
                    wait_bytes(piece(src, half), rsems.at[src * 2 + half])
                if k < far:
                    send(piece(src, half), piece(src, half), ssem, rsems.at[src * 2 + half], b, zdev((z + 8 + way) % NZ))
            yield k

    def ring_reduce(term, out, inn, ssem, rsems):
        for d in range(4, 0, -1):
            right = term((z + d) % NZ)
            terms = {1: right, -1: right if d == 4 else term((z + 8 - d) % NZ)}
            for starts in (True, False):
                for index, (way, half, far) in enumerate(STREAMS):
                    if d > far or starts != (d == far):
                        continue
                    value = terms[way][half * QUARTER : (half + 1) * QUARTER]
                    here = index * 5 + d
                    if d < far:
                        wait_bytes(inn.at[here], rsems.at[here])
                        value = value + inn[here].astype(F32)
                    out[here] = value.astype(BF16)
                    send(out.at[here], inn.at[here - 1], ssem, rsems.at[here - 1], b, zdev((z + 8 + way) % NZ))
            yield None
        own = term(z)
        for index in range(4):
            wait_bytes(inn.at[index * 5], rsems.at[index * 5])
        arrived = [inn[half * 5].astype(F32) + inn[(2 + half) * 5].astype(F32) for half in range(2)]
        yield own + jnp.concatenate(arrived, axis=0)

    def kv_go(block, to):
        send(kvb.at[block], kvb.at[block], kv_send.at[0], kv_recv.at[block], to, e)

    def vi_go(block, to):
        send(vblk.at[block], vblk.at[block], vi_send.at[0], vi_recv.at[block], to, e)

    def along_x(go, block):
        for dx in (1, 3, 2):
            go(block, blk_of(yh, (x + dx) % 4, core))
        go(block, blk_of(yh, x, 1 - core))

    def along_y(go):
        for dy in (1, 3, 2):
            go(b, blk_of((yh + dy) % 4, x, core))
        along_x(go, b)

    def onward_x(go, buf, rsems):
        for dy in (1, 3, 2):
            block = blk_of((yh + 4 - dy) % 4, x, core)
            wait_bytes(buf.at[block], rsems.at[block])
            along_x(go, block)

    def onward_core(go, buf, rsems, dx):
        def one(i, carry):
            block = blk_of((yh + 4 - i) % 4, (x + 4 - dx) % 4, core)
            wait_bytes(buf.at[block], rsems.at[block])
            go(block, blk_of(yh, x, 1 - core))
            return carry

        lax.fori_loop(0, 4, one, 0)

    along_y(kv_go)

    def tell_place(i, carry):
        send(place_all.at[b], place_all.at[b], info_send.at[1], place_recv.at[0], lax.rem(b + i, NB), e)
        return carry

    lax.fori_loop(1, NB, tell_place, 0)

    for copy in locals_[4:9]:
        copy.wait()
    pi = iota((TOK, TOK), 0)
    pj = iota((TOK, TOK), 1)
    fold = jnp.where(pi == 4 * (pj & 31) + (pj >> 5), 1.0, 0.0).astype(BF16)
    row_ids = mm(ids16, jnp.where((li & 31) == ri, 1.0, 0.0).astype(BF16))
    shut = jnp.where((row16 < 3) & (row_ids != row16.astype(F32)), -1e30, 0.0)
    qp = jnp.concatenate([mm(q_in[...], fold), jnp.zeros((HD, TOK), F32), shut], axis=0).astype(BF16)
    unit = (iota((KVR, KVR), 0) == iota((KVR, KVR), 1)).astype(BF16)
    qt = mm_tn(qp, unit).astype(BF16)

    group = iota((HD, TOK), 1) >> 5
    fi = iota((HD, 4 * HD), 0)
    fj = iota((HD, 4 * HD), 1)
    gain = jnp.zeros((HD, TOK), F32)
    for i in range(4):
        column = jnp.sum(jnp.where(fj == fi + i * HD, gain_in[...], 0.0), axis=1, keepdims=True)
        gain = jnp.where(group == i, column, gain)
    gain_hi = gain_in[...].astype(BF16).astype(F32)
    gi = iota((16, 4 * HD), 0)
    gain_rows = jnp.where(gi == 0, gain_hi, jnp.where(gi == 1, gain_in[...] - gain_hi, 0.0)).astype(BF16)

    upper = (iota((TOK, TOK), 0) < iota((TOK, TOK), 1)).astype(BF16)
    ids = 2 * iota((NB, TOK), 0) + y
    hit = jnp.zeros((NB, TOK), F32)
    gate = jnp.zeros((NB, TOK), F32)
    for k in range(8):
        same = routes_in[k : k + 1, :] == ids
        hit = hit + jnp.where(same, 1.0, 0.0)
        gate = gate + jnp.where(same, gates_in[k : k + 1, :], 0.0)
    rank = mm(hit.astype(BF16), upper)
    place = jnp.where(hit > 0.0, rank, -1.0)
    slot3 = iota((NB, SLOT, TOK), 1).astype(F32)
    one_hot = jnp.where(place[:, None, :] == slot3, 1.0, 0.0)
    gated = (one_hot * gate[:, None, :]).reshape(NB * SLOT, TOK)
    dmat[...] = one_hot.reshape(NB * SLOT, TOK).astype(BF16)
    high = gated.astype(BF16)
    dg_hi[...] = high
    dg_lo[...] = (gated - high.astype(F32)).astype(BF16)
    slot_gate = jnp.sum(gated, axis=1, keepdims=True)
    locals_[9].wait()
    back = (mm(dmat[...], cot[...]) * slot_gate).astype(BF16)
    cot_out[...] = back.reshape(NB, SLOT, COLS)
    dispatch(cot_out, cot_in, a2a_send.at[0], set_recv.at[0])

    locals_[10].wait()
    gw = mm(gain_rows, mw[...])
    gw = gw[0:1, :] + gw[1:2, :]
    for c in range(NZ):
        gw_all[e, c : c + 1, :] = gw[:, c * COLS : (c + 1) * COLS]
    to_experts(lambda to: gw_all.at[e], gw_all, e_send.at[0], e_recv.at[0])

    onward_x(kv_go, kvb, kv_recv)

    def kv_arrive(xx, cc):
        for yy in range(4):
            block = blk_of((yh + yy) % 4, xx, cc)
            wait_bytes(kvb.at[block], kv_recv.at[block])

    def attend(state, xx, cc):
        top, total, acc = state
        block = jnp.concatenate([kvb[blk_of(yy, xx, cc)] for yy in range(4)], axis=1)
        s = mm(qt, block)
        new_top = jnp.maximum(top, jnp.max(s, axis=1, keepdims=True))
        shrink = jnp.exp((top - new_top) * (HD ** -0.5))
        w = jnp.exp((s - new_top) * (HD ** -0.5))
        total = total * shrink + jnp.sum(w, axis=1, keepdims=True)
        return new_top, total, acc * shrink + mm_nt(w.astype(BF16), block)

    state = (jnp.full((TOK, 1), -1e30, F32), jnp.zeros((TOK, 1), F32), jnp.zeros((TOK, KVR), F32))
    state = attend(state, x, core)

    wait_bytes(place_all.at[pl.ds(0, NB - 1)], place_recv.at[0])
    places = jnp.sum(place_all[...].astype(F32), axis=1)
    named = jnp.where(places == b.astype(F32), 1.0, 0.0)
    count = jnp.broadcast_to(jnp.sum(named, axis=1, keepdims=True), (NB, TOK))
    below = (iota((NB, NB), 1) < iota((NB, NB), 0)).astype(BF16)
    base = mm(below, count.astype(BF16))
    placed = jnp.sum(count, axis=0, keepdims=True)[:, 0:1]
    q3 = iota((NB, 8, TOK), 1).astype(F32)
    k3 = jnp.where(q3 < 4.0, q3, q3 - 4.0)
    lane3 = iota((NB, 8, TOK), 2).astype(F32)
    mine = jnp.where((lane3 == base[:, None, :] + k3) & (k3 < count[:, None, :]), 1.0, 0.0)
    ga[...] = jnp.where(q3 < 4.0, mine, 0.0).reshape(NB * 8, TOK).astype(BF16)
    gb[...] = jnp.where(q3 < 4.0, 0.0, mine).reshape(NB * 8, TOK).astype(BF16)
    to_shard = jnp.where(place_row == iota((NB, TOK), 0).astype(F32), 1.0, 0.0)
    order = mm(to_shard.astype(BF16), upper)
    order = jnp.where(to_shard > 0.0, order, -1.0)
    theirs = jnp.where(order[:, None, :] == k3, 1.0, 0.0)
    sa[...] = jnp.where(q3 < 4.0, theirs, 0.0).reshape(NB * 8, TOK).astype(BF16)
    sb[...] = jnp.where(q3 < 4.0, 0.0, theirs).reshape(NB * 8, TOK).astype(BF16)

    row_slot = jnp.where(named > 0.0, base + mm(named.astype(BF16), upper), -1.0)
    row3 = iota((NB, MR, TOK), 1)
    slot_lane3 = iota((NB, MR, TOK), 2)
    row_slot = jnp.sum(jnp.where(row3 == slot_lane3, row_slot[:, None, :], 0.0), axis=2, keepdims=True)
    vt[...] = jnp.where(row_slot == slot_lane3.astype(F32), 1.0, 0.0).reshape(NB * MR, TOK).astype(BF16)
    fact = iota((TOK, NB * MR), 0)
    row_id = iota((TOK, NB * MR), 1)
    fact = jnp.where(fact == 0, row_id >> 5, jnp.where(fact == 1, row_id & 31, jnp.where(fact == 2, 1, 0)))
    token_facts = mm(fact.astype(F32).astype(BF16), vt[...]).astype(BF16)

    locals_[11].wait()
    taken = iota((TOK, COLS), 0).astype(F32) < placed
    text_only = jnp.where(taken, 0.0, text[...].astype(F32)).astype(BF16)
    h_out[...] = mm(dmat[...], text_only).astype(BF16).reshape(NB, SLOT, COLS)
    dispatch(h_out, h_in, a2a_send.at[1], set_recv.at[1])
    info_out[...] = mm_nt(dmat[...], token_facts).astype(BF16).reshape(NB, SLOT, TOK)
    dispatch(info_out, info_in, info_send.at[0], set_recv.at[2])


    ci = iota((HALF, SET * SLOT), 0)
    cj = iota((HALF, SET * SLOT), 1)
    cmat[...] = jnp.where((ci == (cj >> 4) * CAPX + (cj & 15)) & ((cj & 15) < CAPX), 1.0, 0.0).astype(BF16)

    onward_core(kv_go, kvb, kv_recv, 1)
    kv_arrive(x, 1 - core)
    state = attend(state, x, 1 - core)
    onward_core(kv_go, kvb, kv_recv, 3)
    state = attend(state, (x + 3) % 4, core)
    onward_core(kv_go, kvb, kv_recv, 2)
    for which in range(2):
        dispatch_wait(cot_in, set_recv.at[0], which)
        xc[z, pl.ds(which * HALF, HALF), :] = packed(cot_in, which).astype(BF16)
    cot_ring = ring_gather(xc, ring_send.at[0], ring_recv.at[0], 0, HALF)
    next(cot_ring)
    kv_arrive((x + 3) % 4, 1 - core)
    state = attend(state, (x + 3) % 4, 1 - core)
    state = attend(state, (x + 1) % 4, core)
    kv_arrive((x + 1) % 4, 1 - core)
    state = attend(state, (x + 1) % 4, 1 - core)
    state = attend(state, (x + 2) % 4, core)
    kv_arrive((x + 2) % 4, 1 - core)
    _, total, acc = attend(state, (x + 2) % 4, 1 - core)
    pick = (iota((HD, KVR), 1) == iota((HD, KVR), 0) + HD).astype(BF16)
    attn = mm_nt(pick, (acc / total).astype(BF16))

    def over_i(row):
        row = row + pltpu.roll(row, 32, 1)
        return row + pltpu.roll(row, 64, 1)

    local_mean = over_i(jnp.broadcast_to(jnp.sum(attn, axis=0, keepdims=True), (8, TOK)))[0:1, :] * (1.0 / (4 * HD))
    centred = attn - local_mean
    squares = over_i(jnp.broadcast_to(jnp.sum(centred * centred, axis=0, keepdims=True), (8, TOK)))
    st_all[e] = jnp.where(iota((8, TOK), 0) == 0, local_mean, squares)
    to_experts(lambda to: st_all.at[e], st_all, e_send.at[1], e_recv.at[1])
    scaled = centred * gain
    left = jnp.concatenate([jnp.where(group == i, scaled, 0.0) for i in range(4)], axis=0).astype(BF16)

    unit128 = (pi == pj).astype(BF16)
    left = mm_nt(unit128, left).astype(BF16)

    def merge_pair(j):
        cols = pl.ds(pl.multiple_of(j * (2 * COLS), 2 * COLS), 2 * COLS)
        v = mm(left, mw[:, cols])
        v = (v[0:32] + v[32:64] + v[64:96] + v[96:128]).astype(BF16)
        vp[2 * j] = v[:, 0:COLS]
        vp[2 * j + 1] = v[:, COLS : 2 * COLS]

    def merge_send(c, member):
        send(vp.at[c], vp_all.at[e], e_send.at[2], e_recv.at[2], b, member * NZ + c)

    def merge_others(i, carry):
        j = (z // 2 + 1 + i) % 4
        merge_pair(j)
        for c in (2 * j, 2 * j + 1):
            merge_send(c, 0)
            merge_send(c, 1)
        return carry

    lax.fori_loop(0, 3, merge_others, 0)
    merge_pair(z // 2)
    merge_send(z + 1 - 2 * (z % 2), 0)
    merge_send(z + 1 - 2 * (z % 2), 1)
    merge_send(z, 1 - y)
    vp_all[e] = vp[z]

    next(cot_ring)

    cv_out[...] = (mm(ga[...], cot[:, 0:TOK]) + mm(gb[...], cot[:, TOK:COLS])).reshape(NB, 8, TOK)
    a2a_start(cv_out, cv_in, row_send.at[0], row_recv.at[0])

    locals_[12].wait()
    locals_[13].wait()

    def gain_chunk(c, carry):
        cols = pl.ds(pl.multiple_of(c * COLS, COLS), COLS)
        g = ng_ref[:, cols]
        wgs[:, cols] = (wg[:, cols].astype(F32) * g).astype(BF16)
        wus[:, cols] = (wu[:, cols].astype(F32) * g).astype(BF16)
        return carry

    lax.fori_loop(0, NZ, gain_chunk, 0)

    for which in range(2):
        dispatch_wait(info_in, set_recv.at[2], which)
        facts = packed(info_in, which)
        row_of = facts[:, 0:1] * 32.0 + facts[:, 1:2] + (facts[:, 2:3] - 1.0)
        hits = jnp.where(row_of == iota((HALF, NB * MR), 1).astype(F32), 1.0, 0.0)
        pick_rows[which] = hits.astype(BF16)
        across = mm_nt(unit128, facts.astype(BF16))
        row_of = across[0:1, :] * 32.0 + across[1:2, :] + (across[2:3, :] - 1.0)
        hits = jnp.where(row_of == iota((NB * MR, HALF), 0).astype(F32), 1.0, 0.0)
        pick_slots[which] = hits.astype(BF16)

    wait_bytes(gw_all.at[pl.ds(0, NE - 1)], e_recv.at[0])
    wait_bytes(st_all.at[pl.ds(0, NE - 1)], e_recv.at[1])
    row_stats = st_all[...]
    first = iota((NE, 8, TOK), 1) == 0
    means = jnp.sum(jnp.where(first, row_stats, 0.0), axis=1)
    mean = jnp.sum(means, axis=0, keepdims=True) * (1.0 / NE)
    spread = means - mean
    inner = jnp.sum(row_stats[:, 1:2, :], axis=0)
    variance = (inner + jnp.sum(spread * spread, axis=0, keepdims=True) * (4.0 * HD)) * (1.0 / MERGE)
    inv_std = lax.rsqrt(variance + EPS)
    normed = (attn - mean) * inv_std
    here_z = iota((NE, NZ, COLS), 1) == z
    gw_slice = jnp.sum(jnp.where(here_z, gw_all[...], 0.0), axis=1)
    shift = lax.dot_general(
        spread, gw_slice, (((0,), (0,)), ((), ())), preferred_element_type=F32, precision=lax.Precision.HIGHEST
    )[0:MR]
    inv_column = jnp.sum(jnp.where(pi == pj, inv_std, 0.0), axis=1, keepdims=True)[0:MR]
    wait_bytes(vp_all.at[pl.ds(0, NE - 1)], e_recv.at[2])
    vision = ((jnp.sum(vp_all[...].astype(F32), axis=0) + shift) * inv_column).astype(BF16)
    vis_all[z] = vision
    vblk[b] = vision
    along_y(vi_go)

    onward_x(vi_go, vblk, vi_recv)
    onward_core(vi_go, vblk, vi_recv, 1)
    next(cot_ring)
    onward_core(vi_go, vblk, vi_recv, 3)
    onward_core(vi_go, vblk, vi_recv, 2)
    a2a_wait(cv_in, row_recv.at[0])
    cv = cv_in[...].reshape(NB * 8, TOK).astype(BF16)
    cv_all[z, :, 0:TOK] = mm_tn(sa[...], cv)[0:MR].astype(BF16)
    cv_all[z, :, TOK:COLS] = mm_tn(sb[...], cv)[0:MR].astype(BF16)

    def vi_from_core(i, carry):
        block = 2 * i + (1 - core)
        wait_bytes(vblk.at[block], vi_recv.at[block])
        return carry

    lax.fori_loop(0, NB // 2, vi_from_core, 0)

    locals_[14].wait()
    act_grad[...] = jnp.zeros_like(act_grad)
    gate_acc[...] = jnp.zeros_like(gate_acc)
    up_acc[...] = jnp.zeros_like(up_acc)
    ss_acc[...] = jnp.zeros_like(ss_acc)

    def act_chunk(c, carry):
        cols = pl.ds(pl.multiple_of(c * COLS, COLS), COLS)
        act_grad[...] += mm_nt(xc[c], wd[:, cols])
        return carry

    def project(c, which):
        cols = pl.ds(pl.multiple_of(c * COLS, COLS), COLS)
        part = pl.ds(which * HALF, HALF)
        rows = xh[c, part, :]
        gate_acc[part, :] += mm_nt(rows, wgs[:, cols])
        up_acc[part, :] += mm_nt(rows, wus[:, cols])
        wide = rows.astype(F32)
        ss_acc[part, :] += wide[:, 0:TOK] * wide[:, 0:TOK] + wide[:, TOK:COLS] * wide[:, TOK:COLS]

    h_rings = [
        ring_gather(xh, ring_send.at[1 + which], ring_recv.at[1 + which], which * HALF, QUARTER) for which in range(2)
    ]

    def h_round(k, which):
        if k == 0:
            dispatch_wait(h_in, set_recv.at[1], which)
            placed_rows = mm(pick_rows[which], vblk[...].reshape(NB * MR, COLS))
            xh[z, pl.ds(which * HALF, HALF), :] = (packed(h_in, which) + placed_rows).astype(BF16)
        next(h_rings[which])

    def h_project(k, which):
        project((z + k) % NZ, which)
        if 0 < k < 4:
            project((z + 8 - k) % NZ, which)

    def hidden_units(which):
        part = pl.ds(which * HALF, HALF)
        inv = lax.rsqrt(jnp.sum(ss_acc[part, :], axis=1, keepdims=True) * (1.0 / WIDTH) + EPS)
        gate_pre = gate_acc[part, :] * inv
        up_proj = up_acc[part, :] * inv
        sig = 1.0 / (1.0 + jnp.exp(-gate_pre))
        grad = act_grad[part, :]
        hidden[0, part, :] = (grad * up_proj * sig * (1.0 + gate_pre * (1.0 - sig))).astype(BF16)
        hidden[1, part, :] = (grad * gate_pre * sig).astype(BF16)
        hidden[2, part, :] = (gate_pre * sig * up_proj).astype(BF16)

    def reducers(which):
        part = pl.ds(which * HALF, HALF)

        def grad_term(c):
            cols = pl.ds(pl.multiple_of(c * COLS, COLS), COLS)
            return mm(hidden[0, part, :], wg[:, cols]) + mm(hidden[1, part, :], wu[:, cols])

        def down_term(c):
            cols = pl.ds(pl.multiple_of(c * COLS, COLS), COLS)
            return mm(hidden[2, part, :], wd[:, cols])

        return [
            ring_reduce(term, rs_out.at[2 * which + j], rs_in.at[2 * which + j], rs_send.at[0], rs_recv.at[2 * which + j])
            for j, term in enumerate((grad_term, down_term))
        ]

    rings = [reducers(which) for which in range(2)]

    def reduce_round(which):
        for ring in rings[which]:
            next(ring)

    def place_grad(which):
        rows = next(rings[which][0]).astype(BF16)
        placed_grad = mm(pick_slots[which], rows).reshape(NB, MR, COLS)
        if which == 0:
            by_row[...] = placed_grad
        else:
            by_row[...] = by_row[...] + placed_grad

    def give_back(which):
        rows = next(rings[which][1]).astype(BF16)
        dn_out[pl.ds(which * SET, SET)] = mm_tn(cmat[...], rows).astype(BF16).reshape(SET, SLOT, COLS)
        if which == 1:
            dn_in[b] = dn_out[SET]
        steps(which, -1, lambda i, to: send(dn_out.at[i], dn_in.at[b], a2a_send.at[2], a2a_recv.at[0], to, e))

    def sum_over_cores():
        for dx in (1, 3, 2, 0):
            xx = lax.rem(x + dx, 4)
            for yy in range(4):
                core_out[xx, yy] = by_row[blk_of(yy, xx, 1 - core)].astype(BF16)
            send(core_out.at[xx], core_in.at[xx], sum_send.at[0], core_recv.at[xx], blk_of(yh, x, 1 - core), e)

    def sum_along_x():
        for dx in (1, 3, 2, 0):
            xx = lax.rem(x + dx, 4)
            wait_bytes(core_in.at[xx], core_recv.at[xx])
            for yy in range(4):
                block = blk_of(yy, xx, core)
                value = by_row[block] + core_in[xx, yy].astype(F32)
                if dx > 0:
                    x_out[dx - 1, yy] = value.astype(BF16)
                else:
                    by_row[block] = value
            if dx > 0:
                send(x_out.at[dx - 1], x_in.at[dx - 1], sum_send.at[1], x_recv.at[dx - 1], blk_of(yh, xx, core), e)

    def sum_along_y():
        for d in (0, 2, 1):
            wait_bytes(x_in.at[d], x_recv.at[d])
        for dy in (2, 1, 3, 0):
            yy = lax.rem(yh + dy, 4)
            block = blk_of(yy, x, core)
            value = by_row[block]
            for d in range(3):
                value = value + x_in[d, yy].astype(F32)
            if dy > 0:
                y_out[dy - 1] = value.astype(BF16)
                send(y_out.at[dy - 1], y_in.at[dy - 1], sum_send.at[2], y_recv.at[dy - 1], blk_of(yy, x, core), e)
            else:
                by_row[block] = value

    for k in range(4):
        h_round(k, 0)
        h_round(k, 1)
        h_project(k, 0)
        h_project(k, 1)
        if k < 2:
            next(cot_ring)
        if k == 0:
            llm_in = jnp.where(taken, mm_tn(vt[...], vblk[...].reshape(NB * MR, COLS)), text[...].astype(F32))
            text[...] = llm_in.astype(BF16)
        if k > 1:
            lax.fori_loop((k - 2) * (NZ // 2), (k - 1) * (NZ // 2), act_chunk, 0)
    h_round(4, 0)
    h_project(4, 0)
    hidden_units(0)
    reduce_round(0)
    h_round(4, 1)
    h_project(4, 1)
    hidden_units(1)
    for which in (0, 1, 0, 1, 0, 1):
        reduce_round(which)
    place_grad(0)
    give_back(0)
    reduce_round(1)
    place_grad(1)
    sum_over_cores()
    give_back(1)
    sum_along_x()
    to_z(vis_all.at[z], vis_all, z_send.at[0], z_recv.at[0])
    to_z(cv_all.at[z], cv_all, z_send.at[1], z_recv.at[1])

    sum_along_y()
    a2a_wait(dn_in, a2a_recv.at[0])
    dn = dn_in[...].reshape(NB * SLOT, COLS)
    mine_sum = mm_tn(dg_hi[...], dn) + mm_tn(dg_lo[...], dn)
    pair_out[...] = mine_sum.astype(BF16)
    own_half = pl.ds(pl.multiple_of(y * (TOK // 2), TOK // 2), TOK // 2)
    other_half = pl.ds(pl.multiple_of((1 - y) * (TOK // 2), TOK // 2), TOK // 2)
    other = (1 - y) * NZ + z
    send(pair_out.at[other_half], pair_in, pair_send.at[0], pair_recv.at[0], b, other)

    def llm_cross(src):
        send(llm_all.at[src, own_half], llm_all.at[src, own_half], llm_send.at[1], llm_recv.at[1, src], b, other)

    wait_bytes(pair_in, pair_recv.at[0])
    layer = pair_out[own_half, :].astype(F32) + pair_in[...].astype(F32)
    llm_all[z, own_half, :] = (text[own_half, :].astype(F32) + layer).astype(BF16)
    def llm_along(src, to):
        part = llm_all.at[src, own_half]
        send(part, part, llm_send.at[0], llm_recv.at[0, src], b, zdev(lax.rem(z + to, NZ)))

    def llm_arrive(distance):
        src = lax.rem(z + distance, NZ)
        wait_bytes(llm_all.at[src, own_half], llm_recv.at[0, src])
        return src

    for to in (2, 6, 1, 7):
        llm_along(z, to)
    llm_cross(z)

    for d in range(3):
        wait_bytes(y_in.at[d], y_recv.at[d])
    row_grad = by_row[b] + (y_in[0].astype(F32) + y_in[1].astype(F32) + y_in[2].astype(F32))
    hg_mine[...] = row_grad.astype(BF16)
    send(hg_mine, hg_other, pair_send.at[1], pair_recv.at[1], b, other)

    def llm_onward(distance, onward):
        src = llm_arrive(distance)
        for to in onward:
            llm_along(src, to)
        llm_cross(src)

    llm_onward(6, (1, 2))
    llm_onward(2, (7,))
    wait_bytes(hg_other, pair_recv.at[1])
    hg_all[z] = (hg_mine[...].astype(F32) + hg_other[...].astype(F32)).astype(BF16)
    to_z(hg_all.at[z], hg_all, z_send.at[2], z_recv.at[2])
    for distance in (7, 1, 5, 3, 4):
        llm_onward(distance, ())

    wait_bytes(vis_all.at[pl.ds(0, NZ - 1)], z_recv.at[0])
    wait_bytes(cv_all.at[pl.ds(0, NZ - 1)], z_recv.at[1])
    wait_bytes(hg_all.at[pl.ds(0, NZ - 1)], z_recv.at[2])

    gw_sum = jnp.sum(gw_all[...], axis=0)
    ssq = jnp.zeros((MR, COLS), F32)
    cross = jnp.zeros((MR, COLS), F32)
    for c in range(NZ):
        v = vis_all[c].astype(F32)
        ghg = hg_all[c].astype(F32) * ng_ref[:, c * COLS : (c + 1) * COLS]
        ssq = ssq + v * v
        cross = cross + ghg * v
    r = lax.rsqrt(jnp.sum(ssq, axis=1, keepdims=True) * (1.0 / WIDTH) + EPS)
    pull = jnp.sum(cross, axis=1, keepdims=True) * (1.0 / WIDTH) * r * r * r
    dot_g = jnp.zeros((MR, COLS), F32)
    dot_v = jnp.zeros((MR, COLS), F32)
    back_scaled = jnp.zeros((4 * HD, TOK), F32)
    for c in range(NZ):
        v = vis_all[c].astype(F32)
        ghg = hg_all[c].astype(F32) * ng_ref[:, c * COLS : (c + 1) * COLS]
        vg = (cv_all[c].astype(F32) + (r * ghg - v * pull)).astype(BF16)
        wide = vg.astype(F32)
        dot_g = dot_g + wide * gw_sum[c : c + 1, :]
        dot_v = dot_v + wide * v
        four = jnp.concatenate([vg, vg, vg, vg], axis=0)
        back_scaled = back_scaled + mm_nt(mw[:, c * COLS : (c + 1) * COLS], four)

    def to_lanes(columns):
        column = jnp.sum(columns, axis=1, keepdims=True)
        column = jnp.concatenate([column, column, column, column], axis=0)
        eye = iota((TOK, TOK), 0) == iota((TOK, TOK), 1)
        return jnp.sum(jnp.where(eye, column, 0.0), axis=0, keepdims=True)

    grad_mean = to_lanes(dot_g) * (1.0 / MERGE)
    cross_mean = to_lanes(dot_v) * (1.0 / MERGE)
    scaled_grad = jnp.zeros((HD, TOK), F32)
    for i in range(4):
        scaled_grad = jnp.where(group == i, back_scaled[i * HD : (i + 1) * HD, :], scaled_grad)
    merged_grad = inv_std * (scaled_grad * gain - grad_mean - normed * cross_mean)
    unfold = jnp.where(pj == 4 * (pi & 31) + (pi >> 5), 1.0, 0.0).astype(BF16)
    part1 = merged_grad.astype(BF16)
    rest = merged_grad - part1.astype(F32)
    part2 = rest.astype(BF16)
    part3 = (rest - part2.astype(F32)).astype(BF16)
    ag_ref[...] = mm(part1, unfold) + mm(part2, unfold) + mm(part3, unfold)
    for src in range(NZ):
        wait_bytes(llm_all.at[src, other_half], llm_recv.at[1, src])
    for c in range(NZ):
        llm_ref[:, c * COLS : (c + 1) * COLS] = llm_all[c]

    wait_bytes(kvb.at[pl.ds(0, NB - 1)], kv_send.at[0])
    for index, buf in enumerate((cot_out, h_out, dn_out)):
        wait_bytes(buf.at[pl.ds(0, NB - 1)], a2a_send.at[index])
    wait_bytes(vblk.at[pl.ds(0, NB - 1)], vi_send.at[0])
    wait_bytes(info_out.at[pl.ds(0, NB - 1)], info_send.at[0])
    wait_bytes(place_all.at[pl.ds(0, NB - 1)], info_send.at[1])
    wait_bytes(cv_out.at[pl.ds(0, NB - 1)], row_send.at[0])
    for index, buf in enumerate((core_out, x_out, y_out)):
        wait_bytes(buf, sum_send.at[index])
    for index, buf in enumerate((gw_all, st_all, vp_all)):
        wait_bytes(buf.at[pl.ds(0, NE - 1)], e_send.at[index])
    for index, buf in enumerate((vis_all, cv_all, hg_all)):
        wait_bytes(buf.at[pl.ds(0, NZ - 1)], z_send.at[index])
    wait_bytes(xc.at[pl.ds(0, NZ - 1)], ring_send.at[0])
    for index in range(2):
        wait_bytes(xh.at[pl.ds(0, NZ - 1), pl.ds(0, HALF)], ring_send.at[1 + index])
    wait_bytes(rs_out.at[:, pl.ds(0, 14)], rs_send.at[0])
    wait_bytes(pair_in, pair_send.at[0])
    wait_bytes(hg_other, pair_send.at[1])
    wait_bytes(llm_all.at[pl.ds(0, NZ - 1), own_half], llm_send.at[0])
    wait_bytes(llm_all.at[:, own_half], llm_send.at[1])


def scratch_shapes():
    V = pltpu.VMEM
    D = pltpu.SemaphoreType.DMA
    routed = [V((NB, SLOT, COLS), BF16)] * 6
    rows = [V((NB, 8, TOK), F32)] * 2
    return (
        [V((HD, TOK), BF16)] * 3
        + [V((1, MR), jnp.int32), V((1, MR), jnp.int32), V((1, 4 * HD), F32), V((1, WIDTH), F32)]
        + [V((8, TOK), jnp.int32), V((8, TOK), F32)]
        + [V((4 * HD, WIDTH), BF16), V((TOK, COLS), BF16), V((TOK, COLS), BF16)]
        + [V((FG, WIDTH), BF16)] * 5
        + [D((15,))]
        + [V((NB, KVR, TOK), BF16), D((1,)), D((NB,))]
        + [V((NB * SLOT, TOK), BF16)] * 3
        + [V((HALF, SET * SLOT), BF16)]
        + [V((NB * 8, TOK), BF16)] * 4
        + routed + [D((3,)), D((1,)), D((3, 2))]
        + [V((NB, MR, COLS), F32)] + [V((4, 4, MR, COLS), BF16)] * 2 + [V((3, 4, MR, COLS), BF16)] * 2
        + [V((3, MR, COLS), BF16)] * 2 + [D((3,)), D((4,)), D((3,)), D((3,))]
        + rows + [D((1,)), D((1,))]
        + [V((NB, MR, COLS), BF16), D((1,)), D((NB,)), V((NB * MR, TOK), BF16), V((2, HALF, NB * MR), BF16), V((2, NB * MR, HALF), BF16)]
        + [V((NB, SLOT, TOK), BF16)] * 2 + [D((2,)), V((NB, 1, TOK), jnp.int32), D((1,))]
        + [V((NE, NZ, COLS), F32), V((NE, 8, TOK), F32), V((NZ, MR, COLS), BF16), V((NE, MR, COLS), BF16)]
        + [V((NZ, MR, COLS), BF16), V((MR, COLS), BF16), V((MR, COLS), BF16), D((3,)), D((3,))]
        + [V((NZ, MR, COLS), BF16)] * 2 + [D((3,)), D((3,))]
        + [V((NZ, ROWS, COLS), BF16)] * 2 + [D((3,)), D((3, 16))]
        + [V((ROWS, FG), F32), V((ROWS, FG), F32), V((ROWS, TOK), F32), V((ROWS, FG), F32), V((3, ROWS, FG), BF16)]
        + [V((4, 20, QUARTER, COLS), BF16)] * 2 + [D((1,)), D((4, 20))]
        + [V((TOK, COLS), BF16), V((TOK // 2, COLS), BF16), D((2,)), D((2,))]
        + [V((NZ, TOK, COLS), BF16), D((2,)), D((2, NZ))]
    )


def body(
    queries, keys, values, image_ids, placement, merge_gain, merge_weight, text, norm_gain,
    w_gate, w_up, w_down, routes, route_gates, cotangent,
):
    vm = pl.BlockSpec(memory_space=pltpu.VMEM)
    anywhere = pl.BlockSpec(memory_space=pl.ANY)
    llm_out, attn_grad = pl.pallas_call(
        kernel,
        out_shape=(
            jax.ShapeDtypeStruct((TOK, WIDTH), BF16),
            jax.ShapeDtypeStruct((HD, TOK), F32),
        ),
        in_specs=[anywhere] * 15,
        out_specs=(vm, vm),
        scratch_shapes=scratch_shapes(),
        compiler_params=pltpu.CompilerParams(
            collective_id=0, has_side_effects=True, vmem_limit_bytes=VMEM_BYTES
        ),
    )(
        queries, keys, values, image_ids[None, :], placement.T, merge_gain, merge_weight, text, norm_gain[None, :],
        w_gate, w_up, w_down, routes.T, route_gates.T, cotangent,
    )
    return llm_out, attn_grad[None]


def solution(mesh):
    return jax.shard_map(
        body,
        mesh=mesh,
        in_specs=(
            P("expert", None, "blk"),
            P("expert", None, "blk"),
            P("expert", None, "blk"),
            P("blk"),
            P("blk", None),
            P("expert", None),
            P("expert", None, None),
            P("blk", None),
            P(),
            P("blk", "expert", None),
            P("blk", "expert", None),
            P("blk", "expert", None),
            P("blk", None),
            P("blk", None),
            P("blk", None),
        ),
        out_specs=(P("blk", None), P("expert", None, "blk")),
        check_vma=False,
    )
```
